128 devices in a mesh: dp: 8 (over x, z_lo), cent: 16 (over z_hi, y, core).
Axes of the slice: x: 4, y: 4, z: 4 (z_hi: 2, z_lo: 2; z = z_hi * 2 + z_lo), core: 2. Of those that a mesh axis runs over, the one named last changes fastest.
Arguments:
- embeddings: bfloat16 [32768, 1536], P('dp'), may hold values from -20 to 20
- assignments: int32 [32768], P('dp'), may hold values from 0 to 16383, as said below
- parents: bfloat16 [8192, 1536], P('cent'), may hold values from -24 to 24
- starting_coarse_label: int32 [16384], P(('cent', 'dp')), may hold values from 0 to 8191
Outputs:
- centroids: bfloat16 [16384, 1536], P(('cent', 'dp'))
- log_total: float32 [16384], P(('cent', 'dp'))
- parent_mass: float32 [8192], P(('cent', 'dp'))
The draws below stay inside these ranges and needn't reach their ends.
Inputs may be any that keep to these rules, and one draw needn't show every extreme that they name: `assignments`: split the centroids into aligned runs of 128. Of the rows of one index of dp, at most 48 have their centroid in any one run; one run reaches 48 from every index of dp.
All inputs are finite; a program needn't handle non-finite values.
Results may differ from the reference program's by a relative error of at most 0.0016.
Values may be sent and summed in bfloat16 or wider, within the bound.
A program may use at most 128 MiB of HBM per device.

```python
import jax
import jax.numpy as jnp
from jax import lax

W = 1536
K1 = 16384
K2 = 8192
ROW_DEV = 4096
ROWS = 32768
N_DP = 8
N_CENT = 16


def draw_embeddings(key, part):
    key = jax.random.fold_in(key, 11)
    second_key = jax.random.fold_in(key, 1)
    values = jnp.clip(jax.random.normal(second_key, (ROWS, W), jnp.float32), -6.0, 6.0)
    return values.astype(jnp.bfloat16)


def draw_parents(key, part):
    key = jax.random.fold_in(key, 23)
    values = jnp.clip(jax.random.normal(key, (K2, W), jnp.float32), -6.0, 6.0)
    return values.astype(jnp.bfloat16)


def draw_assignments(key, part):
    key = jax.random.fold_in(key, 37)
    split_key, forced_key, order_key, member_key = jax.random.split(key, 4)
    buckets = N_DP * N_CENT
    runs = K1 // buckets
    mean_rows = ROW_DEV // buckets
    pairs = buckets // 2
    split = jax.random.randint(split_key, (N_DP, pairs), mean_rows // 2, 3 * mean_rows // 2 + 1)
    forced = jax.random.randint(forced_key, (), 0, pairs)
    split = jnp.where(jnp.arange(pairs, dtype=jnp.int32)[None, :] == forced, 3 * mean_rows // 2, split)
    position = jnp.arange(ROW_DEV, dtype=jnp.int32)
    pair_of = position // (2 * mean_rows)
    inside = position % (2 * mean_rows)
    ordered = 2 * pair_of[None, :] + (inside[None, :] >= jnp.take(split, pair_of, axis=1)).astype(jnp.int32)
    order_keys = jax.random.split(order_key, N_DP)
    orders = jax.vmap(lambda one_key: jax.random.permutation(one_key, ROW_DEV))(order_keys)
    shuffled = jnp.take_along_axis(ordered, orders, axis=1)
    member = jax.random.randint(member_key, (N_DP, ROW_DEV), 0, runs)
    return (shuffled * runs + member).reshape(ROWS).astype(jnp.int32)


def plant(array, stream_key, least, high):
    shape = array.shape
    index_at = [jax.random.randint(jax.random.fold_in(stream_key, axis), (), 0, shape[axis]) for axis in range(len(shape))]
    array = array.at[tuple(index_at)].set(least)
    longest = shape.index(max(shape))
    index_at[longest] = (index_at[longest] + 1) % shape[longest]
    return array.at[tuple(index_at)].set(high)


def setup_inputs(seed: int = 0) -> dict:
    arg_keys = jax.random.split(jax.random.key(seed), 5)
    return {
        "embeddings": draw_embeddings(jax.random.fold_in(arg_keys[4], 71), 0),
        "assignments": draw_assignments(jax.random.fold_in(arg_keys[4], 71), 0),
        "parents": draw_parents(jax.random.fold_in(arg_keys[4], 71), 0),
        "starting_coarse_label": plant(jax.random.randint(arg_keys[3], (K1,), 0, K2), jax.random.fold_in(arg_keys[3], 1), 0, K2 - 1).astype(jnp.int32),
    }


softness_factor = 0.5
retain_coarse_reward = 1.5

def reference(embeddings, assignments, parents, starting_coarse_label):
    sums = jax.ops.segment_sum(embeddings.astype(jnp.float32), assignments, num_segments=K1)
    counts = jax.ops.segment_sum(jnp.ones(assignments.shape, jnp.float32), assignments, num_segments=K1)
    mean = sums / jnp.maximum(counts, 1.0)[:, None]
    scale = jnp.sqrt(lax.optimization_barrier(jnp.sum(mean * mean, axis=1, keepdims=True)) + 1e-06)
    centroids = (mean / scale).astype(jnp.bfloat16)
    weight = lax.optimization_barrier(counts.astype(jnp.bfloat16)).astype(jnp.float32)
    block = min(1024, K1)
    nblock = K1 // block
    coarse_labels = jnp.arange(K2, dtype=jnp.int32)

    def step(mass, items):
        centroid_block_tile, holder_shard_label, weight_block = items
        affinity_grid = jnp.dot(centroid_block_tile, parents.T, preferred_element_type=jnp.float32) / softness_factor
        affinity_grid = affinity_grid + retain_coarse_reward * (holder_shard_label[:, None] == coarse_labels[None, :]).astype(jnp.float32)
        row_top = lax.optimization_barrier(jnp.max(affinity_grid, axis=1))
        log_block = row_top + jnp.log(lax.optimization_barrier(jnp.sum(jnp.exp(affinity_grid - row_top[:, None]), axis=1)))
        resp = jnp.exp(affinity_grid - log_block[:, None])
        mass = mass + jnp.dot(weight_block, resp, precision=lax.Precision.HIGHEST)
        return (mass, log_block)
    mass, log_blocks = lax.scan(step, jnp.zeros((K2,), jnp.float32), (centroids.reshape(nblock, block, W), starting_coarse_label.reshape(nblock, block), weight.reshape(nblock, block)))
    return (centroids, log_blocks.reshape(K1), mass)
```

```python
import jax
import jax.numpy as jnp
from jax import lax
from jax.experimental import pallas as pl
from jax.experimental.pallas import tpu as pltpu
from jax.sharding import PartitionSpec as P

MESH = pl.DeviceIdType.MESH
F32 = jnp.float32
BF16 = jnp.bfloat16

W = 1536
RUN = 128
CAP = 48
DP = 8
SLOTS = DP * CAP
EXT = W + RUN
TILE = 256
NTILE = W // TILE
ROWS = 4096
SLAB = 512
PCH = 256
NPCH = 8
INV_SOFT = 1.0 / 0.5
REWARD = 1.5

RANGES = ((0, 512), (512, 512), (1024, 640))


def kernel(
    a_ref, label_ref, e_hbm, p_hbm,
    cent_ref, logt_ref, mass_ref,
    e_v, oht, bt, slot_v, send, recv, par, cb, meta, scores, mch, sch, stat, fac, mp, sib_in, y_in, ms, mr,
    e_sem, p_sem, row_ss, row_rs, par_ss, par_rs, cb_ss, cb_rs, meta_ss, meta_rs, stat_ss, stat_rs,
    m1_ss, m1_rs, m2_ss, m2_rs,
):
    d = lax.axis_index("dp")
    c = lax.axis_index("cent")
    zlo = d % 2
    zhi = c // 8
    y = (c // 2) % 4
    k = c % 2

    def cent_of(zh, yy, kk):
        return zh * 8 + yy * 2 + kk

    yp, ym, y2 = (y + 1) % 4, (y + 3) % 4, (y + 2) % 4
    flip_d = d - zlo + (1 - zlo)
    group = {
        1: (flip_d, cent_of(1 - zhi, y, k)),
        2: (d, cent_of(zhi, y2, k)),
        3: (flip_d, cent_of(1 - zhi, y2, k)),
    }
    sibling = (d, cent_of(zhi, y, 1 - k))
    up = (d, cent_of(zhi, yp, k))
    down = (d, cent_of(zhi, ym, k))
    up_x = (d, cent_of(zhi, yp, 1 - k))
    down_x = (d, cent_of(zhi, ym, 1 - k))

    def row_peer(r):
        return ((d + r) % DP, c)

    def rcopy(src, dst, ss, rs, dev):
        return pltpu.make_async_remote_copy(
            src_ref=src, dst_ref=dst, send_sem=ss, recv_sem=rs, device_id=dev, device_id_type=MESH
        )

    e_copies = [
        pltpu.make_async_copy(e_hbm.at[:, pl.ds(TILE * n, TILE)], e_v.at[n], e_sem.at[n]) for n in range(NTILE)
    ]
    for cp in e_copies:
        cp.start()
    own_par = pltpu.make_async_copy(p_hbm, par.at[pl.ds(0, SLAB)], p_sem)
    own_par.start()

    barrier = pltpu.get_barrier_semaphore()
    partners = [row_peer(r) for r in range(1, DP)] + [group[1], group[2], group[3], sibling, up, down, up_x, down_x]
    for dev in partners:
        pl.semaphore_signal(barrier, inc=1, device_id=dev, device_id_type=MESH)

    a = a_ref[...]
    rel = lax.shift_right_logical(a, 7) - c * DP
    run_id = lax.broadcasted_iota(jnp.int32, (32, 8, RUN), 1)
    member = (rel[:, None, :] == run_id).astype(F32).reshape(256, RUN)
    member_b = member.astype(BF16)
    upper = (
        lax.broadcasted_iota(jnp.int32, (RUN, RUN), 0) < lax.broadcasted_iota(jnp.int32, (RUN, RUN), 1)
    ).astype(F32).astype(BF16)
    ri = lax.broadcasted_iota(jnp.int32, (256, 256), 0)
    ci = lax.broadcasted_iota(jnp.int32, (256, 256), 1)
    before = (((ri & 7) == (ci & 7)) & (ci < ri)).astype(F32).astype(BF16)
    within = jnp.dot(member_b, upper, preferred_element_type=F32)
    earlier = jnp.dot(before, member_b, preferred_element_type=F32).astype(BF16)
    ahead = jnp.dot(earlier, jnp.ones((RUN, RUN), BF16), preferred_element_type=F32)
    base = ((lax.broadcasted_iota(jnp.int32, (256, RUN), 0) & 7) * CAP + 1).astype(F32)
    slot = jnp.sum((member * (within + ahead + base)).reshape(32, 8, RUN), axis=1) - 1.0
    slot_v[0] = slot.astype(jnp.int32)
    slot_v[1] = a & (RUN - 1)

    pl.semaphore_wait(barrier, len(partners))

    to_up = rcopy(p_hbm.at[pl.ds(0, PCH)], par.at[pl.ds(2 * PCH, PCH)], par_ss.at[0], par_rs.at[0], up)
    to_down = rcopy(p_hbm.at[pl.ds(PCH, PCH)], par.at[pl.ds(3 * PCH, PCH)], par_ss.at[1], par_rs.at[1], down)
    to_sib = rcopy(p_hbm, par.at[pl.ds(4 * PCH, SLAB)], par_ss.at[2], par_rs.at[2], sibling)
    fwd_sib = [
        rcopy(
            par.at[pl.ds((2 + i) * PCH, PCH)], par.at[pl.ds((6 + i) * PCH, PCH)], par_ss.at[3 + i], par_rs.at[3 + i], sibling
        )
        for i in range(2)
    ]
    to_up.start()
    to_down.start()
    to_sib.start()

    def build(b, carry):
        cols = pl.ds(pl.multiple_of(b * RUN, RUN), RUN)
        line = slot_v[0, pl.ds(b, 1), :]
        place = slot_v[1, pl.ds(b, 1), :]
        oht[:, cols] = (lax.broadcasted_iota(jnp.int32, (SLOTS, RUN), 0) == line).astype(F32).astype(BF16)
        bt[:, cols] = (lax.broadcasted_iota(jnp.int32, (RUN, RUN), 0) == place).astype(F32).astype(BF16)
        return carry

    lax.fori_loop(0, ROWS // RUN, build, 0)

    def row_copy(r, g, dev, owner):
        start, size = RANGES[g]
        return rcopy(
            send.at[dev[0], :, pl.ds(start, size)],
            recv.at[owner, :, pl.ds(start, size)],
            row_ss.at[r - 1, g],
            row_rs.at[r - 1, g],
            dev,
        )

    for n in range(NTILE):
        if n == 0:
            ext = lax.dot_general(oht[...], bt[...], (((1,), (1,)), ((), ())), preferred_element_type=F32)
            send[:, :, W:] = ext.astype(BF16).reshape(DP, CAP, RUN)
        e_copies[n].wait()
        part = jnp.dot(oht[...], e_v[n], preferred_element_type=F32)
        send[:, :, TILE * n : TILE * (n + 1)] = part.astype(BF16).reshape(DP, CAP, TILE)
        if n % 2 == 1:
            for r in range(1, DP):
                row_copy(r, n // 2, row_peer(r), d).start()
    recv[d] = send[d]

    for g in range(len(RANGES)):
        for r in range(1, DP):
            row_copy(r, g, row_peer(r), (d + DP - r) % DP).wait_recv()

    got = recv[...].reshape(SLOTS, EXT)
    onehot = got[:, W:]
    sums = lax.dot_general(onehot, got[:, :W], (((0,), (0,)), ((), ())), preferred_element_type=F32)
    counts_col = lax.dot_general(
        onehot, jnp.ones((SLOTS, RUN), BF16), (((0,), (0,)), ((), ())), preferred_element_type=F32
    )[:, :1]
    counts_row = jnp.sum(onehot.astype(F32), axis=0, keepdims=True)
    mean = sums / jnp.maximum(counts_col, 1.0)
    scale = jnp.sqrt(jnp.sum(mean * mean, axis=1, keepdims=True) + 1e-06)
    normed = (mean / scale).astype(BF16)
    cb[0] = normed
    cent_ref[...] = normed
    meta[0, 0:1, :] = counts_row.astype(BF16).astype(F32)
    meta[0, 1:2, :] = label_ref[...].astype(F32)
    meta[0, 2:8, :] = jnp.zeros((6, RUN), F32)

    def half(slot_from, slot_to, h, idx, dev):
        rows = pl.ds(64 * h, 64)
        return rcopy(cb.at[slot_from, rows], cb.at[slot_to, rows], cb_ss.at[idx], cb_rs.at[idx], dev)

    z_first = half(0, 1, 0, 0, group[1])
    z_second = half(0, 1, 1, 1, group[1])
    y_first = half(0, 2, 1, 2, group[2])
    y_second = half(0, 2, 0, 3, group[2])
    fwd_y = half(1, 3, 0, 4, group[2])
    fwd_z = half(2, 3, 1, 5, group[1])
    z_first.start()
    y_first.start()
    metas = {q: rcopy(meta.at[0], meta.at[q], meta_ss.at[q - 1], meta_rs.at[q - 1], group[q]) for q in (1, 2, 3)}
    for q in (1, 2, 3):
        metas[q].start()
    z_second.start()
    y_second.start()

    to_up.wait_recv()
    fwd_sib[0].start()
    to_down.wait_recv()
    fwd_sib[1].start()
    z_first.wait_recv()
    fwd_y.start()
    y_first.wait_recv()
    fwd_z.start()

    own_par.wait()
    to_sib.wait_recv()
    for cp in fwd_sib:
        cp.wait_recv()
    for q in (1, 2, 3):
        metas[q].wait_recv()

    def first_parent(i):
        own, other = k, 1 - k
        lower = cent_of(zhi, ym, 0) * SLAB
        upper_ = cent_of(zhi, yp, 0) * SLAB + PCH
        mine = cent_of(zhi, y, 0) * SLAB
        core = jnp.where(i < 4, own, other) * SLAB
        j = i % 4
        return jnp.where(j < 2, mine + j * PCH, jnp.where(j == 2, lower, upper_)) + core

    def score(pair):
        cols = pl.ds(2 * RUN * pair, 2 * RUN)
        block = cb[2 * pair : 2 * pair + 2].reshape(2 * RUN, W)
        label = jnp.concatenate([meta[2 * pair, 1:2, :], meta[2 * pair + 1, 1:2, :]], axis=1).astype(jnp.int32)

        def step(i, carry):
            s = lax.dot_general(
                par[pl.ds(pl.multiple_of(i * PCH, PCH), PCH), :], block, (((1,), (1,)), ((), ())), preferred_element_type=F32
            )
            ids = lax.broadcasted_iota(jnp.int32, (PCH, 2 * RUN), 0) + first_parent(i)
            s = s * INV_SOFT + jnp.where(ids == label, REWARD, 0.0)
            top = jnp.max(s, axis=0, keepdims=True)
            e = jnp.exp(s - top)
            scores[i, :, cols] = e
            mch[pl.ds(i, 1), cols] = top
            sch[pl.ds(i, 1), cols] = jnp.sum(e, axis=0, keepdims=True)
            return carry

        lax.fori_loop(0, NPCH, step, 0)

    z_second.wait_recv()
    score(0)
    y_second.wait_recv()
    fwd_y.wait_recv()
    fwd_z.wait_recv()
    score(1)

    m_loc = jnp.max(mch[...], axis=0, keepdims=True)
    s_loc = jnp.sum(sch[...] * jnp.exp(mch[...] - m_loc), axis=0, keepdims=True)
    for j in range(4):
        stat[0, j : j + 1, :] = m_loc[:, RUN * j : RUN * (j + 1)]
        stat[0, 4 + j : 5 + j, :] = s_loc[:, RUN * j : RUN * (j + 1)]
    stats = {q: rcopy(stat.at[0], stat.at[q], stat_ss.at[q - 1], stat_rs.at[q - 1], group[q]) for q in (1, 2, 3)}
    for q in (1, 2, 3):
        stats[q].start()
    for q in (1, 2, 3):
        stats[q].wait_recv()
    for j in range(4):
        m = [stat[q, (j ^ q) : (j ^ q) + 1, :] for q in range(4)]
        s = [stat[q, 4 + (j ^ q) : 5 + (j ^ q), :] for q in range(4)]
        top = jnp.maximum(jnp.maximum(m[0], m[1]), jnp.maximum(m[2], m[3]))
        total = sum(s[q] * jnp.exp(m[q] - top) for q in range(4))
        log_total = top + jnp.log(total)
        if j == 0:
            logt_ref[...] = log_total
        cols = slice(RUN * j, RUN * (j + 1))
        fac[:, cols] = meta[j, 0:1, :] * jnp.exp(mch[:, cols] - log_total)

    def mass_step(i, carry):
        f = fac[pl.ds(i, 1), :]
        acc = jnp.zeros((PCH, RUN), F32)
        for j in range(4):
            acc = acc + scores[i, :, RUN * j : RUN * (j + 1)] * f[:, RUN * j : RUN * (j + 1)]
        mp[i] = jnp.sum(acc.T, axis=0, keepdims=True)
        return carry

    lax.fori_loop(0, NPCH, mass_step, 0)

    m1 = [
        rcopy(mp.at[pl.ds(4, 2)], sib_in, m1_ss.at[0], m1_rs.at[0], sibling),
        rcopy(mp.at[2], y_in.at[0], m1_ss.at[1], m1_rs.at[1], down),
        rcopy(mp.at[6], y_in.at[1], m1_ss.at[2], m1_rs.at[2], down_x),
        rcopy(mp.at[3], y_in.at[2], m1_ss.at[3], m1_rs.at[3], up),
        rcopy(mp.at[7], y_in.at[3], m1_ss.at[4], m1_rs.at[4], up_x),
    ]
    for cp in m1:
        cp.start()
    for cp in m1:
        cp.wait_recv()
    halves = (
        mp[0] + sib_in[0] + y_in[0] + y_in[1],
        mp[1] + sib_in[1] + y_in[2] + y_in[3],
    )
    for i in range(DP):
        ms[i, :, :64] = halves[i // 4][:, 64 * (i % 4) : 64 * (i % 4) + 64]
        ms[i, :, 64:] = jnp.zeros((1, 64), F32)
    m2 = []
    for r in range(1, DP):
        dev = row_peer(r)
        cp = rcopy(ms.at[dev[0]], mr.at[d], m2_ss.at[r - 1], m2_rs.at[r - 1], dev)
        cp.start()
    mr[d] = ms[d]
    for r in range(1, DP):
        rcopy(ms.at[row_peer(r)[0]], mr.at[(d + DP - r) % DP], m2_ss.at[r - 1], m2_rs.at[r - 1], row_peer(r)).wait_recv()
    mass_ref[...] = jnp.sum(mr[...], axis=0)[:, :64]

    for cp in [to_up, to_down, to_sib, *fwd_sib, z_first, z_second, y_first, y_second, fwd_y, fwd_z, *m1]:
        cp.wait_send()
    for q in (1, 2, 3):
        metas[q].wait_send()
        stats[q].wait_send()
    for r in range(1, DP):
        for g in range(len(RANGES)):
            row_copy(r, g, row_peer(r), d).wait_send()
        rcopy(ms.at[row_peer(r)[0]], mr.at[d], m2_ss.at[r - 1], m2_rs.at[r - 1], row_peer(r)).wait_send()


def per_device(embeddings, assignments, parents, starting_coarse_label):
    vmem = pl.BlockSpec(memory_space=pltpu.VMEM)
    hbm = pl.BlockSpec(memory_space=pltpu.HBM)
    dma = pltpu.SemaphoreType.DMA
    cent, logt, mass = pl.pallas_call(
        kernel,
        out_shape=(
            jax.ShapeDtypeStruct((RUN, W), BF16),
            jax.ShapeDtypeStruct((1, RUN), F32),
            jax.ShapeDtypeStruct((1, 64), F32),
        ),
        in_specs=[vmem, vmem, hbm, hbm],
        out_specs=(vmem, vmem, vmem),
        scratch_shapes=[
            pltpu.VMEM((NTILE, ROWS, TILE), BF16),
            pltpu.VMEM((SLOTS, ROWS), BF16),
            pltpu.VMEM((RUN, ROWS), BF16),
            pltpu.VMEM((2, 32, RUN), jnp.int32),
            pltpu.VMEM((DP, CAP, EXT), BF16),
            pltpu.VMEM((DP, CAP, EXT), BF16),
            pltpu.VMEM((NPCH * PCH, W), BF16),
            pltpu.VMEM((4, RUN, W), BF16),
            pltpu.VMEM((4, 8, RUN), F32),
            pltpu.VMEM((NPCH, PCH, 4 * RUN), F32),
            pltpu.VMEM((NPCH, 4 * RUN), F32),
            pltpu.VMEM((NPCH, 4 * RUN), F32),
            pltpu.VMEM((4, 8, RUN), F32),
            pltpu.VMEM((NPCH, 4 * RUN), F32),
            pltpu.VMEM((NPCH, 1, PCH), F32),
            pltpu.VMEM((2, 1, PCH), F32),
            pltpu.VMEM((4, 1, PCH), F32),
            pltpu.VMEM((DP, 1, RUN), F32),
            pltpu.VMEM((DP, 1, RUN), F32),
            dma((NTILE,)),
            dma,
            dma((DP - 1, len(RANGES))),
            dma((DP - 1, len(RANGES))),
            dma((5,)),
            dma((5,)),
            dma((6,)),
            dma((6,)),
            dma((3,)),
            dma((3,)),
            dma((3,)),
            dma((3,)),
            dma((5,)),
            dma((5,)),
            dma((DP - 1,)),
            dma((DP - 1,)),
        ],
        compiler_params=pltpu.CompilerParams(collective_id=0, has_side_effects=True, vmem_limit_bytes=56 << 20),
        name="handover",
    )(
        assignments.reshape(32, RUN),
        starting_coarse_label.reshape(1, RUN),
        embeddings,
        parents,
    )
    return cent, logt.reshape(RUN), mass.reshape(64)


def solution(mesh):
    return jax.shard_map(
        per_device,
        mesh=mesh,
        in_specs=(P("dp", None), P("dp"), P("cent", None), P(("cent", "dp"))),
        out_specs=(P(("cent", "dp"), None), P(("cent", "dp")), P(("cent", "dp"))),
        check_vma=False,
    )
```

```python
import jax
import jax.numpy as jnp
from jax import lax
from jax.experimental import pallas as pl
from jax.experimental.pallas import tpu as pltpu
from jax.sharding import PartitionSpec as P

MESH = pl.DeviceIdType.MESH
F32 = jnp.float32
BF16 = jnp.bfloat16

W = 1536
RUN = 128
CAP = 48
DP = 8
SLOTS = DP * CAP
EXT = W + RUN
TILE = 256
NTILE = W // TILE
AHEAD = 2
ROWS = 4096
SLAB = 512
PART = 64
PCH = 512
NPCH = 4
HALF = 256
INV_SOFT = 1.0 / 0.5
REWARD = 1.5

RANGES = ((0, 256), (256, 512), (768, 896))
SEND_AFTER = (0, 2, 5)


def kernel(
    a_ref, label_ref, e_hbm, p_hbm,
    cent_hbm, logt_hbm, mass_hbm,
    e_v, oht, bt, slot_v, send, recv, par, cb, meta, scores, mch, sch, stat, fac, mp, sib_in, ms, mr, logt_v, mass_v,
    e_sem, p_sem, row_ss, row_rs, par_ss, par_rs, cb_ss, cb_rs, meta_ss, meta_rs, stat_ss, stat_rs,
    m1_ss, m1_rs, m2_ss, m2_rs, o_sem,
):
    d = lax.axis_index("dp")
    c = lax.axis_index("cent")
    zlo = d % 2
    zhi = c // 8
    y = (c // 2) % 4
    k = c % 2

    def cent_of(zh, yy, kk):
        return zh * 8 + yy * 2 + kk

    yp, ym, y2 = (y + 1) % 4, (y + 3) % 4, (y + 2) % 4
    flip_d = d - zlo + (1 - zlo)
    group = {
        1: (flip_d, cent_of(1 - zhi, y, k)),
        2: (d, cent_of(zhi, y2, k)),
        3: (flip_d, cent_of(1 - zhi, y2, k)),
    }
    sibling = (d, cent_of(zhi, y, 1 - k))
    up = (d, cent_of(zhi, yp, k))
    down = (d, cent_of(zhi, ym, k))

    def row_peer(r):
        return ((d + r) % DP, c)

    def rcopy(src, dst, ss, rs, dev):
        return pltpu.make_async_remote_copy(
            src_ref=src, dst_ref=dst, send_sem=ss, recv_sem=rs, device_id=dev, device_id_type=MESH
        )

    barrier = pltpu.get_barrier_semaphore()
    mass_from = cent_of(zhi, jnp.where(d < 4, yp, ym), k)
    partners = [row_peer(r) for r in range(1, DP)] + [group[1], group[2], group[3], sibling, up, down]
    partners += [((d + r) % DP, mass_from) for r in range(DP)]
    for dev in partners:
        pl.semaphore_signal(barrier, inc=1, device_id=dev, device_id_type=MESH)

    e_copies = [
        pltpu.make_async_copy(e_hbm.at[:, pl.ds(TILE * n, TILE)], e_v.at[n], e_sem.at[n]) for n in range(NTILE)
    ]
    for cp in e_copies[:AHEAD]:
        cp.start()
    own_par = pltpu.make_async_copy(p_hbm, par.at[pl.ds(0, SLAB)], p_sem)

    a = a_ref[...]
    rel = lax.shift_right_logical(a, 7) - c * DP
    run_id = lax.broadcasted_iota(jnp.int32, (32, 8, RUN), 1)
    member = (rel[:, None, :] == run_id).astype(F32).reshape(256, RUN)
    member_b = member.astype(BF16)
    upper = (
        lax.broadcasted_iota(jnp.int32, (RUN, RUN), 0) < lax.broadcasted_iota(jnp.int32, (RUN, RUN), 1)
    ).astype(F32).astype(BF16)
    ri = lax.broadcasted_iota(jnp.int32, (256, 256), 0)
    ci = lax.broadcasted_iota(jnp.int32, (256, 256), 1)
    before = (((ri & 7) == (ci & 7)) & (ci < ri)).astype(F32).astype(BF16)
    within = jnp.dot(member_b, upper, preferred_element_type=F32)
    earlier = jnp.dot(before, member_b, preferred_element_type=F32).astype(BF16)
    ahead = jnp.dot(earlier, jnp.ones((RUN, RUN), BF16), preferred_element_type=F32)
    base = ((lax.broadcasted_iota(jnp.int32, (256, RUN), 0) & 7) * CAP + 1).astype(F32)
    slot = jnp.sum((member * (within + ahead + base)).reshape(32, 8, RUN), axis=1) - 1.0
    slot_v[0] = slot.astype(jnp.int32)
    slot_v[1] = a & (RUN - 1)

    pl.semaphore_wait(barrier, len(partners))

    to_up = rcopy(p_hbm.at[pl.ds(0, HALF)], par.at[pl.ds(SLAB, HALF)], par_ss.at[0], par_rs.at[0], up)
    to_down = rcopy(p_hbm.at[pl.ds(HALF, HALF)], par.at[pl.ds(SLAB + HALF, HALF)], par_ss.at[1], par_rs.at[1], down)
    to_sib = rcopy(p_hbm, par.at[pl.ds(2 * SLAB, SLAB)], par_ss.at[2], par_rs.at[2], sibling)
    fwd_sib = [
        rcopy(
            par.at[pl.ds(SLAB + i * HALF, HALF)],
            par.at[pl.ds(3 * SLAB + i * HALF, HALF)],
            par_ss.at[3 + i],
            par_rs.at[3 + i],
            sibling,
        )
        for i in range(2)
    ]
    to_up.start()
    to_down.start()

    def build(b, carry):
        cols = pl.ds(pl.multiple_of(b * RUN, RUN), RUN)
        line = slot_v[0, pl.ds(b, 1), :]
        place = slot_v[1, pl.ds(b, 1), :]
        oht[:, cols] = (lax.broadcasted_iota(jnp.int32, (SLOTS, RUN), 0) == line).astype(F32).astype(BF16)
        bt[:, cols] = (lax.broadcasted_iota(jnp.int32, (RUN, RUN), 0) == place).astype(F32).astype(BF16)
        return carry

    lax.fori_loop(0, ROWS // RUN, build, 0)

    def row_copy(r, g, dev, owner):
        start, size = RANGES[g]
        return rcopy(
            send.at[dev[0], :, pl.ds(start, size)],
            recv.at[owner, :, pl.ds(start, size)],
            row_ss.at[r - 1, g],
            row_rs.at[r - 1, g],
            dev,
        )

    for n in range(NTILE):
        e_copies[n].wait()
        if n + AHEAD < NTILE:
            e_copies[n + AHEAD].start()
        if n == 3:
            own_par.start()
            to_sib.start()
        part = jnp.dot(oht[...], e_v[n], preferred_element_type=F32)
        send[:, :, TILE * n : TILE * (n + 1)] = part.astype(BF16).reshape(DP, CAP, TILE)
        if n == NTILE - 1:
            ext = lax.dot_general(oht[...], bt[...], (((1,), (1,)), ((), ())), preferred_element_type=F32)
            send[:, :, W:] = ext.astype(BF16).reshape(DP, CAP, RUN)
        if n in SEND_AFTER:
            for r in range(1, DP):
                row_copy(r, SEND_AFTER.index(n), row_peer(r), d).start()
    recv[d] = send[d]

    for g in range(len(RANGES)):
        for r in range(1, DP):
            row_copy(r, g, row_peer(r), (d + DP - r) % DP).wait_recv()

    got = recv[...].reshape(SLOTS, EXT)
    onehot = got[:, W:]
    sums = lax.dot_general(onehot, got[:, :W], (((0,), (0,)), ((), ())), preferred_element_type=F32)
    counts_col = lax.dot_general(
        onehot, jnp.ones((SLOTS, RUN), BF16), (((0,), (0,)), ((), ())), preferred_element_type=F32
    )[:, :1]
    counts_row = jnp.sum(onehot.astype(F32), axis=0, keepdims=True)
    mean = sums / jnp.maximum(counts_col, 1.0)
    scale = jnp.sqrt(jnp.sum(mean * mean, axis=1, keepdims=True) + 1e-06)
    normed = (mean / scale).astype(BF16)
    cb[0] = normed
    cent_out = pltpu.make_async_copy(cb.at[0], cent_hbm, o_sem.at[0])
    cent_out.start()
    meta[0, 0:1, :] = counts_row.astype(BF16).astype(F32)
    meta[0, 1:2, :] = label_ref[...].astype(F32)
    meta[0, 2:8, :] = jnp.zeros((6, RUN), F32)

    def half(slot_from, slot_to, h, idx, dev):
        rows = pl.ds(64 * h, 64)
        return rcopy(cb.at[slot_from, rows], cb.at[slot_to, rows], cb_ss.at[idx], cb_rs.at[idx], dev)

    z_first = half(0, 1, 0, 0, group[1])
    z_second = half(0, 1, 1, 1, group[1])
    y_first = half(0, 2, 1, 2, group[2])
    y_second = half(0, 2, 0, 3, group[2])
    fwd_y = half(1, 3, 0, 4, group[2])
    fwd_z = half(2, 3, 1, 5, group[1])
    z_first.start()
    y_first.start()
    metas = {q: rcopy(meta.at[0], meta.at[q], meta_ss.at[q - 1], meta_rs.at[q - 1], group[q]) for q in (1, 2, 3)}
    for q in (1, 2, 3):
        metas[q].start()
    z_second.start()
    y_second.start()

    to_up.wait_recv()
    fwd_sib[0].start()
    to_down.wait_recv()
    fwd_sib[1].start()
    z_first.wait_recv()
    fwd_y.start()
    y_first.wait_recv()
    fwd_z.start()

    own_par.wait()
    to_sib.wait_recv()
    for cp in fwd_sib:
        cp.wait_recv()
    for q in (1, 2, 3):
        metas[q].wait_recv()

    def parent_ids(i):
        core = jnp.where(i < 2, k, 1 - k)
        low = cent_of(zhi, jnp.where(i % 2 == 0, y, ym), core) * SLAB
        high = cent_of(zhi, jnp.where(i % 2 == 0, y, yp), core) * SLAB
        line = lax.broadcasted_iota(jnp.int32, (PCH, 2 * RUN), 0)
        return line + jnp.where(line < HALF, low, high)

    def score(pair):
        cols = pl.ds(2 * RUN * pair, 2 * RUN)
        block = cb[2 * pair : 2 * pair + 2].reshape(2 * RUN, W)
        label = jnp.concatenate([meta[2 * pair, 1:2, :], meta[2 * pair + 1, 1:2, :]], axis=1).astype(jnp.int32)

        def step(i, carry):
            s = lax.dot_general(
                par[pl.ds(pl.multiple_of(i * PCH, PCH), PCH), :], block, (((1,), (1,)), ((), ())), preferred_element_type=F32
            )
            s = s * INV_SOFT + jnp.where(parent_ids(i) == label, REWARD, 0.0)
            top = jnp.max(s, axis=0, keepdims=True)
            e = jnp.exp(s - top)
            scores[i, :, cols] = e
            mch[pl.ds(i, 1), cols] = top
            sch[pl.ds(i, 1), cols] = jnp.sum(e, axis=0, keepdims=True)
            return carry

        lax.fori_loop(0, NPCH, step, 0)

    z_second.wait_recv()
    score(0)
    y_second.wait_recv()
    fwd_y.wait_recv()
    fwd_z.wait_recv()
    score(1)

    m_loc = jnp.max(mch[...], axis=0, keepdims=True)
    s_loc = jnp.sum(sch[...] * jnp.exp(mch[...] - m_loc), axis=0, keepdims=True)
    for j in range(4):
        stat[0, j : j + 1, :] = m_loc[:, RUN * j : RUN * (j + 1)]
        stat[0, 4 + j : 5 + j, :] = s_loc[:, RUN * j : RUN * (j + 1)]
    stats = {q: rcopy(stat.at[0], stat.at[q], stat_ss.at[q - 1], stat_rs.at[q - 1], group[q]) for q in (1, 2, 3)}
    for q in (1, 2, 3):
        stats[q].start()
    for q in (1, 2, 3):
        stats[q].wait_recv()
    for j in range(4):
        m = [stat[q, (j ^ q) : (j ^ q) + 1, :] for q in range(4)]
        s = [stat[q, 4 + (j ^ q) : 5 + (j ^ q), :] for q in range(4)]
        top = jnp.maximum(jnp.maximum(m[0], m[1]), jnp.maximum(m[2], m[3]))
        total = sum(s[q] * jnp.exp(m[q] - top) for q in range(4))
        log_total = top + jnp.log(total)
        if j == 0:
            logt_v[...] = log_total
            logt_out = pltpu.make_async_copy(logt_v, logt_hbm, o_sem.at[1])
            logt_out.start()
        cols = slice(RUN * j, RUN * (j + 1))
        fac[:, cols] = meta[j, 0:1, :] * jnp.exp(mch[:, cols] - log_total)

    def mass_step(i, carry):
        f = fac[pl.ds(i, 1), :]
        acc = jnp.zeros((PCH, RUN), F32)
        for j in range(4):
            acc = acc + scores[i, :, RUN * j : RUN * (j + 1)] * f[:, RUN * j : RUN * (j + 1)]
        mp[i] = jnp.sum(acc.T, axis=0, keepdims=True)
        return carry

    lax.fori_loop(0, NPCH, mass_step, 0)

    to_sib_mass = rcopy(mp.at[pl.ds(2, 2)], sib_in, m1_ss, m1_rs, sibling)
    to_sib_mass.start()
    to_sib_mass.wait_recv()
    own_slab = mp[0] + sib_in[0]
    shared = mp[1] + sib_in[1]
    for i in range(DP):
        ms[i, :, :PART] = own_slab[:, PART * i : PART * (i + 1)]
        ms[i, :, PART:] = jnp.zeros((1, RUN - PART), F32)
        ms[DP + i, :, :PART] = shared[:, PART * i : PART * (i + 1)]
        ms[DP + i, :, PART:] = jnp.zeros((1, RUN - PART), F32)

    m2 = []
    for r in range(1, DP):
        m2.append(rcopy(ms.at[(d + r) % DP], mr.at[d], m2_ss.at[r - 1], m2_rs.at[d], row_peer(r)))
    for r in range(4):
        lo, hi = (d + r) % 4, 4 + (d + r) % 4
        m2.append(rcopy(ms.at[DP + lo], mr.at[DP + d], m2_ss.at[7 + r], m2_rs.at[DP + d], (lo, cent_of(zhi, ym, k))))
        m2.append(rcopy(ms.at[DP + hi], mr.at[DP + d], m2_ss.at[11 + r], m2_rs.at[DP + d], (hi, cent_of(zhi, yp, k))))
    for cp in m2:
        cp.start()
    mr[d] = ms[d]
    for r in range(1, DP):
        src = (d + r) % DP
        rcopy(ms.at[0], mr.at[src], m2_ss.at[0], m2_rs.at[src], row_peer(r)).wait_recv()
    for r in range(DP):
        rcopy(ms.at[0], mr.at[DP + r], m2_ss.at[0], m2_rs.at[DP + r], row_peer(1)).wait_recv()
    mass_v[...] = jnp.sum(mr[...], axis=0)[:, :PART]
    mass_out = pltpu.make_async_copy(mass_v, mass_hbm, o_sem.at[2])
    mass_out.start()

    for cp in [to_up, to_down, to_sib, *fwd_sib, z_first, z_second, y_first, y_second, fwd_y, fwd_z, to_sib_mass, *m2]:
        cp.wait_send()
    for q in (1, 2, 3):
        metas[q].wait_send()
        stats[q].wait_send()
    for r in range(1, DP):
        for g in range(len(RANGES)):
            row_copy(r, g, row_peer(r), d).wait_send()
    cent_out.wait()
    logt_out.wait()
    mass_out.wait()


def hand_on(cent, logt, mass, cent_out, logt_out, mass_out, sem):
    pairs = ((cent, cent_out), (logt, logt_out), (mass, mass_out))
    copies = [pltpu.make_async_copy(src, dst, sem.at[i]) for i, (src, dst) in enumerate(pairs)]
    for cp in copies:
        cp.start()
    for cp in copies:
        cp.wait()


def per_device(embeddings, assignments, parents, starting_coarse_label):
    vmem = pl.BlockSpec(memory_space=pltpu.VMEM)
    hbm = pl.BlockSpec(memory_space=pltpu.HBM)
    dma = pltpu.SemaphoreType.DMA
    cent, logt, mass = pl.pallas_call(
        kernel,
        out_shape=(
            jax.ShapeDtypeStruct((RUN, W), BF16),
            jax.ShapeDtypeStruct((1, RUN), F32),
            jax.ShapeDtypeStruct((1, PART), F32),
        ),
        in_specs=[vmem, vmem, hbm, hbm],
        out_specs=(hbm, hbm, hbm),
        scratch_shapes=[
            pltpu.VMEM((NTILE, ROWS, TILE), BF16),
            pltpu.VMEM((SLOTS, ROWS), BF16),
            pltpu.VMEM((RUN, ROWS), BF16),
            pltpu.VMEM((2, 32, RUN), jnp.int32),
            pltpu.VMEM((DP, CAP, EXT), BF16),
            pltpu.VMEM((DP, CAP, EXT), BF16),
            pltpu.VMEM((NPCH * PCH, W), BF16),
            pltpu.VMEM((4, RUN, W), BF16),
            pltpu.VMEM((4, 8, RUN), F32),
            pltpu.VMEM((NPCH, PCH, 4 * RUN), F32),
            pltpu.VMEM((NPCH, 4 * RUN), F32),
            pltpu.VMEM((NPCH, 4 * RUN), F32),
            pltpu.VMEM((4, 8, RUN), F32),
            pltpu.VMEM((NPCH, 4 * RUN), F32),
            pltpu.VMEM((NPCH, 1, PCH), F32),
            pltpu.VMEM((2, 1, PCH), F32),
            pltpu.VMEM((2 * DP, 1, RUN), F32),
            pltpu.VMEM((2 * DP, 1, RUN), F32),
            pltpu.VMEM((1, RUN), F32),
            pltpu.VMEM((1, PART), F32),
            dma((NTILE,)),
            dma,
            dma((DP - 1, len(RANGES))),
            dma((DP - 1, len(RANGES))),
            dma((5,)),
            dma((5,)),
            dma((6,)),
            dma((6,)),
            dma((3,)),
            dma((3,)),
            dma((3,)),
            dma((3,)),
            dma,
            dma,
            dma((2 * DP - 1,)),
            dma((2 * DP,)),
            dma((3,)),
        ],
        compiler_params=pltpu.CompilerParams(collective_id=0, has_side_effects=True, vmem_limit_bytes=56 << 20),
        name="handover",
    )(
        assignments.reshape(32, RUN),
        starting_coarse_label.reshape(1, RUN),
        embeddings,
        parents,
    )
    cent, logt, mass = pl.pallas_call(
        hand_on,
        out_shape=tuple(jax.ShapeDtypeStruct(v.shape, v.dtype) for v in (cent, logt, mass)),
        in_specs=[hbm, hbm, hbm],
        out_specs=(hbm, hbm, hbm),
        scratch_shapes=[dma((3,))],
        name="finish",
    )(cent, logt, mass)
    return cent, logt.reshape(RUN), mass.reshape(PART)


def solution(mesh):
    return jax.shard_map(
        per_device,
        mesh=mesh,
        in_specs=(P("dp", None), P("dp"), P("cent", None), P(("cent", "dp"))),
        out_specs=(P(("cent", "dp"), None), P(("cent", "dp")), P(("cent", "dp"))),
        check_vma=False,
    )
```

```python
import jax
import jax.numpy as jnp
from jax import lax
from jax.experimental import pallas as pl
from jax.experimental.pallas import tpu as pltpu
from jax.sharding import PartitionSpec as P

MESH = pl.DeviceIdType.MESH
F32 = jnp.float32
BF16 = jnp.bfloat16

W = 1536
RUN = 128
CAP = 48
DP = 8
SLOTS = DP * CAP
EXT = W + RUN
TILE = 256
NTILE = W // TILE
AHEAD = 2
ROWS = 4096
SLAB = 512
PART = 64
PCH = 1024
NPCH = 2
HALF = 256
INV_SOFT = 1.0 / 0.5
REWARD = 1.5

RANGES = ((0, 256), (256, 512), (768, 896))
SEND_AFTER = (0, 2, 5)


def kernel(
    a_ref, label_ref, e_hbm, p_hbm,
    cent_hbm, logt_hbm, mass_hbm,
    e_v, oht, bt, slot_v, send, recv, par, cb, meta, scores, mch, sch, stat, fac, mp, sib_in, ms, mr, logt_v, mass_v,
    e_sem, p_sem, row_ss, row_rs, par_ss, par_rs, cb_ss, cb_rs, meta_ss, meta_rs, stat_ss, stat_rs,
    m1_ss, m1_rs, m2_ss, m2_rs, o_sem,
):
    d = lax.axis_index("dp")
    c = lax.axis_index("cent")
    zlo = d % 2
    zhi = c // 8
    y = (c // 2) % 4
    k = c % 2

    def cent_of(zh, yy, kk):
        return zh * 8 + yy * 2 + kk

    yp, ym, y2 = (y + 1) % 4, (y + 3) % 4, (y + 2) % 4
    flip_d = d - zlo + (1 - zlo)
    group = {
        1: (flip_d, cent_of(1 - zhi, y, k)),
        2: (d, cent_of(zhi, y2, k)),
        3: (flip_d, cent_of(1 - zhi, y2, k)),
    }
    sibling = (d, cent_of(zhi, y, 1 - k))
    up = (d, cent_of(zhi, yp, k))
    down = (d, cent_of(zhi, ym, k))

    def row_peer(r):
        return ((d + r) % DP, c)

    def rcopy(src, dst, ss, rs, dev):
        return pltpu.make_async_remote_copy(
            src_ref=src, dst_ref=dst, send_sem=ss, recv_sem=rs, device_id=dev, device_id_type=MESH
        )

    barrier = pltpu.get_barrier_semaphore()
    mass_from = cent_of(zhi, jnp.where(d < 4, yp, ym), k)
    partners = [row_peer(r) for r in range(1, DP)] + [group[1], group[2], group[3], sibling, up, down]
    partners += [((d + r) % DP, mass_from) for r in range(DP)]
    for dev in partners:
        pl.semaphore_signal(barrier, inc=1, device_id=dev, device_id_type=MESH)

    e_copies = [
        pltpu.make_async_copy(e_hbm.at[:, pl.ds(TILE * n, TILE)], e_v.at[n], e_sem.at[n]) for n in range(NTILE)
    ]
    for cp in e_copies[:AHEAD]:
        cp.start()
    own_par = pltpu.make_async_copy(p_hbm, par.at[pl.ds(0, SLAB)], p_sem)

    a = a_ref[...]
    rel = lax.shift_right_logical(a, 7) - c * DP
    run_id = lax.broadcasted_iota(jnp.int32, (32, 8, RUN), 1)
    member = (rel[:, None, :] == run_id).astype(F32).reshape(256, RUN)
    member_b = member.astype(BF16)
    upper = (
        lax.broadcasted_iota(jnp.int32, (RUN, RUN), 0) < lax.broadcasted_iota(jnp.int32, (RUN, RUN), 1)
    ).astype(F32).astype(BF16)
    ri = lax.broadcasted_iota(jnp.int32, (256, 256), 0)
    ci = lax.broadcasted_iota(jnp.int32, (256, 256), 1)
    before = (((ri & 7) == (ci & 7)) & (ci < ri)).astype(F32).astype(BF16)
    within = jnp.dot(member_b, upper, preferred_element_type=F32)
    earlier = jnp.dot(before, member_b, preferred_element_type=F32).astype(BF16)
    ahead = jnp.dot(earlier, jnp.ones((RUN, RUN), BF16), preferred_element_type=F32)
    base = ((lax.broadcasted_iota(jnp.int32, (256, RUN), 0) & 7) * CAP + 1).astype(F32)
    slot = jnp.sum((member * (within + ahead + base)).reshape(32, 8, RUN), axis=1) - 1.0
    slot_v[0] = slot.astype(jnp.int32)
    slot_v[1] = a & (RUN - 1)

    for cp in e_copies[AHEAD : 2 * AHEAD]:
        cp.start()
    pl.semaphore_wait(barrier, len(partners))

    to_up = rcopy(p_hbm.at[pl.ds(0, HALF)], par.at[pl.ds(SLAB, HALF)], par_ss.at[0], par_rs.at[0], up)
    to_down = rcopy(p_hbm.at[pl.ds(HALF, HALF)], par.at[pl.ds(SLAB + HALF, HALF)], par_ss.at[1], par_rs.at[1], down)
    to_sib = rcopy(p_hbm, par.at[pl.ds(2 * SLAB, SLAB)], par_ss.at[2], par_rs.at[2], sibling)
    fwd_sib = [
        rcopy(
            par.at[pl.ds(SLAB + i * HALF, HALF)],
            par.at[pl.ds(3 * SLAB + i * HALF, HALF)],
            par_ss.at[3 + i],
            par_rs.at[3 + i],
            sibling,
        )
        for i in range(2)
    ]
    to_up.start()
    to_down.start()

    for cp in e_copies[2 * AHEAD :]:
        cp.start()

    def build(b, carry):
        cols = pl.ds(pl.multiple_of(b * RUN, RUN), RUN)
        line = slot_v[0, pl.ds(b, 1), :]
        place = slot_v[1, pl.ds(b, 1), :]
        oht[:, cols] = (lax.broadcasted_iota(jnp.int32, (SLOTS, RUN), 0) == line).astype(F32).astype(BF16)
        bt[:, cols] = (lax.broadcasted_iota(jnp.int32, (RUN, RUN), 0) == place).astype(F32).astype(BF16)
        return carry

    lax.fori_loop(0, ROWS // RUN, build, 0)

    def row_copy(r, g, dev, owner):
        start, size = RANGES[g]
        return rcopy(
            send.at[dev[0], :, pl.ds(start, size)],
            recv.at[owner, :, pl.ds(start, size)],
            row_ss.at[r - 1, g],
            row_rs.at[r - 1, g],
            dev,
        )

    for n in range(NTILE):
        e_copies[n].wait()
        if n == 2:
            own_par.start()
            to_sib.start()
        part = jnp.dot(oht[...], e_v[n], preferred_element_type=F32)
        send[:, :, TILE * n : TILE * (n + 1)] = part.astype(BF16).reshape(DP, CAP, TILE)
        if n == NTILE - 1:
            ext = lax.dot_general(oht[...], bt[...], (((1,), (1,)), ((), ())), preferred_element_type=F32)
            send[:, :, W:] = ext.astype(BF16).reshape(DP, CAP, RUN)
        if n in SEND_AFTER:
            for r in range(1, DP):
                row_copy(r, SEND_AFTER.index(n), row_peer(r), d).start()
    recv[d] = send[d]

    ms[...] = jnp.zeros_like(ms)

    for g in range(len(RANGES)):
        for r in range(1, DP):
            row_copy(r, g, row_peer(r), (d + DP - r) % DP).wait_recv()

    got = recv[...].reshape(SLOTS, EXT)
    onehot = got[:, W:]
    sums = lax.dot_general(onehot, got[:, :W], (((0,), (0,)), ((), ())), preferred_element_type=F32)
    counts_col = lax.dot_general(
        onehot, jnp.ones((SLOTS, RUN), BF16), (((0,), (0,)), ((), ())), preferred_element_type=F32
    )[:, :1]
    counts_row = jnp.sum(onehot.astype(F32), axis=0, keepdims=True)
    mean = sums / jnp.maximum(counts_col, 1.0)
    scale = jnp.sqrt(jnp.sum(mean * mean, axis=1, keepdims=True) + 1e-06)
    normed = (mean / scale).astype(BF16)
    cb[0] = normed
    cent_out = pltpu.make_async_copy(cb.at[0], cent_hbm, o_sem.at[0])
    cent_out.start()
    meta[0, 0:1, :] = counts_row.astype(BF16).astype(F32)
    meta[0, 1:2, :] = label_ref[...].astype(F32)
    meta[0, 2:8, :] = jnp.zeros((6, RUN), F32)

    def half(slot_from, slot_to, h, idx, dev):
        rows = pl.ds(64 * h, 64)
        return rcopy(cb.at[slot_from, rows], cb.at[slot_to, rows], cb_ss.at[idx], cb_rs.at[idx], dev)

    z_first = half(0, 1, 0, 0, group[1])
    z_second = half(0, 1, 1, 1, group[1])
    y_first = half(0, 2, 1, 2, group[2])
    y_second = half(0, 2, 0, 3, group[2])
    fwd_y = half(1, 3, 0, 4, group[2])
    fwd_z = half(2, 3, 1, 5, group[1])
    z_first.start()
    y_first.start()
    metas = {q: rcopy(meta.at[0], meta.at[q], meta_ss.at[q - 1], meta_rs.at[q - 1], group[q]) for q in (1, 2, 3)}
    for q in (1, 2, 3):
        metas[q].start()
    z_second.start()
    y_second.start()

    for r in range(1, DP):
        for g in range(len(RANGES)):
            row_copy(r, g, row_peer(r), d).wait_send()
    to_up.wait_recv()
    fwd_sib[0].start()
    to_down.wait_recv()
    fwd_sib[1].start()
    z_first.wait_recv()
    fwd_y.start()
    y_first.wait_recv()
    fwd_z.start()

    own_par.wait()
    to_sib.wait_recv()
    for cp in fwd_sib:
        cp.wait_recv()
    for q in (1, 2, 3):
        metas[q].wait_recv()

    def parent_ids(i):
        core = jnp.where(i == 0, k, 1 - k)
        mine, low, high = (cent_of(zhi, v, core) * SLAB for v in (y, ym, yp))
        line = lax.broadcasted_iota(jnp.int32, (PCH, 2 * RUN), 0)
        return (line & (SLAB - 1)) + jnp.where(line < SLAB, mine, jnp.where(line < SLAB + HALF, low, high))

    def score(pair):
        cols = pl.ds(2 * RUN * pair, 2 * RUN)
        block = cb[2 * pair : 2 * pair + 2].reshape(2 * RUN, W)
        label = jnp.concatenate([meta[2 * pair, 1:2, :], meta[2 * pair + 1, 1:2, :]], axis=1).astype(jnp.int32)

        def step(i, carry):
            s = lax.dot_general(
                par[pl.ds(pl.multiple_of(i * PCH, PCH), PCH), :], block, (((1,), (1,)), ((), ())), preferred_element_type=F32
            )
            s = s * INV_SOFT + jnp.where(parent_ids(i) == label, REWARD, 0.0)
            top = jnp.max(s, axis=0, keepdims=True)
            e = jnp.exp(s - top)
            scores[i, :, cols] = e
            mch[pl.ds(i, 1), cols] = top
            sch[pl.ds(i, 1), cols] = jnp.sum(e, axis=0, keepdims=True)
            return carry

        lax.fori_loop(0, NPCH, step, 0)

    z_second.wait_recv()
    score(0)
    for cp in [to_up, to_down, to_sib, *fwd_sib, *metas.values(), z_first, z_second, y_first]:
        cp.wait_send()
    cent_out.wait()
    y_second.wait_recv()
    fwd_y.wait_recv()
    fwd_z.wait_recv()
    score(1)

    m_loc = jnp.max(mch[...], axis=0, keepdims=True)
    s_loc = jnp.sum(sch[...] * jnp.exp(mch[...] - m_loc), axis=0, keepdims=True)
    for j in range(4):
        stat[0, j : j + 1, :] = m_loc[:, RUN * j : RUN * (j + 1)]
        stat[0, 4 + j : 5 + j, :] = s_loc[:, RUN * j : RUN * (j + 1)]
    stats = {q: rcopy(stat.at[0], stat.at[q], stat_ss.at[q - 1], stat_rs.at[q - 1], group[q]) for q in (1, 2, 3)}
    for q in (1, 2, 3):
        stats[q].start()
    for cp in [y_second, fwd_y, fwd_z]:
        cp.wait_send()
    for q in (1, 2, 3):
        stats[q].wait_recv()
    for j in range(4):
        m = [stat[q, (j ^ q) : (j ^ q) + 1, :] for q in range(4)]
        s = [stat[q, 4 + (j ^ q) : 5 + (j ^ q), :] for q in range(4)]
        top = jnp.maximum(jnp.maximum(m[0], m[1]), jnp.maximum(m[2], m[3]))
        total = sum(s[q] * jnp.exp(m[q] - top) for q in range(4))
        log_total = top + jnp.log(total)
        if j == 0:
            logt_v[...] = log_total
            logt_out = pltpu.make_async_copy(logt_v, logt_hbm, o_sem.at[1])
            logt_out.start()
        cols = slice(RUN * j, RUN * (j + 1))
        fac[:, cols] = meta[j, 0:1, :] * jnp.exp(mch[:, cols] - log_total)

    def mass_step(i, carry):
        f = fac[pl.ds(i, 1), :]
        acc = jnp.zeros((PCH, RUN), F32)
        for j in range(4):
            acc = acc + scores[i, :, RUN * j : RUN * (j + 1)] * f[:, RUN * j : RUN * (j + 1)]
        mp[i] = jnp.sum(acc.T, axis=0, keepdims=True)
        return carry

    lax.fori_loop(0, NPCH, mass_step, 0)

    to_sib_mass = rcopy(mp.at[1], sib_in, m1_ss, m1_rs, sibling)
    to_sib_mass.start()
    to_sib_mass.wait_recv()
    both = mp[0] + sib_in[...]
    for i in range(2 * DP):
        ms[i, :, :PART] = both[:, PART * i : PART * (i + 1)]

    m2 = []
    for r in range(1, DP):
        m2.append(rcopy(ms.at[(d + r) % DP], mr.at[d], m2_ss.at[r - 1], m2_rs.at[d], row_peer(r)))
    for r in range(4):
        lo, hi = (d + r) % 4, 4 + (d + r) % 4
        m2.append(rcopy(ms.at[DP + lo], mr.at[DP + d], m2_ss.at[7 + r], m2_rs.at[DP + d], (lo, cent_of(zhi, ym, k))))
        m2.append(rcopy(ms.at[DP + hi], mr.at[DP + d], m2_ss.at[11 + r], m2_rs.at[DP + d], (hi, cent_of(zhi, yp, k))))
    for cp in m2:
        cp.start()
    mr[d] = ms[d]
    for r in range(1, DP):
        src = (d + r) % DP
        rcopy(ms.at[0], mr.at[src], m2_ss.at[0], m2_rs.at[src], row_peer(r)).wait_recv()
    for r in range(DP):
        rcopy(ms.at[0], mr.at[DP + r], m2_ss.at[0], m2_rs.at[DP + r], row_peer(1)).wait_recv()
    mass_v[...] = jnp.sum(mr[...], axis=0)[:, :PART]
    mass_out = pltpu.make_async_copy(mass_v, mass_hbm, o_sem.at[2])
    mass_out.start()

    for cp in [to_sib_mass, *stats.values(), *m2]:
        cp.wait_send()
    logt_out.wait()
    mass_out.wait()


def hand_on(cent, logt, mass, cent_out, logt_out, mass_out):
    cent_out[...] = cent[...]
    logt_out[...] = logt[...]
    mass_out[...] = mass[...]


def per_device(embeddings, assignments, parents, starting_coarse_label):
    vmem = pl.BlockSpec(memory_space=pltpu.VMEM)
    hbm = pl.BlockSpec(memory_space=pltpu.HBM)
    dma = pltpu.SemaphoreType.DMA
    cent, logt, mass = pl.pallas_call(
        kernel,
        out_shape=(
            jax.ShapeDtypeStruct((RUN, W), BF16),
            jax.ShapeDtypeStruct((1, RUN), F32),
            jax.ShapeDtypeStruct((1, PART), F32),
        ),
        in_specs=[vmem, vmem, hbm, hbm],
        out_specs=(hbm, hbm, hbm),
        scratch_shapes=[
            pltpu.VMEM((NTILE, ROWS, TILE), BF16),
            pltpu.VMEM((SLOTS, ROWS), BF16),
            pltpu.VMEM((RUN, ROWS), BF16),
            pltpu.VMEM((2, 32, RUN), jnp.int32),
            pltpu.VMEM((DP, CAP, EXT), BF16),
            pltpu.VMEM((DP, CAP, EXT), BF16),
            pltpu.VMEM((NPCH * PCH, W), BF16),
            pltpu.VMEM((4, RUN, W), BF16),
            pltpu.VMEM((4, 8, RUN), F32),
            pltpu.VMEM((NPCH, PCH, 4 * RUN), F32),
            pltpu.VMEM((NPCH, 4 * RUN), F32),
            pltpu.VMEM((NPCH, 4 * RUN), F32),
            pltpu.VMEM((4, 8, RUN), F32),
            pltpu.VMEM((NPCH, 4 * RUN), F32),
            pltpu.VMEM((NPCH, 1, PCH), F32),
            pltpu.VMEM((1, PCH), F32),
            pltpu.VMEM((2 * DP, 1, RUN), F32),
            pltpu.VMEM((2 * DP, 1, RUN), F32),
            pltpu.VMEM((1, RUN), F32),
            pltpu.VMEM((1, PART), F32),
            dma((NTILE,)),
            dma,
            dma((DP - 1, len(RANGES))),
            dma((DP - 1, len(RANGES))),
            dma((5,)),
            dma((5,)),
            dma((6,)),
            dma((6,)),
            dma((3,)),
            dma((3,)),
            dma((3,)),
            dma((3,)),
            dma,
            dma,
            dma((2 * DP - 1,)),
            dma((2 * DP,)),
            dma((3,)),
        ],
        compiler_params=pltpu.CompilerParams(collective_id=0, has_side_effects=True, vmem_limit_bytes=56 << 20),
        name="handover",
    )(
        assignments.reshape(32, RUN),
        starting_coarse_label.reshape(1, RUN),
        embeddings,
        parents,
    )
    cent, logt, mass = pl.pallas_call(
        hand_on,
        out_shape=tuple(jax.ShapeDtypeStruct(v.shape, v.dtype) for v in (cent, logt, mass)),
        in_specs=[vmem, vmem, vmem],
        out_specs=(vmem, vmem, vmem),
        name="finish",
    )(cent, logt, mass)
    return cent, logt.reshape(RUN), mass.reshape(PART)


def solution(mesh):
    return jax.shard_map(
        per_device,
        mesh=mesh,
        in_specs=(P("dp", None), P("dp"), P("cent", None), P(("cent", "dp"))),
        out_specs=(P(("cent", "dp"), None), P(("cent", "dp")), P(("cent", "dp"))),
        check_vma=False,
    )
```

```python
import jax
import jax.numpy as jnp
from jax import lax
from jax.experimental import pallas as pl
from jax.experimental.pallas import tpu as pltpu
from jax.sharding import PartitionSpec as P

MESH = pl.DeviceIdType.MESH
F32 = jnp.float32
BF16 = jnp.bfloat16

W = 1536
RUN = 128
CAP = 48
DP = 8
SLOTS = DP * CAP
TILE = 256
NTILE = W // TILE
AHEAD = 2
ROWS = 4096
SLAB = 512
PART = 64
PCH = 1024
NPCH = 2
HALF = 256
INV_SOFT = 1.0 / 0.5
REWARD = 1.5

RANGES = ((0, 256), (256, 512), (768, 768))
SEND_AFTER = (0, 2, 5)


def kernel(
    a_ref, label_ref, e_hbm, p_hbm,
    cent_hbm, logt_hbm, mr,
    e_v, oht, place, slot_v, send, recv, id_send, id_recv, par, cb, meta, scores, mch, sch, stat, fac, mp, sib_in, ms, logt_v,
    e_sem, p_sem, row_ss, row_rs, id_ss, id_rs, par_ss, par_rs, cb_ss, cb_rs, meta_ss, meta_rs, stat_ss, stat_rs,
    m1_ss, m1_rs, m2_ss, m2_rs, o_sem,
):
    d = lax.axis_index("dp")
    c = lax.axis_index("cent")
    zlo = d % 2
    zhi = c // 8
    y = (c // 2) % 4
    k = c % 2

    def cent_of(zh, yy, kk):
        return zh * 8 + yy * 2 + kk

    yp, ym, y2 = (y + 1) % 4, (y + 3) % 4, (y + 2) % 4
    flip_d = d - zlo + (1 - zlo)
    group = {
        1: (flip_d, cent_of(1 - zhi, y, k)),
        2: (d, cent_of(zhi, y2, k)),
        3: (flip_d, cent_of(1 - zhi, y2, k)),
    }
    sibling = (d, cent_of(zhi, y, 1 - k))
    up = (d, cent_of(zhi, yp, k))
    down = (d, cent_of(zhi, ym, k))

    def row_peer(r):
        return ((d + r) % DP, c)

    def rcopy(src, dst, ss, rs, dev):
        return pltpu.make_async_remote_copy(
            src_ref=src, dst_ref=dst, send_sem=ss, recv_sem=rs, device_id=dev, device_id_type=MESH
        )

    barrier = pltpu.get_barrier_semaphore()
    mass_from = cent_of(zhi, jnp.where(d < 4, yp, ym), k)
    partners = [row_peer(r) for r in range(1, DP)] + [group[1], group[2], group[3], sibling, up, down]
    partners += [((d + r) % DP, mass_from) for r in range(DP)]
    for dev in partners:
        pl.semaphore_signal(barrier, inc=1, device_id=dev, device_id_type=MESH)

    e_copies = [
        pltpu.make_async_copy(e_hbm.at[:, pl.ds(TILE * n, TILE)], e_v.at[n], e_sem.at[n]) for n in range(NTILE)
    ]
    for cp in e_copies[:AHEAD]:
        cp.start()
    own_par = pltpu.make_async_copy(p_hbm, par.at[pl.ds(0, SLAB)], p_sem)

    a = a_ref[...]
    rel = lax.shift_right_logical(a, 7) - c * DP
    run_id = lax.broadcasted_iota(jnp.int32, (32, 8, RUN), 1)
    member = (rel[:, None, :] == run_id).astype(F32).reshape(256, RUN)
    member_b = member.astype(BF16)
    upper = (
        lax.broadcasted_iota(jnp.int32, (RUN, RUN), 0) < lax.broadcasted_iota(jnp.int32, (RUN, RUN), 1)
    ).astype(F32).astype(BF16)
    ri = lax.broadcasted_iota(jnp.int32, (256, 256), 0)
    ci = lax.broadcasted_iota(jnp.int32, (256, 256), 1)
    before = (((ri & 7) == (ci & 7)) & (ci < ri)).astype(F32).astype(BF16)
    within = jnp.dot(member_b, upper, preferred_element_type=F32)
    earlier = jnp.dot(before, member_b, preferred_element_type=F32).astype(BF16)
    ahead = jnp.dot(earlier, jnp.ones((RUN, RUN), BF16), preferred_element_type=F32)
    base = ((lax.broadcasted_iota(jnp.int32, (256, RUN), 0) & 7) * CAP + 1).astype(F32)
    slot = jnp.sum((member * (within + ahead + base)).reshape(32, 8, RUN), axis=1) - 1.0
    slot_v[...] = slot.astype(jnp.int32)
    spot = ((a & (RUN - 1)) + 1).astype(F32)
    for b in range(ROWS // RUN):
        place[:, RUN * b : RUN * (b + 1)] = jnp.broadcast_to(spot[b : b + 1, :], (16, RUN)).astype(BF16)

    for cp in e_copies[AHEAD:]:
        cp.start()

    to_up = rcopy(p_hbm.at[pl.ds(0, HALF)], par.at[pl.ds(SLAB, HALF)], par_ss.at[0], par_rs.at[0], up)
    to_down = rcopy(p_hbm.at[pl.ds(HALF, HALF)], par.at[pl.ds(SLAB + HALF, HALF)], par_ss.at[1], par_rs.at[1], down)
    to_sib = rcopy(p_hbm, par.at[pl.ds(2 * SLAB, SLAB)], par_ss.at[2], par_rs.at[2], sibling)
    fwd_sib = [
        rcopy(
            par.at[pl.ds(SLAB + i * HALF, HALF)],
            par.at[pl.ds(3 * SLAB + i * HALF, HALF)],
            par_ss.at[3 + i],
            par_rs.at[3 + i],
            sibling,
        )
        for i in range(2)
    ]
    def build(b, carry):
        cols = pl.ds(pl.multiple_of(b * RUN, RUN), RUN)
        line = slot_v[pl.ds(b, 1), :]
        oht[:, cols] = (lax.broadcasted_iota(jnp.int32, (SLOTS, RUN), 0) == line).astype(F32).astype(BF16)
        return carry

    lax.fori_loop(0, ROWS // RUN, build, 0)

    def row_copy(r, g, dev, owner):
        start, size = RANGES[g]
        return rcopy(
            send.at[dev[0], :, pl.ds(start, size)],
            recv.at[owner, :, pl.ds(start, size)],
            row_ss.at[g],
            row_rs.at[g],
            dev,
        )

    def row_total(g):
        start, size = RANGES[g]
        cols = pl.ds(start, size)
        part = pl.ds(0, DP - 1)
        return rcopy(send.at[part, :, cols], recv.at[part, :, cols], row_ss.at[g], row_rs.at[g], row_peer(1))

    id_total = rcopy(id_send.at[pl.ds(0, DP - 1)], id_recv.at[pl.ds(0, DP - 1)], id_ss, id_rs, row_peer(1))

    for n in range(NTILE):
        e_copies[n].wait()
        part = jnp.dot(oht[...], e_v[n], preferred_element_type=F32)
        send[:, :, TILE * n : TILE * (n + 1)] = part.astype(BF16).reshape(DP, CAP, TILE)
        if n == 0:
            pl.semaphore_wait(barrier, len(partners))
        if n in SEND_AFTER:
            for r in range(1, DP):
                row_copy(r, SEND_AFTER.index(n), row_peer(r), d).start()
        if n == 0:
            to_up.start()
            to_down.start()
        if n == 2:
            own_par.start()
            to_sib.start()
            spots = lax.dot_general(place[...], oht[...], (((1,), (1,)), ((), ())), preferred_element_type=F32)[:8]
            lane = lax.broadcasted_iota(jnp.int32, (DP, SLOTS), 1)
            mine = jnp.where(lane // CAP == lax.broadcasted_iota(jnp.int32, (DP, SLOTS), 0), spots, 0.0).astype(BF16)
            lo = lax.broadcasted_iota(jnp.int32, (SLOTS, SLOTS), 0)
            hi = lax.broadcasted_iota(jnp.int32, (SLOTS, SLOTS), 1)
            shift = ((lo % CAP == hi % CAP) & (hi // CAP == d)).astype(F32).astype(BF16)
            moved = jnp.dot(mine, shift, preferred_element_type=F32)
            for i in range(DP):
                id_send[i] = moved[i : i + 1, :]
            for r in range(1, DP):
                dev = row_peer(r)
                rcopy(id_send.at[dev[0]], id_recv.at[d], id_ss, id_rs, dev).start()
    recv[d] = send[d]
    id_recv[d] = id_send[d]
    ms[...] = jnp.zeros_like(ms)

    id_total.wait_recv()
    ids = jnp.sum(id_recv[...], axis=0).astype(jnp.int32) - 1
    onehot = (lax.broadcasted_iota(jnp.int32, (RUN, SLOTS), 0) == ids).astype(F32)
    counts_col = jnp.sum(onehot, axis=1, keepdims=True)
    onehot = onehot.astype(BF16)
    counts_row = lax.dot_general(jnp.ones((16, SLOTS), BF16), onehot, (((1,), (1,)), ((), ())), preferred_element_type=F32)[:1]
    for g in range(len(RANGES)):
        row_total(g).wait_recv()
    sums = jnp.dot(onehot, recv[...].reshape(SLOTS, W), preferred_element_type=F32)
    mean = sums / jnp.maximum(counts_col, 1.0)
    scale = jnp.sqrt(jnp.sum(mean * mean, axis=1, keepdims=True) + 1e-06)
    normed = (mean / scale).astype(BF16)
    cb[0] = normed
    cent_out = pltpu.make_async_copy(cb.at[0], cent_hbm, o_sem.at[0])
    cent_out.start()
    meta[0, 0:1, :] = counts_row.astype(BF16).astype(F32)
    meta[0, 1:2, :] = label_ref[...].astype(F32)
    meta[0, 2:8, :] = jnp.zeros((6, RUN), F32)

    def half(slot_from, slot_to, h, idx, dev):
        rows = pl.ds(64 * h, 64)
        return rcopy(cb.at[slot_from, rows], cb.at[slot_to, rows], cb_ss.at[idx], cb_rs.at[idx], dev)

    z_first = half(0, 1, 0, 0, group[1])
    z_second = half(0, 1, 1, 1, group[1])
    y_first = half(0, 2, 1, 2, group[2])
    y_second = half(0, 2, 0, 3, group[2])
    fwd_y = half(1, 3, 0, 4, group[2])
    fwd_z = half(2, 3, 1, 5, group[1])
    z_first.start()
    y_first.start()
    metas = {q: rcopy(meta.at[0], meta.at[q], meta_ss.at[q - 1], meta_rs.at[q - 1], group[q]) for q in (1, 2, 3)}
    for q in (1, 2, 3):
        metas[q].start()
    z_second.start()
    y_second.start()

    for g in range(len(RANGES)):
        row_total(g).wait_send()
    id_total.wait_send()
    to_up.wait_recv()
    fwd_sib[0].start()
    to_down.wait_recv()
    fwd_sib[1].start()
    z_first.wait_recv()
    fwd_y.start()
    y_first.wait_recv()
    fwd_z.start()

    own_par.wait()
    to_sib.wait_recv()
    for cp in fwd_sib:
        cp.wait_recv()
    for q in (1, 2, 3):
        metas[q].wait_recv()

    def parent_ids(i):
        core = jnp.where(i == 0, k, 1 - k)
        mine, low, high = (cent_of(zhi, v, core) * SLAB for v in (y, ym, yp))
        line = lax.broadcasted_iota(jnp.int32, (PCH, 2 * RUN), 0)
        return (line & (SLAB - 1)) + jnp.where(line < SLAB, mine, jnp.where(line < SLAB + HALF, low, high))

    def score(pair):
        cols = pl.ds(2 * RUN * pair, 2 * RUN)
        block = cb[2 * pair : 2 * pair + 2].reshape(2 * RUN, W)
        label = jnp.concatenate([meta[2 * pair, 1:2, :], meta[2 * pair + 1, 1:2, :]], axis=1).astype(jnp.int32)

        def step(i, carry):
            s = lax.dot_general(
                par[pl.ds(pl.multiple_of(i * PCH, PCH), PCH), :], block, (((1,), (1,)), ((), ())), preferred_element_type=F32
            )
            s = s * INV_SOFT + jnp.where(parent_ids(i) == label, REWARD, 0.0)
            top = jnp.max(s, axis=0, keepdims=True)
            e = jnp.exp(s - top)
            scores[i, :, cols] = e
            mch[pl.ds(i, 1), cols] = top
            sch[pl.ds(i, 1), cols] = jnp.sum(e, axis=0, keepdims=True)
            return carry

        lax.fori_loop(0, NPCH, step, 0)

    z_second.wait_recv()
    score(0)
    for cp in [to_up, to_down, to_sib, *fwd_sib, *metas.values(), z_first, z_second, y_first]:
        cp.wait_send()
    cent_out.wait()
    y_second.wait_recv()
    fwd_y.wait_recv()
    fwd_z.wait_recv()
    score(1)

    m_loc = jnp.max(mch[...], axis=0, keepdims=True)
    s_loc = jnp.sum(sch[...] * jnp.exp(mch[...] - m_loc), axis=0, keepdims=True)
    for j in range(4):
        stat[0, j : j + 1, :] = m_loc[:, RUN * j : RUN * (j + 1)]
        stat[0, 4 + j : 5 + j, :] = s_loc[:, RUN * j : RUN * (j + 1)]
    stats = {q: rcopy(stat.at[0], stat.at[q], stat_ss.at[q - 1], stat_rs.at[q - 1], group[q]) for q in (1, 2, 3)}
    for q in (1, 2, 3):
        stats[q].start()
    for cp in [y_second, fwd_y, fwd_z]:
        cp.wait_send()
    for q in (1, 2, 3):
        stats[q].wait_recv()
    for j in range(4):
        m = [stat[q, (j ^ q) : (j ^ q) + 1, :] for q in range(4)]
        s = [stat[q, 4 + (j ^ q) : 5 + (j ^ q), :] for q in range(4)]
        top = jnp.maximum(jnp.maximum(m[0], m[1]), jnp.maximum(m[2], m[3]))
        total = sum(s[q] * jnp.exp(m[q] - top) for q in range(4))
        log_total = top + jnp.log(total)
        if j == 0:
            logt_v[...] = log_total
            logt_out = pltpu.make_async_copy(logt_v, logt_hbm, o_sem.at[1])
            logt_out.start()
        cols = slice(RUN * j, RUN * (j + 1))
        fac[:, cols] = meta[j, 0:1, :] * jnp.exp(mch[:, cols] - log_total)

    def mass_step(i, carry):
        f = fac[pl.ds(i, 1), :]
        acc = jnp.zeros((PCH, RUN), F32)
        for j in range(4):
            acc = acc + scores[i, :, RUN * j : RUN * (j + 1)] * f[:, RUN * j : RUN * (j + 1)]
        mp[i] = jnp.sum(acc.T, axis=0, keepdims=True)
        return carry

    lax.fori_loop(0, NPCH, mass_step, 0)

    to_sib_mass = rcopy(mp.at[1], sib_in, m1_ss, m1_rs, sibling)
    to_sib_mass.start()
    to_sib_mass.wait_recv()
    both = mp[0] + sib_in[...]
    for i in range(2 * DP):
        ms[i, :, :PART] = both[:, PART * i : PART * (i + 1)]

    def mass_copy(line, to_line, dev):
        rcopy(ms.at[line], mr.at[to_line], m2_ss, m2_rs, dev).start()

    for r in range(4):
        lo, hi = (d + r) % 4, 4 + (d + r) % 4
        mass_copy(DP + lo, DP + d, (lo, cent_of(zhi, ym, k)))
        mass_copy(DP + hi, DP + d, (hi, cent_of(zhi, yp, k)))
    for r in range(1, DP):
        mass_copy((d + r) % DP, d, row_peer(r))
    own_mass = pltpu.make_async_copy(ms.at[d], mr.at[d], o_sem.at[2])
    own_mass.start()
    for cp in [to_sib_mass, *stats.values()]:
        cp.wait_send()
    logt_out.wait()
    own_mass.wait()
    lines = pl.ds(0, 2 * DP - 1)
    rcopy(ms.at[lines], mr.at[lines], m2_ss, m2_rs, row_peer(1)).wait()


def hand_on(cent, logt, terms, cent_out, logt_out, mass_out):
    cent_out[...] = cent[...]
    logt_out[...] = logt[...]
    mass_out[...] = jnp.sum(terms[...], axis=0)[:, :PART]


def per_device(embeddings, assignments, parents, starting_coarse_label):
    vmem = pl.BlockSpec(memory_space=pltpu.VMEM)
    hbm = pl.BlockSpec(memory_space=pltpu.HBM)
    anywhere = pl.BlockSpec(memory_space=pl.ANY)
    dma = pltpu.SemaphoreType.DMA
    cent, logt, terms = pl.pallas_call(
        kernel,
        out_shape=(
            jax.ShapeDtypeStruct((RUN, W), BF16),
            jax.ShapeDtypeStruct((1, RUN), F32),
            jax.ShapeDtypeStruct((2 * DP, 1, RUN), F32),
        ),
        in_specs=[vmem, vmem, hbm, hbm],
        out_specs=(anywhere, anywhere, anywhere),
        scratch_shapes=[
            pltpu.VMEM((NTILE, ROWS, TILE), BF16),
            pltpu.VMEM((SLOTS, ROWS), BF16),
            pltpu.VMEM((16, ROWS), BF16),
            pltpu.VMEM((32, RUN), jnp.int32),
            pltpu.VMEM((DP, CAP, W), BF16),
            pltpu.VMEM((DP, CAP, W), BF16),
            pltpu.VMEM((DP, 1, SLOTS), F32),
            pltpu.VMEM((DP, 1, SLOTS), F32),
            pltpu.VMEM((NPCH * PCH, W), BF16),
            pltpu.VMEM((4, RUN, W), BF16),
            pltpu.VMEM((4, 8, RUN), F32),
            pltpu.VMEM((NPCH, PCH, 4 * RUN), F32),
            pltpu.VMEM((NPCH, 4 * RUN), F32),
            pltpu.VMEM((NPCH, 4 * RUN), F32),
            pltpu.VMEM((4, 8, RUN), F32),
            pltpu.VMEM((NPCH, 4 * RUN), F32),
            pltpu.VMEM((NPCH, 1, PCH), F32),
            pltpu.VMEM((1, PCH), F32),
            pltpu.VMEM((2 * DP, 1, RUN), F32),
            pltpu.VMEM((1, RUN), F32),
            dma((NTILE,)),
            dma,
            dma((len(RANGES),)),
            dma((len(RANGES),)),
            dma,
            dma,
            dma((5,)),
            dma((5,)),
            dma((6,)),
            dma((6,)),
            dma((3,)),
            dma((3,)),
            dma((3,)),
            dma((3,)),
            dma,
            dma,
            dma,
            dma,
            dma((3,)),
        ],
        compiler_params=pltpu.CompilerParams(collective_id=0, has_side_effects=True, vmem_limit_bytes=53 << 20),
        name="handover",
    )(
        assignments.reshape(32, RUN),
        starting_coarse_label.reshape(1, RUN),
        embeddings,
        parents,
    )
    cent, logt, mass = pl.pallas_call(
        hand_on,
        out_shape=(
            jax.ShapeDtypeStruct((RUN, W), BF16),
            jax.ShapeDtypeStruct((1, RUN), F32),
            jax.ShapeDtypeStruct((1, PART), F32),
        ),
        in_specs=[vmem, vmem, vmem],
        out_specs=(vmem, vmem, vmem),
        compiler_params=pltpu.CompilerParams(vmem_limit_bytes=2 << 20),
        name="finish",
    )(cent, logt, terms)
    return cent, logt.reshape(RUN), mass.reshape(PART)


def solution(mesh):
    return jax.shard_map(
        per_device,
        mesh=mesh,
        in_specs=(P("dp", None), P("dp"), P("cent", None), P(("cent", "dp"))),
        out_specs=(P(("cent", "dp"), None), P(("cent", "dp")), P(("cent", "dp"))),
        check_vma=False,
    )
```

```python
import jax
import jax.numpy as jnp
from jax import lax
from jax.experimental import pallas as pl
from jax.experimental.pallas import tpu as pltpu
from jax.sharding import PartitionSpec as P

MESH = pl.DeviceIdType.MESH
F32 = jnp.float32
BF16 = jnp.bfloat16

W = 1536
RUN = 128
CAP = 48
DP = 8
SLOTS = DP * CAP
TILE = 256
NTILE = W // TILE
ROWS = 4096
SLAB = 512
PART = 64
PCH = 1024
NPCH = 2
HALF = 256
INV_SOFT = 1.0 / 0.5
REWARD = 1.5

RANGES = ((0, 256), (256, 512), (768, 768))
SEND_AFTER = (0, 2, 5)


def kernel(
    a_hbm, label_hbm, e_hbm, p_hbm,
    cent_hbm, logt_hbm, mr,
    a_v, label_v, e_v, oht, place, slot_v, send, recv, id_send, id_recv, par, cb, meta, scores, mch, sch, stat, fac, mp, sib_in, ms, logt_v,
    e_sem, p_sem, row_ss, row_rs, id_ss, id_rs, par_ss, par_rs, cb_ss, cb_rs, meta_ss, meta_rs, stat_ss, stat_rs,
    m1_ss, m1_rs, m2_ss, m2_rs, o_sem, in_sem,
):
    d = lax.axis_index("dp")
    c = lax.axis_index("cent")
    zlo = d % 2
    zhi = c // 8
    y = (c // 2) % 4
    k = c % 2

    def cent_of(zh, yy, kk):
        return zh * 8 + yy * 2 + kk

    yp, ym, y2 = (y + 1) % 4, (y + 3) % 4, (y + 2) % 4
    flip_d = d - zlo + (1 - zlo)
    group = {
        1: (flip_d, cent_of(1 - zhi, y, k)),
        2: (d, cent_of(zhi, y2, k)),
        3: (flip_d, cent_of(1 - zhi, y2, k)),
    }
    sibling = (d, cent_of(zhi, y, 1 - k))
    up = (d, cent_of(zhi, yp, k))
    down = (d, cent_of(zhi, ym, k))

    def row_peer(r):
        return ((d + r) % DP, c)

    def rcopy(src, dst, ss, rs, dev):
        return pltpu.make_async_remote_copy(
            src_ref=src, dst_ref=dst, send_sem=ss, recv_sem=rs, device_id=dev, device_id_type=MESH
        )

    load_a = pltpu.make_async_copy(a_hbm, a_v, in_sem.at[0])
    load_label = pltpu.make_async_copy(label_hbm, label_v, in_sem.at[1])
    e_copies = [
        pltpu.make_async_copy(e_hbm.at[:, pl.ds(TILE * n, TILE)], e_v.at[n], e_sem.at[n]) for n in range(NTILE)
    ]
    own_par = pltpu.make_async_copy(p_hbm, par.at[pl.ds(0, SLAB)], p_sem)
    load_a.start()
    e_copies[0].start()

    barrier = pltpu.get_barrier_semaphore()
    mass_from = cent_of(zhi, jnp.where(d < 4, yp, ym), k)
    partners = [row_peer(r) for r in range(1, DP)] + [group[1], group[2], group[3], sibling, up, down]
    partners += [((d + r) % DP, mass_from) for r in range(DP)]
    for dev in partners:
        pl.semaphore_signal(barrier, inc=1, device_id=dev, device_id_type=MESH)

    e_copies[1].start()
    load_label.start()
    load_a.wait()

    a = a_v[...]
    rel = lax.shift_right_logical(a, 7) - c * DP
    run_id = lax.broadcasted_iota(jnp.int32, (32, 8, RUN), 1)
    member = (rel[:, None, :] == run_id).astype(F32).reshape(256, RUN)
    member_b = member.astype(BF16)
    upper = (
        lax.broadcasted_iota(jnp.int32, (RUN, RUN), 0) < lax.broadcasted_iota(jnp.int32, (RUN, RUN), 1)
    ).astype(F32).astype(BF16)
    ri = lax.broadcasted_iota(jnp.int32, (256, 256), 0)
    ci = lax.broadcasted_iota(jnp.int32, (256, 256), 1)
    before = (((ri & 7) == (ci & 7)) & (ci < ri)).astype(F32).astype(BF16)
    within = jnp.dot(member_b, upper, preferred_element_type=F32)
    earlier = jnp.dot(before, member_b, preferred_element_type=F32).astype(BF16)
    ahead = jnp.dot(earlier, jnp.ones((RUN, RUN), BF16), preferred_element_type=F32)
    base = ((lax.broadcasted_iota(jnp.int32, (256, RUN), 0) & 7) * CAP + 1).astype(F32)
    slot = jnp.sum((member * (within + ahead + base)).reshape(32, 8, RUN), axis=1) - 1.0
    slot_v[...] = slot.astype(jnp.int32)
    spot = ((a & (RUN - 1)) + 1).astype(F32)
    for b in range(ROWS // RUN):
        place[:, RUN * b : RUN * (b + 1)] = jnp.broadcast_to(spot[b : b + 1, :], (16, RUN)).astype(BF16)

    to_up = rcopy(p_hbm.at[pl.ds(0, HALF)], par.at[pl.ds(SLAB, HALF)], par_ss.at[0], par_rs.at[0], up)
    to_down = rcopy(p_hbm.at[pl.ds(HALF, HALF)], par.at[pl.ds(SLAB + HALF, HALF)], par_ss.at[1], par_rs.at[1], down)
    to_sib = rcopy(p_hbm, par.at[pl.ds(2 * SLAB, SLAB)], par_ss.at[2], par_rs.at[2], sibling)
    fwd_sib = [
        rcopy(
            par.at[pl.ds(SLAB + i * HALF, HALF)],
            par.at[pl.ds(3 * SLAB + i * HALF, HALF)],
            par_ss.at[3 + i],
            par_rs.at[3 + i],
            sibling,
        )
        for i in range(2)
    ]
    def build(b, carry):
        cols = pl.ds(pl.multiple_of(b * RUN, RUN), RUN)
        line = slot_v[pl.ds(b, 1), :]
        oht[:, cols] = (lax.broadcasted_iota(jnp.int32, (SLOTS, RUN), 0) == line).astype(F32).astype(BF16)
        return carry

    lax.fori_loop(0, ROWS // RUN, build, 0)

    for cp in e_copies[2:]:
        cp.start()

    def row_copy(r, g, dev, owner):
        start, size = RANGES[g]
        return rcopy(
            send.at[dev[0], :, pl.ds(start, size)],
            recv.at[owner, :, pl.ds(start, size)],
            row_ss.at[g],
            row_rs.at[g],
            dev,
        )

    def row_total(g):
        start, size = RANGES[g]
        cols = pl.ds(start, size)
        part = pl.ds(0, DP - 1)
        return rcopy(send.at[part, :, cols], recv.at[part, :, cols], row_ss.at[g], row_rs.at[g], row_peer(1))

    id_total = rcopy(id_send.at[pl.ds(0, DP - 1)], id_recv.at[pl.ds(0, DP - 1)], id_ss, id_rs, row_peer(1))

    for n in range(NTILE):
        e_copies[n].wait()
        part = jnp.dot(oht[...], e_v[n], preferred_element_type=F32)
        send[:, :, TILE * n : TILE * (n + 1)] = part.astype(BF16).reshape(DP, CAP, TILE)
        if n == 0:
            pl.semaphore_wait(barrier, len(partners))
        if n in SEND_AFTER:
            for r in range(1, DP):
                row_copy(r, SEND_AFTER.index(n), row_peer(r), d).start()
        if n == 0:
            to_up.start()
            to_down.start()
        if n == 2:
            own_par.start()
            to_sib.start()
            spots = lax.dot_general(place[...], oht[...], (((1,), (1,)), ((), ())), preferred_element_type=F32)[:8]
            lane = lax.broadcasted_iota(jnp.int32, (DP, SLOTS), 1)
            mine = jnp.where(lane // CAP == lax.broadcasted_iota(jnp.int32, (DP, SLOTS), 0), spots, 0.0).astype(BF16)
            lo = lax.broadcasted_iota(jnp.int32, (SLOTS, SLOTS), 0)
            hi = lax.broadcasted_iota(jnp.int32, (SLOTS, SLOTS), 1)
            shift = ((lo % CAP == hi % CAP) & (hi // CAP == d)).astype(F32).astype(BF16)
            moved = jnp.dot(mine, shift, preferred_element_type=F32)
            for i in range(DP):
                id_send[i] = moved[i : i + 1, :]
            for r in range(1, DP):
                dev = row_peer(r)
                rcopy(id_send.at[dev[0]], id_recv.at[d], id_ss, id_rs, dev).start()
    recv[d] = send[d]
    id_recv[d] = id_send[d]
    ms[...] = jnp.zeros_like(ms)

    id_total.wait_recv()
    ids = jnp.sum(id_recv[...], axis=0).astype(jnp.int32) - 1
    onehot = (lax.broadcasted_iota(jnp.int32, (RUN, SLOTS), 0) == ids).astype(F32)
    counts_col = jnp.sum(onehot, axis=1, keepdims=True)
    onehot = onehot.astype(BF16)
    counts_row = lax.dot_general(jnp.ones((16, SLOTS), BF16), onehot, (((1,), (1,)), ((), ())), preferred_element_type=F32)[:1]
    for g in range(len(RANGES)):
        row_total(g).wait_recv()
    sums = jnp.dot(onehot, recv[...].reshape(SLOTS, W), preferred_element_type=F32)
    mean = sums / jnp.maximum(counts_col, 1.0)
    scale = jnp.sqrt(jnp.sum(mean * mean, axis=1, keepdims=True) + 1e-06)
    normed = (mean / scale).astype(BF16)
    cb[0] = normed
    cent_out = pltpu.make_async_copy(cb.at[0], cent_hbm, o_sem.at[0])
    cent_out.start()
    load_label.wait()
    meta[0, 0:1, :] = counts_row.astype(BF16).astype(F32)
    meta[0, 1:2, :] = label_v[...].astype(F32)
    meta[0, 2:8, :] = jnp.zeros((6, RUN), F32)

    def half(slot_from, slot_to, h, idx, dev):
        rows = pl.ds(64 * h, 64)
        return rcopy(cb.at[slot_from, rows], cb.at[slot_to, rows], cb_ss.at[idx], cb_rs.at[idx], dev)

    z_first = half(0, 1, 0, 0, group[1])
    z_second = half(0, 1, 1, 1, group[1])
    y_first = half(0, 2, 1, 2, group[2])
    y_second = half(0, 2, 0, 3, group[2])
    fwd_y = half(1, 3, 0, 4, group[2])
    fwd_z = half(2, 3, 1, 5, group[1])
    z_first.start()
    y_first.start()
    metas = {q: rcopy(meta.at[0], meta.at[q], meta_ss.at[q - 1], meta_rs.at[q - 1], group[q]) for q in (1, 2, 3)}
    for q in (3, 2, 1):
        metas[q].start()
    z_second.start()
    y_second.start()

    for g in range(len(RANGES)):
        row_total(g).wait_send()
    id_total.wait_send()
    to_up.wait_recv()
    fwd_sib[0].start()
    to_down.wait_recv()
    fwd_sib[1].start()
    z_first.wait_recv()
    fwd_y.start()
    y_first.wait_recv()
    fwd_z.start()

    own_par.wait()
    to_sib.wait_recv()
    for cp in fwd_sib:
        cp.wait_recv()
    for q in (1, 2, 3):
        metas[q].wait_recv()

    def parent_ids(i):
        core = jnp.where(i == 0, k, 1 - k)
        mine, low, high = (cent_of(zhi, v, core) * SLAB for v in (y, ym, yp))
        line = lax.broadcasted_iota(jnp.int32, (PCH, 2 * RUN), 0)
        return (line & (SLAB - 1)) + jnp.where(line < SLAB, mine, jnp.where(line < SLAB + HALF, low, high))

    def score(pair):
        cols = pl.ds(2 * RUN * pair, 2 * RUN)
        block = cb[2 * pair : 2 * pair + 2].reshape(2 * RUN, W)
        label = jnp.concatenate([meta[2 * pair, 1:2, :], meta[2 * pair + 1, 1:2, :]], axis=1).astype(jnp.int32)

        def step(i, carry):
            s = lax.dot_general(
                par[pl.ds(pl.multiple_of(i * PCH, PCH), PCH), :], block, (((1,), (1,)), ((), ())), preferred_element_type=F32
            )
            s = s * INV_SOFT + jnp.where(parent_ids(i) == label, REWARD, 0.0)
            top = jnp.max(s, axis=0, keepdims=True)
            e = jnp.exp(s - top)
            scores[i, :, cols] = e
            mch[pl.ds(i, 1), cols] = top
            sch[pl.ds(i, 1), cols] = jnp.sum(e, axis=0, keepdims=True)
            return carry

        lax.fori_loop(0, NPCH, step, 0)

    z_second.wait_recv()
    score(0)
    for cp in [to_up, to_down, to_sib, *fwd_sib, *metas.values(), z_first, z_second, y_first]:
        cp.wait_send()
    cent_out.wait()
    y_second.wait_recv()
    fwd_y.wait_recv()
    fwd_z.wait_recv()
    score(1)

    m_loc = jnp.max(mch[...], axis=0, keepdims=True)
    s_loc = jnp.sum(sch[...] * jnp.exp(mch[...] - m_loc), axis=0, keepdims=True)
    for j in range(4):
        stat[0, j : j + 1, :] = m_loc[:, RUN * j : RUN * (j + 1)]
        stat[0, 4 + j : 5 + j, :] = s_loc[:, RUN * j : RUN * (j + 1)]
    stats = {q: rcopy(stat.at[0], stat.at[q], stat_ss.at[q - 1], stat_rs.at[q - 1], group[q]) for q in (1, 2, 3)}
    for q in (3, 2, 1):
        stats[q].start()
    for cp in [y_second, fwd_y, fwd_z]:
        cp.wait_send()
    for q in (1, 2, 3):
        stats[q].wait_recv()
    for j in range(4):
        m = [stat[q, (j ^ q) : (j ^ q) + 1, :] for q in range(4)]
        s = [stat[q, 4 + (j ^ q) : 5 + (j ^ q), :] for q in range(4)]
        top = jnp.maximum(jnp.maximum(m[0], m[1]), jnp.maximum(m[2], m[3]))
        total = sum(s[q] * jnp.exp(m[q] - top) for q in range(4))
        log_total = top + jnp.log(total)
        if j == 0:
            logt_v[...] = log_total
            logt_out = pltpu.make_async_copy(logt_v, logt_hbm, o_sem.at[1])
            logt_out.start()
        cols = slice(RUN * j, RUN * (j + 1))
        fac[:, cols] = meta[j, 0:1, :] * jnp.exp(mch[:, cols] - log_total)

    def mass_step(i, carry):
        f = fac[pl.ds(i, 1), :]
        acc = jnp.zeros((PCH, RUN), F32)
        for j in range(4):
            acc = acc + scores[i, :, RUN * j : RUN * (j + 1)] * f[:, RUN * j : RUN * (j + 1)]
        mp[i] = jnp.sum(acc.T, axis=0, keepdims=True)
        return carry

    lax.fori_loop(0, NPCH, mass_step, 0)

    to_sib_mass = rcopy(mp.at[1], sib_in, m1_ss, m1_rs, sibling)
    to_sib_mass.start()
    to_sib_mass.wait_recv()
    both = mp[0] + sib_in[...]
    for i in range(2 * DP):
        ms[i, :, :PART] = both[:, PART * i : PART * (i + 1)]

    def mass_copy(line, to_line, dev):
        rcopy(ms.at[line], mr.at[to_line], m2_ss, m2_rs, dev).start()

    for r in range(4):
        lo, hi = (d + r) % 4, 4 + (d + r) % 4
        mass_copy(DP + lo, DP + d, (lo, cent_of(zhi, ym, k)))
        mass_copy(DP + hi, DP + d, (hi, cent_of(zhi, yp, k)))
    for r in range(1, DP):
        mass_copy((d + r) % DP, d, row_peer(r))
    own_mass = pltpu.make_async_copy(ms.at[d], mr.at[d], o_sem.at[2])
    own_mass.start()
    for cp in [to_sib_mass, *stats.values()]:
        cp.wait_send()
    logt_out.wait()
    own_mass.wait()
    lines = pl.ds(0, 2 * DP - 1)
    rcopy(ms.at[lines], mr.at[lines], m2_ss, m2_rs, row_peer(1)).wait()


def hand_on(cent, logt, terms, cent_out, logt_out, mass_out):
    cent_out[...] = cent[...]
    logt_out[...] = logt[...]
    mass_out[...] = jnp.sum(terms[...], axis=0)[:, :PART]


def per_device(embeddings, assignments, parents, starting_coarse_label):
    vmem = pl.BlockSpec(memory_space=pltpu.VMEM)
    hbm = pl.BlockSpec(memory_space=pltpu.HBM)
    anywhere = pl.BlockSpec(memory_space=pl.ANY)
    dma = pltpu.SemaphoreType.DMA
    operands = (assignments.reshape(32, RUN), starting_coarse_label.reshape(1, RUN), embeddings, parents)
    cent, logt, terms = pl.pallas_call(
        kernel,
        out_shape=(
            jax.ShapeDtypeStruct((RUN, W), BF16),
            jax.ShapeDtypeStruct((1, RUN), F32),
            jax.ShapeDtypeStruct((2 * DP, 1, RUN), F32),
        ),
        in_specs=[hbm, hbm, hbm, hbm],
        out_specs=(anywhere, anywhere, anywhere),
        scratch_shapes=[
            pltpu.VMEM((32, RUN), jnp.int32),
            pltpu.VMEM((1, RUN), jnp.int32),
            pltpu.VMEM((NTILE, ROWS, TILE), BF16),
            pltpu.VMEM((SLOTS, ROWS), BF16),
            pltpu.VMEM((16, ROWS), BF16),
            pltpu.VMEM((32, RUN), jnp.int32),
            pltpu.VMEM((DP, CAP, W), BF16),
            pltpu.VMEM((DP, CAP, W), BF16),
            pltpu.VMEM((DP, 1, SLOTS), F32),
            pltpu.VMEM((DP, 1, SLOTS), F32),
            pltpu.VMEM((NPCH * PCH, W), BF16),
            pltpu.VMEM((4, RUN, W), BF16),
            pltpu.VMEM((4, 8, RUN), F32),
            pltpu.VMEM((NPCH, PCH, 4 * RUN), F32),
            pltpu.VMEM((NPCH, 4 * RUN), F32),
            pltpu.VMEM((NPCH, 4 * RUN), F32),
            pltpu.VMEM((4, 8, RUN), F32),
            pltpu.VMEM((NPCH, 4 * RUN), F32),
            pltpu.VMEM((NPCH, 1, PCH), F32),
            pltpu.VMEM((1, PCH), F32),
            pltpu.VMEM((2 * DP, 1, RUN), F32),
            pltpu.VMEM((1, RUN), F32),
            dma((NTILE,)),
            dma,
            dma((len(RANGES),)),
            dma((len(RANGES),)),
            dma,
            dma,
            dma((5,)),
            dma((5,)),
            dma((6,)),
            dma((6,)),
            dma((3,)),
            dma((3,)),
            dma((3,)),
            dma((3,)),
            dma,
            dma,
            dma,
            dma,
            dma((3,)),
            dma((2,)),
        ],
        compiler_params=pltpu.CompilerParams(collective_id=0, has_side_effects=True, vmem_limit_bytes=52 << 20),
        name="handover",
    )(
        *(pltpu.with_memory_space_constraint(v, pltpu.HBM) for v in operands),
    )
    cent, logt, mass = pl.pallas_call(
        hand_on,
        out_shape=(
            jax.ShapeDtypeStruct((RUN, W), BF16),
            jax.ShapeDtypeStruct((1, RUN), F32),
            jax.ShapeDtypeStruct((1, PART), F32),
        ),
        in_specs=[vmem, vmem, vmem],
        out_specs=(vmem, vmem, vmem),
        compiler_params=pltpu.CompilerParams(vmem_limit_bytes=2 << 20),
        name="finish",
    )(cent, logt, terms)
    return cent, logt.reshape(RUN), mass.reshape(PART)


def solution(mesh):
    return jax.shard_map(
        per_device,
        mesh=mesh,
        in_specs=(P("dp", None), P("dp"), P("cent", None), P(("cent", "dp"))),
        out_specs=(P(("cent", "dp"), None), P(("cent", "dp")), P(("cent", "dp"))),
        check_vma=False,
    )
```

```python
import jax
import jax.numpy as jnp
from jax import lax
from jax.experimental import pallas as pl
from jax.experimental.pallas import tpu as pltpu
from jax.sharding import PartitionSpec as P

MESH = pl.DeviceIdType.MESH
F32 = jnp.float32
BF16 = jnp.bfloat16

W = 1536
RUN = 128
CAP = 48
DP = 8
SLOTS = DP * CAP
TILE = 256
NTILE = W // TILE
ROWS = 4096
SLAB = 512
PART = 64
EARLY, LATE = 1536, 512
BLK = 128
PIECES = (0, 2, 1, 3)
INV_SOFT = 1.0 / 0.5
REWARD = 1.5

RANGES = ((0, 256), (256, 512), (768, 768))
SEND_AFTER = (0, 2, 5)


def kernel(
    a_hbm, label_hbm, e_hbm, p_hbm,
    cent_hbm, logt_hbm, mr,
    a_v, label_v, e_v, oht, place, slot_v, send, recv, id_send, id_recv, par, cb, meta, scores_e, scores_l, mch, sch, stat, fac, mp, sib_in, ms, logt_v,
    e_sem, p_sem, row_ss, row_rs, id_ss, id_rs, par_ss, par_rs, cb_ss, cb_rs, meta_ss, meta_rs, stat_ss, stat_rs,
    m1_ss, m1_rs, m2_ss, m2_rs, o_sem, in_sem,
):
    d = lax.axis_index("dp")
    c = lax.axis_index("cent")
    zlo = d % 2
    zhi = c // 8
    y = (c // 2) % 4
    k = c % 2

    def cent_of(zh, yy, kk):
        return zh * 8 + yy * 2 + kk

    yp, ym, y2 = (y + 1) % 4, (y + 3) % 4, (y + 2) % 4
    x = d // 2
    q = x % 2
    xp, xm = (x + 1) % 4, (x + 3) % 4
    other_z = cent_of(1 - zhi, y, k)
    ZN, XM, XP, ZXM, ZXP = 1, 2, 3, 4, 5
    group = {
        ZN: (x * 2 + 1 - zlo, other_z),
        XM: (xm * 2 + zlo, c),
        XP: (xp * 2 + zlo, c),
        ZXM: (xm * 2 + 1 - zlo, other_z),
        ZXP: (xp * 2 + 1 - zlo, other_z),
    }
    inverse = {ZN: ZN, XM: XP, XP: XM, ZXM: ZXP, ZXP: ZXM}
    sibling = (d, cent_of(zhi, y, 1 - k))
    up = (d, cent_of(zhi, yp, k))
    down = (d, cent_of(zhi, ym, k))
    y_of = (y, ym, yp, y2)

    def owner(t, ra, rb):
        a, b = (x // 2 + ra) % 2, (zlo + rb) % 2
        return 4 * t + 2 * a + b, ((2 * a + q) * 2 + b, cent_of(zhi, y_of[t], k))

    owners = [(t, ra, rb) for t in (3, 2, 1, 0) for ra in (1, 0) for rb in (1, 0) if (t, ra, rb) != (0, 0, 0)]

    def row_peer(r):
        return ((d + r) % DP, c)

    def rcopy(src, dst, ss, rs, dev):
        return pltpu.make_async_remote_copy(
            src_ref=src, dst_ref=dst, send_sem=ss, recv_sem=rs, device_id=dev, device_id_type=MESH
        )

    load_a = pltpu.make_async_copy(a_hbm, a_v, in_sem.at[0])
    load_label = pltpu.make_async_copy(label_hbm, label_v, in_sem.at[1])
    e_copies = [
        pltpu.make_async_copy(e_hbm.at[:, pl.ds(TILE * n, TILE)], e_v.at[n], e_sem.at[n]) for n in range(NTILE)
    ]
    def mine(a):
        return p_hbm.at[pl.ds(pl.multiple_of(2 * BLK * a + BLK * q, BLK), BLK)]

    def place_of(core, t, a=0, n=1):
        start = (EARLY + 256 * core if t == 3 else 768 * core + 256 * t) + BLK * a
        return par.at[pl.ds(start, BLK * n)]

    own_par = [pltpu.make_async_copy(mine(a), place_of(0, 0, a), p_sem.at[a]) for a in range(2)]
    load_a.start()
    e_copies[0].start()

    barrier = pltpu.get_barrier_semaphore()
    partners = [row_peer(r) for r in range(1, DP)] + [group[ZN], group[ZXM], group[ZXP], sibling]
    partners += [owner(*o)[1] for o in owners if o[0] != 0]
    for dev in partners:
        pl.semaphore_signal(barrier, inc=1, device_id=dev, device_id_type=MESH)

    e_copies[1].start()
    load_label.start()
    load_a.wait()

    a = a_v[...]
    rel = lax.shift_right_logical(a, 7) - c * DP
    run_id = lax.broadcasted_iota(jnp.int32, (32, 8, RUN), 1)
    member = (rel[:, None, :] == run_id).astype(F32).reshape(256, RUN)
    member_b = member.astype(BF16)
    upper = (
        lax.broadcasted_iota(jnp.int32, (RUN, RUN), 0) < lax.broadcasted_iota(jnp.int32, (RUN, RUN), 1)
    ).astype(F32).astype(BF16)
    ri = lax.broadcasted_iota(jnp.int32, (256, 256), 0)
    ci = lax.broadcasted_iota(jnp.int32, (256, 256), 1)
    before = (((ri & 7) == (ci & 7)) & (ci < ri)).astype(F32).astype(BF16)
    within = jnp.dot(member_b, upper, preferred_element_type=F32)
    earlier = jnp.dot(before, member_b, preferred_element_type=F32).astype(BF16)
    ahead = jnp.dot(earlier, jnp.ones((RUN, RUN), BF16), preferred_element_type=F32)
    base = ((lax.broadcasted_iota(jnp.int32, (256, RUN), 0) & 7) * CAP + 1).astype(F32)
    slot = jnp.sum((member * (within + ahead + base)).reshape(32, 8, RUN), axis=1) - 1.0
    slot_v[...] = slot.astype(jnp.int32)
    spot = ((a & (RUN - 1)) + 1).astype(F32)
    for b in range(ROWS // RUN):
        place[:, RUN * b : RUN * (b + 1)] = jnp.broadcast_to(spot[b : b + 1, :], (16, RUN)).astype(BF16)

    def par_copy(src, dst, idx, dev):
        return rcopy(src, dst, par_ss.at[idx], par_rs.at[idx], dev)

    to_up = [par_copy(mine(a), place_of(0, 1, a), a, up) for a in range(2)]
    to_down = [par_copy(mine(a), place_of(0, 2, a), 2 + a, down) for a in range(2)]
    on_up = par_copy(place_of(0, 1, 0), place_of(0, 3, 0), 4, up)
    on_down = par_copy(place_of(0, 2, 1), place_of(0, 3, 1), 5, down)
    to_sib = [par_copy(mine(a), place_of(1, 0, a), 6 + a, sibling) for a in range(2)]
    sib_early = [par_copy(place_of(0, t, 0, 2), place_of(1, t, 0, 2), 7 + t, sibling) for t in (1, 2)]
    sib_late = [par_copy(place_of(0, 3, a), place_of(1, 3, a), 10 + a, sibling) for a in range(2)]

    def build(b, carry):
        cols = pl.ds(pl.multiple_of(b * RUN, RUN), RUN)
        line = slot_v[pl.ds(b, 1), :]
        oht[:, cols] = (lax.broadcasted_iota(jnp.int32, (SLOTS, RUN), 0) == line).astype(F32).astype(BF16)
        return carry

    lax.fori_loop(0, ROWS // RUN, build, 0)

    for cp in e_copies[2:]:
        cp.start()

    def row_copy(r, g, dev, owner):
        start, size = RANGES[g]
        return rcopy(
            send.at[dev[0], :, pl.ds(start, size)],
            recv.at[owner, :, pl.ds(start, size)],
            row_ss.at[g],
            row_rs.at[g],
            dev,
        )

    def row_total(g):
        start, size = RANGES[g]
        cols = pl.ds(start, size)
        part = pl.ds(0, DP - 1)
        return rcopy(send.at[part, :, cols], recv.at[part, :, cols], row_ss.at[g], row_rs.at[g], row_peer(1))

    id_total = rcopy(id_send.at[pl.ds(0, DP - 1)], id_recv.at[pl.ds(0, DP - 1)], id_ss, id_rs, row_peer(1))

    for n in range(NTILE):
        e_copies[n].wait()
        part = jnp.dot(oht[...], e_v[n], preferred_element_type=F32)
        send[:, :, TILE * n : TILE * (n + 1)] = part.astype(BF16).reshape(DP, CAP, TILE)
        if n == 0:
            pl.semaphore_wait(barrier, len(partners))
        if n in SEND_AFTER:
            for r in range(1, DP):
                row_copy(r, SEND_AFTER.index(n), row_peer(r), d).start()
        if n == 0:
            for cp in (to_up[0], to_down[1], to_up[1], to_down[0]):
                cp.start()
        if n == 2:
            for cp in (*own_par, *to_sib):
                cp.start()
            spots = lax.dot_general(place[...], oht[...], (((1,), (1,)), ((), ())), preferred_element_type=F32)[:8]
            lane = lax.broadcasted_iota(jnp.int32, (DP, SLOTS), 1)
            mine = jnp.where(lane // CAP == lax.broadcasted_iota(jnp.int32, (DP, SLOTS), 0), spots, 0.0).astype(BF16)
            lo = lax.broadcasted_iota(jnp.int32, (SLOTS, SLOTS), 0)
            hi = lax.broadcasted_iota(jnp.int32, (SLOTS, SLOTS), 1)
            shift = ((lo % CAP == hi % CAP) & (hi // CAP == d)).astype(F32).astype(BF16)
            moved = jnp.dot(mine, shift, preferred_element_type=F32)
            for i in range(DP):
                id_send[i] = moved[i : i + 1, :]
            for r in range(1, DP):
                dev = row_peer(r)
                rcopy(id_send.at[dev[0]], id_recv.at[d], id_ss, id_rs, dev).start()
    recv[d] = send[d]
    id_recv[d] = id_send[d]
    ms[...] = jnp.zeros_like(ms)

    id_total.wait_recv()
    ids = jnp.sum(id_recv[...], axis=0).astype(jnp.int32) - 1
    onehot = (lax.broadcasted_iota(jnp.int32, (RUN, SLOTS), 0) == ids).astype(F32)
    counts_col = jnp.sum(onehot, axis=1, keepdims=True)
    onehot = onehot.astype(BF16)
    counts_row = lax.dot_general(jnp.ones((16, SLOTS), BF16), onehot, (((1,), (1,)), ((), ())), preferred_element_type=F32)[:1]
    for g in range(len(RANGES)):
        row_total(g).wait_recv()
    sums = jnp.dot(onehot, recv[...].reshape(SLOTS, W), preferred_element_type=F32)
    mean = sums / jnp.maximum(counts_col, 1.0)
    scale = jnp.sqrt(jnp.sum(mean * mean, axis=1, keepdims=True) + 1e-06)
    normed = (mean / scale).astype(BF16)
    cb[0] = normed
    cent_out = pltpu.make_async_copy(cb.at[0], cent_hbm, o_sem.at[0])
    cent_out.start()
    load_label.wait()
    meta[0, 0:1, :] = counts_row.astype(BF16).astype(F32)
    meta[0, 1:2, :] = label_v[...].astype(F32)
    meta[0, 2:8, :] = jnp.zeros((6, RUN), F32)

    def cent_copy(src, dst, start, size, idx, dev):
        rows = pl.ds(start, size)
        return rcopy(cb.at[src, rows], cb.at[dst, rows], cb_ss.at[idx], cb_rs.at[idx], dev)

    over_z = [cent_copy(0, 2, 32 * i, 32, i, group[ZN]) for i in range(4)]
    over_x = [cent_copy(0, 1, 64 * h, 64, 4 + h, group[(XP, XM)[h]]) for h in range(2)]
    pass_on = [cent_copy(2, 3, 32 * i, 32, 6 + i, group[(XP, XM)[i // 2]]) for i in range(4)]
    over_z[PIECES[0]].start()
    for cp in over_x:
        cp.start()
    for i in PIECES[1:]:
        over_z[i].start()
    metas = {p: rcopy(meta.at[0], meta.at[inverse[p]], meta_ss.at[p], meta_rs.at[inverse[p]], group[p]) for p in group}
    for p in (ZXM, ZXP, ZN, XM, XP):
        metas[p].start()

    def arrived(p):
        return rcopy(meta.at[0], meta.at[p], meta_ss.at[p], meta_rs.at[p], group[p])

    to_up[0].wait_recv()
    on_up.start()
    to_down[1].wait_recv()
    on_down.start()
    for g in range(len(RANGES)):
        row_total(g).wait_send()
    id_total.wait_send()
    to_up[1].wait_recv()
    sib_early[0].start()
    to_down[0].wait_recv()
    sib_early[1].start()
    for i in PIECES[:2]:
        over_z[i].wait_recv()
        pass_on[i].start()
    for cp in own_par:
        cp.wait()
    for cp in (*to_sib, *over_x, *sib_early):
        cp.wait_recv()
    for p in group:
        arrived(p).wait_recv()

    low_lanes = lax.broadcasted_iota(jnp.int32, (1, RUN), 1) < RUN // 2

    def halves(low, high):
        return jnp.where(low_lanes, low, high)

    def meta_line(i):
        return [
            meta[0, i : i + 1, :],
            halves(meta[XM, i : i + 1, :], meta[XP, i : i + 1, :]),
            meta[ZN, i : i + 1, :],
            halves(meta[ZXM, i : i + 1, :], meta[ZXP, i : i + 1, :]),
        ]

    weights, labels = meta_line(0), meta_line(1)

    def first_ids(early):
        found = []
        for core in (k, 1 - k):
            for t in (0, 1, 2) if early else (3,):
                for a in range(2):
                    found.append(cent_of(zhi, y_of[t], core) * SLAB + 2 * BLK * a + BLK * q)
        return found

    def score(pair, early):
        cols = slice(2 * RUN * pair, 2 * RUN * (pair + 1))
        block = cb[2 * pair : 2 * pair + 2].reshape(2 * RUN, W)
        label = jnp.concatenate([labels[2 * pair], labels[2 * pair + 1]], axis=1).astype(jnp.int32)
        some = par[:EARLY, :] if early else par[EARLY:, :]
        s = lax.dot_general(some, block, (((1,), (1,)), ((), ())), preferred_element_type=F32)
        line = lax.broadcasted_iota(jnp.int32, (BLK, 2 * RUN), 0)
        s = jnp.concatenate(
            [
                s[BLK * i : BLK * (i + 1)] * INV_SOFT + jnp.where(line == label - first, REWARD, 0.0)
                for i, first in enumerate(first_ids(early))
            ],
            axis=0,
        )
        top = jnp.max(s, axis=0, keepdims=True)
        e = jnp.exp(s - top)
        (scores_e if early else scores_l)[:, cols] = e
        row = 0 if early else 1
        mch[row : row + 1, cols] = top
        sch[row : row + 1, cols] = jnp.sum(e, axis=0, keepdims=True)

    score(0, True)
    for i in PIECES[2:]:
        over_z[i].wait_recv()
        pass_on[i].start()
    on_up.wait_recv()
    sib_late[0].start()
    on_down.wait_recv()
    sib_late[1].start()
    for cp in (*to_up, *to_down, *to_sib, *sib_early, *metas.values(), *over_x):
        cp.wait_send()
    cent_out.wait()
    for cp in sib_late:
        cp.wait_recv()
    score(0, False)
    for cp in pass_on:
        cp.wait_recv()
    score(1, True)
    score(1, False)

    m_loc = jnp.max(mch[...], axis=0, keepdims=True)
    s_loc = jnp.sum(sch[...] * jnp.exp(mch[...] - m_loc), axis=0, keepdims=True)
    for j in range(4):
        stat[0, j : j + 1, :] = m_loc[:, RUN * j : RUN * (j + 1)]
        stat[0, 4 + j : 5 + j, :] = s_loc[:, RUN * j : RUN * (j + 1)]
    stats = {p: rcopy(stat.at[0], stat.at[inverse[p]], stat_ss.at[p], stat_rs.at[inverse[p]], group[p]) for p in group}
    for p in (ZXM, ZXP, ZN, XM, XP):
        stats[p].start()
    for cp in (*over_z, *pass_on, on_up, on_down, *sib_late):
        cp.wait_send()
    for p in group:
        rcopy(stat.at[0], stat.at[p], stat_ss.at[p], stat_rs.at[p], group[p]).wait_recv()
    elsewhere = (
        (((XP, 1), (XM, 1)), ((ZN, 2), (ZN, 2)), ((ZXP, 3), (ZXM, 3))),
        (((XM, 0), (XP, 0)), ((ZXM, 2), (ZXP, 2)), ((ZN, 3), (ZN, 3))),
        (((ZN, 0), (ZN, 0)), ((XP, 3), (XM, 3)), ((ZXP, 1), (ZXM, 1))),
        (((ZXM, 0), (ZXP, 0)), ((XM, 2), (XP, 2)), ((ZN, 1), (ZN, 1))),
    )
    for j in range(4):

        def line(at, i):
            return stat[at[0], i + at[1] : i + at[1] + 1, :]

        m = [stat[0, j : j + 1, :]] + [halves(line(lo, 0), line(hi, 0)) for lo, hi in elsewhere[j]]
        s = [stat[0, 4 + j : 5 + j, :]] + [halves(line(lo, 4), line(hi, 4)) for lo, hi in elsewhere[j]]
        top = jnp.maximum(jnp.maximum(m[0], m[1]), jnp.maximum(m[2], m[3]))
        total = sum(s[i] * jnp.exp(m[i] - top) for i in range(4))
        log_total = top + jnp.log(total)
        if j == 0:
            logt_v[...] = log_total
            logt_out = pltpu.make_async_copy(logt_v, logt_hbm, o_sem.at[1])
            logt_out.start()
        cols = slice(RUN * j, RUN * (j + 1))
        fac[:, cols] = weights[j] * jnp.exp(mch[:, cols] - log_total)

    for row, (scores, count) in enumerate(((scores_e, EARLY), (scores_l, LATE))):
        acc = jnp.zeros((count, RUN), F32)
        for j in range(4):
            cols = slice(RUN * j, RUN * (j + 1))
            acc = acc + scores[:, cols] * fac[row : row + 1, cols]
        total = jnp.sum(acc.T, axis=0, keepdims=True)
        at = slice(0, 768) if row == 0 else slice(768, 1024)
        mp[0, :, at] = total[:, : count // 2]
        mp[1, :, at] = total[:, count // 2 :]

    to_sib_mass = rcopy(mp.at[1], sib_in, m1_ss, m1_rs, sibling)
    to_sib_mass.start()
    to_sib_mass.wait_recv()
    both = mp[0] + sib_in[...]
    for i in range(2 * DP):
        ms[i, :, :PART] = both[:, PART * i : PART * (i + 1)]

    for i, o in enumerate(owners):
        at, dev = owner(*o)
        rcopy(ms.at[at], mr.at[i], m2_ss, m2_rs, dev).start()
    own_mass = pltpu.make_async_copy(ms.at[owner(0, 0, 0)[0]], mr.at[2 * DP - 1], o_sem.at[2])
    own_mass.start()
    for cp in [to_sib_mass, *stats.values()]:
        cp.wait_send()
    logt_out.wait()
    own_mass.wait()
    lines = pl.ds(0, 2 * DP - 1)
    rcopy(ms.at[lines], mr.at[lines], m2_ss, m2_rs, row_peer(1)).wait()


def hand_on(cent, logt, terms, cent_out, logt_out, mass_out):
    cent_out[...] = cent[...]
    logt_out[...] = logt[...]
    mass_out[...] = jnp.sum(terms[...], axis=0)[:, :PART]


def per_device(embeddings, assignments, parents, starting_coarse_label):
    vmem = pl.BlockSpec(memory_space=pltpu.VMEM)
    hbm = pl.BlockSpec(memory_space=pltpu.HBM)
    anywhere = pl.BlockSpec(memory_space=pl.ANY)
    dma = pltpu.SemaphoreType.DMA
    operands = (assignments.reshape(32, RUN), starting_coarse_label.reshape(1, RUN), embeddings, parents)
    cent, logt, terms = pl.pallas_call(
        kernel,
        out_shape=(
            jax.ShapeDtypeStruct((RUN, W), BF16),
            jax.ShapeDtypeStruct((1, RUN), F32),
            jax.ShapeDtypeStruct((2 * DP, 1, RUN), F32),
        ),
        in_specs=[hbm, hbm, hbm, hbm],
        out_specs=(anywhere, anywhere, anywhere),
        scratch_shapes=[
            pltpu.VMEM((32, RUN), jnp.int32),
            pltpu.VMEM((1, RUN), jnp.int32),
            pltpu.VMEM((NTILE, ROWS, TILE), BF16),
            pltpu.VMEM((SLOTS, ROWS), BF16),
            pltpu.VMEM((16, ROWS), BF16),
            pltpu.VMEM((32, RUN), jnp.int32),
            pltpu.VMEM((DP, CAP, W), BF16),
            pltpu.VMEM((DP, CAP, W), BF16),
            pltpu.VMEM((DP, 1, SLOTS), F32),
            pltpu.VMEM((DP, 1, SLOTS), F32),
            pltpu.VMEM((EARLY + LATE, W), BF16),
            pltpu.VMEM((4, RUN, W), BF16),
            pltpu.VMEM((6, 8, RUN), F32),
            pltpu.VMEM((EARLY, 4 * RUN), F32),
            pltpu.VMEM((LATE, 4 * RUN), F32),
            pltpu.VMEM((2, 4 * RUN), F32),
            pltpu.VMEM((2, 4 * RUN), F32),
            pltpu.VMEM((6, 8, RUN), F32),
            pltpu.VMEM((2, 4 * RUN), F32),
            pltpu.VMEM((2, 1, 1024), F32),
            pltpu.VMEM((1, 1024), F32),
            pltpu.VMEM((2 * DP, 1, RUN), F32),
            pltpu.VMEM((1, RUN), F32),
            dma((NTILE,)),
            dma((2,)),
            dma((len(RANGES),)),
            dma((len(RANGES),)),
            dma,
            dma,
            dma((12,)),
            dma((12,)),
            dma((10,)),
            dma((10,)),
            dma((6,)),
            dma((6,)),
            dma((6,)),
            dma((6,)),
            dma,
            dma,
            dma,
            dma,
            dma((3,)),
            dma((2,)),
        ],
        compiler_params=pltpu.CompilerParams(collective_id=0, has_side_effects=True, vmem_limit_bytes=52 << 20),
        name="handover",
    )(
        *(pltpu.with_memory_space_constraint(v, pltpu.HBM) for v in operands),
    )
    cent, logt, mass = pl.pallas_call(
        hand_on,
        out_shape=(
            jax.ShapeDtypeStruct((RUN, W), BF16),
            jax.ShapeDtypeStruct((1, RUN), F32),
            jax.ShapeDtypeStruct((1, PART), F32),
        ),
        in_specs=[vmem, vmem, vmem],
        out_specs=(vmem, vmem, vmem),
        compiler_params=pltpu.CompilerParams(vmem_limit_bytes=2 << 20),
        name="finish",
    )(cent, logt, terms)
    return cent, logt.reshape(RUN), mass.reshape(PART)


def solution(mesh):
    return jax.shard_map(
        per_device,
        mesh=mesh,
        in_specs=(P("dp", None), P("dp"), P("cent", None), P(("cent", "dp"))),
        out_specs=(P(("cent", "dp"), None), P(("cent", "dp")), P(("cent", "dp"))),
        check_vma=False,
    )
```

```python
import jax
import jax.numpy as jnp
from jax import lax
from jax.experimental import pallas as pl
from jax.experimental.pallas import tpu as pltpu
from jax.sharding import PartitionSpec as P

MESH = pl.DeviceIdType.MESH
F32 = jnp.float32
BF16 = jnp.bfloat16

W = 1536
RUN = 128
CAP = 48
DP = 8
SLOTS = DP * CAP
TILE = 256
NTILE = W // TILE
ROWS = 4096
SLAB = 512
PART = 64
EARLY, LATE = 1536, 512
BLK = 128
MCH = 512
PIECES = (0, 2, 1, 3)
INV_SOFT = 1.0 / 0.5
REWARD = 1.5

RANGES = ((0, 256), (256, 512), (768, 768))
SEND_AFTER = (0, 2, 5)


def kernel(
    a_hbm, label_hbm, e_hbm, p_hbm,
    cent_hbm, logt_hbm, mr,
    a_v, label_v, e_v, oht, place, slot_v, send, recv, id_send, id_recv, par, cb, meta, scores, mch, sch, stat, fac, terms, mp, sib_in, ms, logt_v,
    e_sem, p_sem, row_ss, row_rs, id_ss, id_rs, par_ss, par_rs, cb_ss, cb_rs, meta_ss, meta_rs, stat_ss, stat_rs,
    m1_ss, m1_rs, m2_ss, m2_rs, o_sem, in_sem,
):
    d = lax.axis_index("dp")
    c = lax.axis_index("cent")
    zlo = d % 2
    zhi = c // 8
    y = (c // 2) % 4
    k = c % 2

    def cent_of(zh, yy, kk):
        return zh * 8 + yy * 2 + kk

    yp, ym, y2 = (y + 1) % 4, (y + 3) % 4, (y + 2) % 4
    x = d // 2
    q = x % 2
    xp, xm = (x + 1) % 4, (x + 3) % 4
    other_z = cent_of(1 - zhi, y, k)
    ZN, XM, XP, ZXM, ZXP = 1, 2, 3, 4, 5
    group = {
        ZN: (x * 2 + 1 - zlo, other_z),
        XM: (xm * 2 + zlo, c),
        XP: (xp * 2 + zlo, c),
        ZXM: (xm * 2 + 1 - zlo, other_z),
        ZXP: (xp * 2 + 1 - zlo, other_z),
    }
    inverse = {ZN: ZN, XM: XP, XP: XM, ZXM: ZXP, ZXP: ZXM}
    sibling = (d, cent_of(zhi, y, 1 - k))
    up = (d, cent_of(zhi, yp, k))
    down = (d, cent_of(zhi, ym, k))
    y_of = (y, ym, yp, y2)

    def owner(t, ra, rb):
        a, b = (x // 2 + ra) % 2, (zlo + rb) % 2
        return 4 * t + 2 * a + b, ((2 * a + q) * 2 + b, cent_of(zhi, y_of[t], k))

    owners = [(t, ra, rb) for t in (3, 2, 1, 0) for ra in (1, 0) for rb in (1, 0) if (t, ra, rb) != (0, 0, 0)]

    def row_peer(r):
        return ((d + r) % DP, c)

    def rcopy(src, dst, ss, rs, dev):
        return pltpu.make_async_remote_copy(
            src_ref=src, dst_ref=dst, send_sem=ss, recv_sem=rs, device_id=dev, device_id_type=MESH
        )

    load_a = pltpu.make_async_copy(a_hbm, a_v, in_sem.at[0])
    load_label = pltpu.make_async_copy(label_hbm, label_v, in_sem.at[1])
    e_copies = [
        pltpu.make_async_copy(e_hbm.at[:, pl.ds(TILE * n, TILE)], e_v.at[n], e_sem.at[n]) for n in range(NTILE)
    ]
    def mine(a):
        return p_hbm.at[pl.ds(pl.multiple_of(2 * BLK * a + BLK * q, BLK), BLK)]

    def place_of(core, t, a=0, n=1):
        start = (EARLY + 256 * core if t == 3 else 768 * core + 256 * t) + BLK * a
        return par.at[pl.ds(start, BLK * n)]

    own_par = [pltpu.make_async_copy(mine(a), place_of(0, 0, a), p_sem.at[a]) for a in range(2)]
    load_a.start()
    e_copies[0].start()

    barrier = pltpu.get_barrier_semaphore()
    partners = [row_peer(r) for r in range(1, DP)] + [group[ZN], group[ZXM], group[ZXP], sibling]
    partners += [owner(*o)[1] for o in owners if o[0] != 0]
    for dev in partners:
        pl.semaphore_signal(barrier, inc=1, device_id=dev, device_id_type=MESH)

    e_copies[1].start()
    load_label.start()
    load_a.wait()

    a = a_v[...]
    rel = lax.shift_right_logical(a, 7) - c * DP
    run_id = lax.broadcasted_iota(jnp.int32, (32, 8, RUN), 1)
    member = (rel[:, None, :] == run_id).astype(F32).reshape(256, RUN)
    member_b = member.astype(BF16)
    upper = (
        lax.broadcasted_iota(jnp.int32, (RUN, RUN), 0) < lax.broadcasted_iota(jnp.int32, (RUN, RUN), 1)
    ).astype(F32).astype(BF16)
    ri = lax.broadcasted_iota(jnp.int32, (256, 256), 0)
    ci = lax.broadcasted_iota(jnp.int32, (256, 256), 1)
    before = (((ri & 7) == (ci & 7)) & (ci < ri)).astype(F32).astype(BF16)
    within = jnp.dot(member_b, upper, preferred_element_type=F32)
    earlier = jnp.dot(before, member_b, preferred_element_type=F32).astype(BF16)
    ahead = jnp.dot(earlier, jnp.ones((RUN, RUN), BF16), preferred_element_type=F32)
    base = ((lax.broadcasted_iota(jnp.int32, (256, RUN), 0) & 7) * CAP + 1).astype(F32)
    slot = jnp.sum((member * (within + ahead + base)).reshape(32, 8, RUN), axis=1) - 1.0
    slot_v[...] = slot.astype(jnp.int32)
    spot = ((a & (RUN - 1)) + 1).astype(F32)
    for b in range(ROWS // RUN):
        place[:, RUN * b : RUN * (b + 1)] = jnp.broadcast_to(spot[b : b + 1, :], (16, RUN)).astype(BF16)

    def par_copy(src, dst, idx, dev):
        return rcopy(src, dst, par_ss.at[idx], par_rs.at[idx], dev)

    to_up = [par_copy(mine(a), place_of(0, 1, a), a, up) for a in range(2)]
    to_down = [par_copy(mine(a), place_of(0, 2, a), 2 + a, down) for a in range(2)]
    on_up = par_copy(place_of(0, 1, 0), place_of(0, 3, 0), 4, up)
    on_down = par_copy(place_of(0, 2, 1), place_of(0, 3, 1), 5, down)
    to_sib = [par_copy(mine(a), place_of(1, 0, a), 6 + a, sibling) for a in range(2)]
    sib_early = [par_copy(place_of(0, t, 0, 2), place_of(1, t, 0, 2), 7 + t, sibling) for t in (1, 2)]
    sib_late = [par_copy(place_of(0, 3, a), place_of(1, 3, a), 10 + a, sibling) for a in range(2)]

    def build(b, carry):
        cols = pl.ds(pl.multiple_of(b * RUN, RUN), RUN)
        line = slot_v[pl.ds(b, 1), :]
        oht[:, cols] = (lax.broadcasted_iota(jnp.int32, (SLOTS, RUN), 0) == line).astype(F32).astype(BF16)
        return carry

    lax.fori_loop(0, ROWS // RUN, build, 0)

    for cp in e_copies[2:]:
        cp.start()

    def row_copy(r, g, dev, owner):
        start, size = RANGES[g]
        return rcopy(
            send.at[dev[0], :, pl.ds(start, size)],
            recv.at[owner, :, pl.ds(start, size)],
            row_ss.at[g],
            row_rs.at[g],
            dev,
        )

    def row_total(g):
        start, size = RANGES[g]
        cols = pl.ds(start, size)
        part = pl.ds(0, DP - 1)
        return rcopy(send.at[part, :, cols], recv.at[part, :, cols], row_ss.at[g], row_rs.at[g], row_peer(1))

    id_total = rcopy(id_send.at[pl.ds(0, DP - 1)], id_recv.at[pl.ds(0, DP - 1)], id_ss, id_rs, row_peer(1))

    for n in range(NTILE):
        e_copies[n].wait()
        part = jnp.dot(oht[...], e_v[n], preferred_element_type=F32)
        send[:, :, TILE * n : TILE * (n + 1)] = part.astype(BF16).reshape(DP, CAP, TILE)
        if n == 0:
            pl.semaphore_wait(barrier, len(partners))
        if n in SEND_AFTER:
            for r in range(1, DP):
                row_copy(r, SEND_AFTER.index(n), row_peer(r), d).start()
        if n == 0:
            for cp in (to_up[0], to_down[1], to_up[1], to_down[0]):
                cp.start()
        if n == 2:
            for cp in (*own_par, *to_sib):
                cp.start()
            spots = lax.dot_general(place[...], oht[...], (((1,), (1,)), ((), ())), preferred_element_type=F32)[:8]
            lane = lax.broadcasted_iota(jnp.int32, (DP, SLOTS), 1)
            mine = jnp.where(lane // CAP == lax.broadcasted_iota(jnp.int32, (DP, SLOTS), 0), spots, 0.0).astype(BF16)
            lo = lax.broadcasted_iota(jnp.int32, (SLOTS, SLOTS), 0)
            hi = lax.broadcasted_iota(jnp.int32, (SLOTS, SLOTS), 1)
            shift = ((lo % CAP == hi % CAP) & (hi // CAP == d)).astype(F32).astype(BF16)
            moved = jnp.dot(mine, shift, preferred_element_type=F32)
            for i in range(DP):
                id_send[i] = moved[i : i + 1, :]
            for r in range(1, DP):
                dev = row_peer(r)
                rcopy(id_send.at[dev[0]], id_recv.at[d], id_ss, id_rs, dev).start()
    recv[d] = send[d]
    id_recv[d] = id_send[d]
    ms[...] = jnp.zeros_like(ms)

    id_total.wait_recv()
    ids = jnp.sum(id_recv[...], axis=0).astype(jnp.int32) - 1
    onehot = (lax.broadcasted_iota(jnp.int32, (RUN, SLOTS), 0) == ids).astype(F32)
    counts_col = jnp.sum(onehot, axis=1, keepdims=True)
    onehot = onehot.astype(BF16)
    counts_row = lax.dot_general(jnp.ones((16, SLOTS), BF16), onehot, (((1,), (1,)), ((), ())), preferred_element_type=F32)[:1]
    for g in range(len(RANGES)):
        row_total(g).wait_recv()
    sums = jnp.dot(onehot, recv[...].reshape(SLOTS, W), preferred_element_type=F32)
    mean = sums / jnp.maximum(counts_col, 1.0)
    scale = jnp.sqrt(jnp.sum(mean * mean, axis=1, keepdims=True) + 1e-06)
    normed = (mean / scale).astype(BF16)
    cb[0] = normed
    cent_out = pltpu.make_async_copy(cb.at[0], cent_hbm, o_sem.at[0])
    cent_out.start()
    load_label.wait()
    meta[0, 0:1, :] = counts_row.astype(BF16).astype(F32)
    meta[0, 1:2, :] = label_v[...].astype(F32)
    meta[0, 2:8, :] = jnp.zeros((6, RUN), F32)

    def cent_copy(src, dst, start, size, idx, dev):
        rows = pl.ds(start, size)
        return rcopy(cb.at[src, rows], cb.at[dst, rows], cb_ss.at[idx], cb_rs.at[idx], dev)

    over_z = [cent_copy(0, 2, 32 * i, 32, i, group[ZN]) for i in range(4)]
    over_x = [cent_copy(0, 1, 64 * h, 64, 4 + h, group[(XP, XM)[h]]) for h in range(2)]
    pass_on = [cent_copy(2, 3, 32 * i, 32, 6 + i, group[(XP, XM)[i // 2]]) for i in range(4)]
    over_z[PIECES[0]].start()
    for cp in over_x:
        cp.start()
    for i in PIECES[1:]:
        over_z[i].start()
    metas = {p: rcopy(meta.at[0], meta.at[inverse[p]], meta_ss.at[p], meta_rs.at[inverse[p]], group[p]) for p in group}
    for p in (ZXM, ZXP, ZN, XM, XP):
        metas[p].start()

    def arrived(p):
        return rcopy(meta.at[0], meta.at[p], meta_ss.at[p], meta_rs.at[p], group[p])

    to_up[0].wait_recv()
    on_up.start()
    to_down[1].wait_recv()
    on_down.start()
    for g in range(len(RANGES)):
        row_total(g).wait_send()
    id_total.wait_send()
    to_up[1].wait_recv()
    sib_early[0].start()
    to_down[0].wait_recv()
    sib_early[1].start()
    for i in PIECES:
        over_z[i].wait_recv()
        pass_on[i].start()
    on_up.wait_recv()
    sib_late[0].start()
    on_down.wait_recv()
    sib_late[1].start()
    for cp in own_par:
        cp.wait()
    for cp in (*to_sib, *over_x, *sib_early):
        cp.wait_recv()
    for p in group:
        arrived(p).wait_recv()

    low_lanes = lax.broadcasted_iota(jnp.int32, (1, RUN), 1) < RUN // 2

    def halves(low, high):
        return jnp.where(low_lanes, low, high)

    def meta_line(i):
        return [
            meta[0, i : i + 1, :],
            halves(meta[XM, i : i + 1, :], meta[XP, i : i + 1, :]),
            meta[ZN, i : i + 1, :],
            halves(meta[ZXM, i : i + 1, :], meta[ZXP, i : i + 1, :]),
        ]

    weights, labels = meta_line(0), meta_line(1)

    firsts = [
        cent_of(zhi, y_of[t], core) * SLAB + 2 * BLK * a + BLK * q
        for times in ((0, 1, 2), (3,))
        for core in (k, 1 - k)
        for t in times
        for a in range(2)
    ]

    def score(pair, size, first_step, steps):
        cols = slice(2 * RUN * pair, 2 * RUN * (pair + 1))
        label = jnp.concatenate([labels[2 * pair], labels[2 * pair + 1]], axis=1).astype(jnp.int32)
        per = size // BLK

        def step(i, carry):
            rows = pl.ds(pl.multiple_of(i * size, size), size)
            block = cb[2 * pair : 2 * pair + 2].reshape(2 * RUN, W)
            s = lax.dot_general(par[rows, :], block, (((1,), (1,)), ((), ())), preferred_element_type=F32)
            line = lax.broadcasted_iota(jnp.int32, (BLK, 2 * RUN), 0)
            parts = []
            for b in range(per):
                first = firsts[per * first_step + b]
                for other in range(first_step + 1, first_step + steps):
                    first = jnp.where(i == other, firsts[per * other + b], first)
                bonus = jnp.where(line == label - first, REWARD, 0.0)
                parts.append(s[BLK * b : BLK * (b + 1)] * INV_SOFT + bonus)
            s = jnp.concatenate(parts, axis=0)
            top = jnp.max(s, axis=0, keepdims=True)
            e = jnp.exp(s - top)
            scores[rows, cols] = e
            total = jnp.sum(e, axis=0, keepdims=True)
            for h in range(size // MCH):
                at = pl.ds(i * (size // MCH) + h, 1)
                mch[at, cols] = top
                sch[at, cols] = total if h == 0 else jnp.zeros_like(total)
            return carry

        lax.fori_loop(first_step, first_step + steps, step, 0)

    score(0, MCH, 0, 3)
    for cp in (*to_up, *to_down, *to_sib, *sib_early, *metas.values(), *over_x):
        cp.wait_send()
    cent_out.wait()
    for cp in sib_late:
        cp.wait_recv()
    score(0, MCH, 3, 1)
    for cp in pass_on:
        cp.wait_recv()
    score(1, 2 * MCH, 0, 2)

    m_loc = jnp.max(mch[...], axis=0, keepdims=True)
    s_loc = jnp.sum(sch[...] * jnp.exp(mch[...] - m_loc), axis=0, keepdims=True)
    for j in range(4):
        stat[0, j : j + 1, :] = m_loc[:, RUN * j : RUN * (j + 1)]
        stat[0, 4 + j : 5 + j, :] = s_loc[:, RUN * j : RUN * (j + 1)]
    stats = {p: rcopy(stat.at[0], stat.at[inverse[p]], stat_ss.at[p], stat_rs.at[inverse[p]], group[p]) for p in group}
    for p in (ZXM, ZXP, ZN, XM, XP):
        stats[p].start()
    for cp in (*over_z, *pass_on, on_up, on_down, *sib_late):
        cp.wait_send()
    for p in group:
        rcopy(stat.at[0], stat.at[p], stat_ss.at[p], stat_rs.at[p], group[p]).wait_recv()
    elsewhere = (
        (((XP, 1), (XM, 1)), ((ZN, 2), (ZN, 2)), ((ZXP, 3), (ZXM, 3))),
        (((XM, 0), (XP, 0)), ((ZXM, 2), (ZXP, 2)), ((ZN, 3), (ZN, 3))),
        (((ZN, 0), (ZN, 0)), ((XP, 3), (XM, 3)), ((ZXP, 1), (ZXM, 1))),
        (((ZXM, 0), (ZXP, 0)), ((XM, 2), (XP, 2)), ((ZN, 1), (ZN, 1))),
    )
    for j in range(4):

        def line(at, i):
            return stat[at[0], i + at[1] : i + at[1] + 1, :]

        m = [stat[0, j : j + 1, :]] + [halves(line(lo, 0), line(hi, 0)) for lo, hi in elsewhere[j]]
        s = [stat[0, 4 + j : 5 + j, :]] + [halves(line(lo, 4), line(hi, 4)) for lo, hi in elsewhere[j]]
        top = jnp.maximum(jnp.maximum(m[0], m[1]), jnp.maximum(m[2], m[3]))
        total = sum(s[i] * jnp.exp(m[i] - top) for i in range(4))
        log_total = top + jnp.log(total)
        if j == 0:
            logt_v[...] = log_total
            logt_out = pltpu.make_async_copy(logt_v, logt_hbm, o_sem.at[1])
            logt_out.start()
        cols = slice(RUN * j, RUN * (j + 1))
        fac[:, cols] = weights[j] * jnp.exp(mch[:, cols] - log_total)

    def mass_step(i, carry):
        f = fac[pl.ds(i, 1), :]
        rows = pl.ds(pl.multiple_of(i * MCH, MCH), MCH)
        acc = jnp.zeros((MCH, RUN), F32)
        for j in range(4):
            cols = slice(RUN * j, RUN * (j + 1))
            acc = acc + scores[rows, cols] * f[:, cols]
        terms[i] = jnp.sum(acc.T, axis=0, keepdims=True)
        return carry

    lax.fori_loop(0, 4, mass_step, 0)
    mp[0, :, 0:512] = terms[0]
    mp[0, :, 512:768] = terms[1][:, :256]
    mp[0, :, 768:1024] = terms[3][:, :256]
    mp[1, :, 0:256] = terms[1][:, 256:]
    mp[1, :, 256:768] = terms[2]
    mp[1, :, 768:1024] = terms[3][:, 256:]

    to_sib_mass = rcopy(mp.at[1], sib_in, m1_ss, m1_rs, sibling)
    to_sib_mass.start()
    to_sib_mass.wait_recv()
    both = mp[0] + sib_in[...]
    for i in range(2 * DP):
        ms[i, :, :PART] = both[:, PART * i : PART * (i + 1)]

    for i, o in enumerate(owners):
        at, dev = owner(*o)
        rcopy(ms.at[at], mr.at[i], m2_ss, m2_rs, dev).start()
    own_mass = pltpu.make_async_copy(ms.at[owner(0, 0, 0)[0]], mr.at[2 * DP - 1], o_sem.at[2])
    own_mass.start()
    for cp in [to_sib_mass, *stats.values()]:
        cp.wait_send()
    logt_out.wait()
    own_mass.wait()
    lines = pl.ds(0, 2 * DP - 1)
    rcopy(ms.at[lines], mr.at[lines], m2_ss, m2_rs, row_peer(1)).wait()


def hand_on(cent, logt, terms, cent_out, logt_out, mass_out):
    cent_out[...] = cent[...]
    logt_out[...] = logt[...]
    mass_out[...] = jnp.sum(terms[...], axis=0)[:, :PART]


def per_device(embeddings, assignments, parents, starting_coarse_label):
    vmem = pl.BlockSpec(memory_space=pltpu.VMEM)
    hbm = pl.BlockSpec(memory_space=pltpu.HBM)
    anywhere = pl.BlockSpec(memory_space=pl.ANY)
    dma = pltpu.SemaphoreType.DMA
    operands = (assignments.reshape(32, RUN), starting_coarse_label.reshape(1, RUN), embeddings, parents)
    cent, logt, terms = pl.pallas_call(
        kernel,
        out_shape=(
            jax.ShapeDtypeStruct((RUN, W), BF16),
            jax.ShapeDtypeStruct((1, RUN), F32),
            jax.ShapeDtypeStruct((2 * DP, 1, RUN), F32),
        ),
        in_specs=[hbm, hbm, hbm, hbm],
        out_specs=(anywhere, anywhere, anywhere),
        scratch_shapes=[
            pltpu.VMEM((32, RUN), jnp.int32),
            pltpu.VMEM((1, RUN), jnp.int32),
            pltpu.VMEM((NTILE, ROWS, TILE), BF16),
            pltpu.VMEM((SLOTS, ROWS), BF16),
            pltpu.VMEM((16, ROWS), BF16),
            pltpu.VMEM((32, RUN), jnp.int32),
            pltpu.VMEM((DP, CAP, W), BF16),
            pltpu.VMEM((DP, CAP, W), BF16),
            pltpu.VMEM((DP, 1, SLOTS), F32),
            pltpu.VMEM((DP, 1, SLOTS), F32),
            pltpu.VMEM((EARLY + LATE, W), BF16),
            pltpu.VMEM((4, RUN, W), BF16),
            pltpu.VMEM((6, 8, RUN), F32),
            pltpu.VMEM((EARLY + LATE, 4 * RUN), F32),
            pltpu.VMEM((4, 4 * RUN), F32),
            pltpu.VMEM((4, 4 * RUN), F32),
            pltpu.VMEM((6, 8, RUN), F32),
            pltpu.VMEM((4, 4 * RUN), F32),
            pltpu.VMEM((4, 1, MCH), F32),
            pltpu.VMEM((2, 1, 1024), F32),
            pltpu.VMEM((1, 1024), F32),
            pltpu.VMEM((2 * DP, 1, RUN), F32),
            pltpu.VMEM((1, RUN), F32),
            dma((NTILE,)),
            dma((2,)),
            dma((len(RANGES),)),
            dma((len(RANGES),)),
            dma,
            dma,
            dma((12,)),
            dma((12,)),
            dma((10,)),
            dma((10,)),
            dma((6,)),
            dma((6,)),
            dma((6,)),
            dma((6,)),
            dma,
            dma,
            dma,
            dma,
            dma((3,)),
            dma((2,)),
        ],
        compiler_params=pltpu.CompilerParams(collective_id=0, has_side_effects=True, vmem_limit_bytes=52 << 20),
        name="handover",
    )(
        *(pltpu.with_memory_space_constraint(v, pltpu.HBM) for v in operands),
    )
    cent, logt, mass = pl.pallas_call(
        hand_on,
        out_shape=(
            jax.ShapeDtypeStruct((RUN, W), BF16),
            jax.ShapeDtypeStruct((1, RUN), F32),
            jax.ShapeDtypeStruct((1, PART), F32),
        ),
        in_specs=[vmem, vmem, vmem],
        out_specs=(vmem, vmem, vmem),
        compiler_params=pltpu.CompilerParams(vmem_limit_bytes=2 << 20),
        name="finish",
    )(cent, logt, terms)
    return cent, logt.reshape(RUN), mass.reshape(PART)


def solution(mesh):
    return jax.shard_map(
        per_device,
        mesh=mesh,
        in_specs=(P("dp", None), P("dp"), P("cent", None), P(("cent", "dp"))),
        out_specs=(P(("cent", "dp"), None), P(("cent", "dp")), P(("cent", "dp"))),
        check_vma=False,
    )
```

```python
import jax
import jax.numpy as jnp
from jax import lax
from jax.experimental import pallas as pl
from jax.experimental.pallas import tpu as pltpu
from jax.sharding import PartitionSpec as P

MESH = pl.DeviceIdType.MESH
F32 = jnp.float32
BF16 = jnp.bfloat16

W = 1536
RUN = 128
CAP = 48
DP = 8
SLOTS = DP * CAP
TILE = 256
NTILE = W // TILE
ROWS = 4096
SLAB = 512
PART = 64
EARLY, LATE = 1536, 512
BLK = 128
MCH = 512
PIECES = (0, 2, 1, 3)
INV_SOFT = 1.0 / 0.5
REWARD = 1.5

RANGES = ((0, 256), (256, 512), (768, 768))
SEND_AFTER = (0, 2, 5)
FAR_FIRST = (5, 3, 4, 6, 2, 7, 1)


def kernel(
    a_hbm, label_hbm, e_hbm, p_hbm,
    cent_hbm, logt_hbm, mr,
    a_v, label_v, e_v, oht, place, slot_v, send, recv, id_send, id_recv, par, cb, meta, scores, mch, sch, stat, fac, terms, mp, sib_in, ms, logt_v,
    e_sem, p_sem, row_ss, row_rs, id_ss, id_rs, par_ss, par_rs, cb_ss, cb_rs, meta_ss, meta_rs, stat_ss, stat_rs,
    m1_ss, m1_rs, m2_ss, m2_rs, o_sem, in_sem,
):
    d = lax.axis_index("dp")
    c = lax.axis_index("cent")
    zlo = d % 2
    zhi = c // 8
    y = (c // 2) % 4
    k = c % 2

    def cent_of(zh, yy, kk):
        return zh * 8 + yy * 2 + kk

    yp, ym, y2 = (y + 1) % 4, (y + 3) % 4, (y + 2) % 4
    x = d // 2
    q = x % 2
    xp, xm = (x + 1) % 4, (x + 3) % 4
    other_z = cent_of(1 - zhi, y, k)
    ZN, XM, XP, ZXM, ZXP = 1, 2, 3, 4, 5
    group = {
        ZN: (x * 2 + 1 - zlo, other_z),
        XM: (xm * 2 + zlo, c),
        XP: (xp * 2 + zlo, c),
        ZXM: (xm * 2 + 1 - zlo, other_z),
        ZXP: (xp * 2 + 1 - zlo, other_z),
    }
    inverse = {ZN: ZN, XM: XP, XP: XM, ZXM: ZXP, ZXP: ZXM}
    sibling = (d, cent_of(zhi, y, 1 - k))
    up = (d, cent_of(zhi, yp, k))
    down = (d, cent_of(zhi, ym, k))
    y_of = (y, ym, yp, y2)

    def owner(t, ra, rb):
        a, b = (x // 2 + ra) % 2, (zlo + rb) % 2
        return 4 * t + 2 * a + b, ((2 * a + q) * 2 + b, cent_of(zhi, y_of[t], k))

    owners = [(t, ra, rb) for t in (3, 2, 1, 0) for ra in (1, 0) for rb in (1, 0) if (t, ra, rb) != (0, 0, 0)]

    def row_peer(r):
        return ((d + r) % DP, c)

    def rcopy(src, dst, ss, rs, dev):
        return pltpu.make_async_remote_copy(
            src_ref=src, dst_ref=dst, send_sem=ss, recv_sem=rs, device_id=dev, device_id_type=MESH
        )

    load_a = pltpu.make_async_copy(a_hbm, a_v, in_sem.at[0])
    load_label = pltpu.make_async_copy(label_hbm, label_v, in_sem.at[1])
    e_copies = [
        pltpu.make_async_copy(e_hbm.at[:, pl.ds(TILE * n, TILE)], e_v.at[n], e_sem.at[n]) for n in range(NTILE)
    ]
    def mine(a):
        return p_hbm.at[pl.ds(pl.multiple_of(2 * BLK * a + BLK * q, BLK), BLK)]

    def place_of(core, t, a=0, n=1):
        start = (EARLY + 256 * core if t == 3 else 768 * core + 256 * t) + BLK * a
        return par.at[pl.ds(start, BLK * n)]

    own_par = [pltpu.make_async_copy(mine(a), place_of(0, 0, a), p_sem.at[a]) for a in range(2)]
    load_a.start()
    e_copies[0].start()

    barrier = pltpu.get_barrier_semaphore()
    partners = [row_peer(r) for r in range(1, DP)] + [group[ZN], group[ZXM], group[ZXP], sibling]
    partners += [owner(*o)[1] for o in owners if o[0] != 0]
    for dev in partners:
        pl.semaphore_signal(barrier, inc=1, device_id=dev, device_id_type=MESH)

    e_copies[1].start()
    load_label.start()
    load_a.wait()

    a = a_v[...]
    rel = lax.shift_right_logical(a, 7) - c * DP
    run_id = lax.broadcasted_iota(jnp.int32, (32, 8, RUN), 1)
    member = (rel[:, None, :] == run_id).astype(F32).reshape(256, RUN)
    member_b = member.astype(BF16)
    upper = (
        lax.broadcasted_iota(jnp.int32, (RUN, RUN), 0) < lax.broadcasted_iota(jnp.int32, (RUN, RUN), 1)
    ).astype(F32).astype(BF16)
    ri = lax.broadcasted_iota(jnp.int32, (256, 256), 0)
    ci = lax.broadcasted_iota(jnp.int32, (256, 256), 1)
    before = (((ri & 7) == (ci & 7)) & (ci < ri)).astype(F32).astype(BF16)
    within = jnp.dot(member_b, upper, preferred_element_type=F32)
    earlier = jnp.dot(before, member_b, preferred_element_type=F32).astype(BF16)
    ahead = jnp.dot(earlier, jnp.ones((RUN, RUN), BF16), preferred_element_type=F32)
    base = ((lax.broadcasted_iota(jnp.int32, (256, RUN), 0) & 7) * CAP + 1).astype(F32)
    slot = jnp.sum((member * (within + ahead + base)).reshape(32, 8, RUN), axis=1) - 1.0
    slot_v[...] = slot.astype(jnp.int32)
    spot = ((a & (RUN - 1)) + 1).astype(F32)
    for b in range(ROWS // RUN):
        place[:, RUN * b : RUN * (b + 1)] = jnp.broadcast_to(spot[b : b + 1, :], (16, RUN)).astype(BF16)

    def par_copy(src, dst, idx, dev):
        return rcopy(src, dst, par_ss.at[idx], par_rs.at[idx], dev)

    to_up = [par_copy(mine(a), place_of(0, 1, a), a, up) for a in range(2)]
    to_down = [par_copy(mine(a), place_of(0, 2, a), 2 + a, down) for a in range(2)]
    on_up = par_copy(place_of(0, 1, 0), place_of(0, 3, 0), 4, up)
    on_down = par_copy(place_of(0, 2, 1), place_of(0, 3, 1), 5, down)
    to_sib = [par_copy(mine(a), place_of(1, 0, a), 6 + a, sibling) for a in range(2)]
    sib_early = [par_copy(place_of(0, t, 0, 2), place_of(1, t, 0, 2), 7 + t, sibling) for t in (1, 2)]
    sib_late = [par_copy(place_of(0, 3, a), place_of(1, 3, a), 10 + a, sibling) for a in range(2)]

    def build(b, carry):
        cols = pl.ds(pl.multiple_of(b * RUN, RUN), RUN)
        line = slot_v[pl.ds(b, 1), :]
        oht[:, cols] = (lax.broadcasted_iota(jnp.int32, (SLOTS, RUN), 0) == line).astype(F32).astype(BF16)
        return carry

    lax.fori_loop(0, ROWS // RUN, build, 0)

    for cp in e_copies[2:]:
        cp.start()
    pl.semaphore_wait(barrier, len(partners))
    for cp in (to_up[0], to_down[1], to_up[1], to_down[0]):
        cp.start()

    def row_copy(r, g, dev, owner):
        start, size = RANGES[g]
        return rcopy(
            send.at[dev[0], :, pl.ds(start, size)],
            recv.at[owner, :, pl.ds(start, size)],
            row_ss.at[g],
            row_rs.at[g],
            dev,
        )

    def row_total(g):
        start, size = RANGES[g]
        cols = pl.ds(start, size)
        part = pl.ds(0, DP - 1)
        return rcopy(send.at[part, :, cols], recv.at[part, :, cols], row_ss.at[g], row_rs.at[g], row_peer(1))

    id_total = rcopy(id_send.at[pl.ds(0, DP - 1)], id_recv.at[pl.ds(0, DP - 1)], id_ss, id_rs, row_peer(1))

    for n in range(NTILE):
        e_copies[n].wait()
        part = jnp.dot(oht[...], e_v[n], preferred_element_type=F32)
        send[:, :, TILE * n : TILE * (n + 1)] = part.astype(BF16).reshape(DP, CAP, TILE)
        if n in SEND_AFTER:
            for r in FAR_FIRST:
                row_copy(r, SEND_AFTER.index(n), row_peer(r), d).start()
        if n == 2:
            for cp in (*own_par, *to_sib):
                cp.start()
            spots = lax.dot_general(place[...], oht[...], (((1,), (1,)), ((), ())), preferred_element_type=F32)[:8]
            lane = lax.broadcasted_iota(jnp.int32, (DP, SLOTS), 1)
            mine = jnp.where(lane // CAP == lax.broadcasted_iota(jnp.int32, (DP, SLOTS), 0), spots, 0.0).astype(BF16)
            lo = lax.broadcasted_iota(jnp.int32, (SLOTS, SLOTS), 0)
            hi = lax.broadcasted_iota(jnp.int32, (SLOTS, SLOTS), 1)
            shift = ((lo % CAP == hi % CAP) & (hi // CAP == d)).astype(F32).astype(BF16)
            moved = jnp.dot(mine, shift, preferred_element_type=F32)
            for i in range(DP):
                id_send[i] = moved[i : i + 1, :]
            for r in range(1, DP):
                dev = row_peer(r)
                rcopy(id_send.at[dev[0]], id_recv.at[d], id_ss, id_rs, dev).start()
    recv[d] = send[d]
    id_recv[d] = id_send[d]
    ms[...] = jnp.zeros_like(ms)
    to_up[0].wait_recv()
    on_up.start()
    to_down[1].wait_recv()
    on_down.start()

    id_total.wait_recv()
    ids = jnp.sum(id_recv[...], axis=0).astype(jnp.int32) - 1
    onehot = (lax.broadcasted_iota(jnp.int32, (RUN, SLOTS), 0) == ids).astype(F32)
    counts_col = jnp.sum(onehot, axis=1, keepdims=True)
    onehot = onehot.astype(BF16)
    counts_row = lax.dot_general(jnp.ones((16, SLOTS), BF16), onehot, (((1,), (1,)), ((), ())), preferred_element_type=F32)[:1]
    for g in range(len(RANGES)):
        row_total(g).wait_recv()
    sums = jnp.dot(onehot, recv[...].reshape(SLOTS, W), preferred_element_type=F32)
    mean = sums / jnp.maximum(counts_col, 1.0)
    scale = jnp.sqrt(jnp.sum(mean * mean, axis=1, keepdims=True) + 1e-06)
    normed = (mean / scale).astype(BF16)
    cb[0] = normed
    cent_out = pltpu.make_async_copy(cb.at[0], cent_hbm, o_sem.at[0])
    cent_out.start()
    load_label.wait()
    meta[0, 0:1, :] = counts_row.astype(BF16).astype(F32)
    meta[0, 1:2, :] = label_v[...].astype(F32)
    meta[0, 2:8, :] = jnp.zeros((6, RUN), F32)

    def cent_copy(src, dst, start, size, idx, dev):
        rows = pl.ds(start, size)
        return rcopy(cb.at[src, rows], cb.at[dst, rows], cb_ss.at[idx], cb_rs.at[idx], dev)

    over_z = [cent_copy(0, 2, 32 * i, 32, i, group[ZN]) for i in range(4)]
    over_x = [cent_copy(0, 1, 64 * h, 64, 4 + h, group[(XP, XM)[h]]) for h in range(2)]
    pass_on = [cent_copy(2, 3, 32 * i, 32, 6 + i, group[(XP, XM)[i // 2]]) for i in range(4)]
    over_z[PIECES[0]].start()
    for cp in over_x:
        cp.start()
    for i in PIECES[1:]:
        over_z[i].start()
    metas = {p: rcopy(meta.at[0], meta.at[inverse[p]], meta_ss.at[p], meta_rs.at[inverse[p]], group[p]) for p in group}
    for p in (ZXM, ZXP, ZN, XM, XP):
        metas[p].start()

    def arrived(p):
        return rcopy(meta.at[0], meta.at[p], meta_ss.at[p], meta_rs.at[p], group[p])

    for g in range(len(RANGES)):
        row_total(g).wait_send()
    id_total.wait_send()
    to_up[1].wait_recv()
    sib_early[0].start()
    to_down[0].wait_recv()
    sib_early[1].start()
    for i in PIECES:
        over_z[i].wait_recv()
        pass_on[i].start()
    on_up.wait_recv()
    sib_late[0].start()
    on_down.wait_recv()
    sib_late[1].start()
    for cp in own_par:
        cp.wait()
    for cp in (*to_sib, *over_x, *sib_early):
        cp.wait_recv()
    for p in group:
        arrived(p).wait_recv()

    low_lanes = lax.broadcasted_iota(jnp.int32, (1, RUN), 1) < RUN // 2

    def halves(low, high):
        return jnp.where(low_lanes, low, high)

    def meta_line(i):
        return [
            meta[0, i : i + 1, :],
            halves(meta[XM, i : i + 1, :], meta[XP, i : i + 1, :]),
            meta[ZN, i : i + 1, :],
            halves(meta[ZXM, i : i + 1, :], meta[ZXP, i : i + 1, :]),
        ]

    weights, labels = meta_line(0), meta_line(1)

    firsts = [
        cent_of(zhi, y_of[t], core) * SLAB + 2 * BLK * a + BLK * q
        for times in ((0, 1, 2), (3,))
        for core in (k, 1 - k)
        for t in times
        for a in range(2)
    ]

    def score(pair, size, first_step, steps):
        cols = slice(2 * RUN * pair, 2 * RUN * (pair + 1))
        label = jnp.concatenate([labels[2 * pair], labels[2 * pair + 1]], axis=1).astype(jnp.int32)
        per = size // BLK

        def step(i, carry):
            rows = pl.ds(pl.multiple_of(i * size, size), size)
            block = cb[2 * pair : 2 * pair + 2].reshape(2 * RUN, W)
            s = lax.dot_general(par[rows, :], block, (((1,), (1,)), ((), ())), preferred_element_type=F32)
            line = lax.broadcasted_iota(jnp.int32, (BLK, 2 * RUN), 0)
            parts = []
            for b in range(per):
                first = firsts[per * first_step + b]
                for other in range(first_step + 1, first_step + steps):
                    first = jnp.where(i == other, firsts[per * other + b], first)
                bonus = jnp.where(line == label - first, REWARD, 0.0)
                parts.append(s[BLK * b : BLK * (b + 1)] * INV_SOFT + bonus)
            s = jnp.concatenate(parts, axis=0)
            top = jnp.max(s, axis=0, keepdims=True)
            e = jnp.exp(s - top)
            scores[rows, cols] = e
            total = jnp.sum(e, axis=0, keepdims=True)
            for h in range(size // MCH):
                at = pl.ds(i * (size // MCH) + h, 1)
                mch[at, cols] = top
                sch[at, cols] = total if h == 0 else jnp.zeros_like(total)
            return carry

        lax.fori_loop(first_step, first_step + steps, step, 0)

    score(0, MCH, 0, 3)
    for cp in (*to_up, *to_down, *to_sib, *sib_early, *metas.values(), *over_x):
        cp.wait_send()
    cent_out.wait()
    for cp in sib_late:
        cp.wait_recv()
    score(0, MCH, 3, 1)
    for cp in pass_on:
        cp.wait_recv()
    score(1, 2 * MCH, 0, 2)

    m_loc = jnp.max(mch[...], axis=0, keepdims=True)
    s_loc = jnp.sum(sch[...] * jnp.exp(mch[...] - m_loc), axis=0, keepdims=True)
    for j in range(4):
        stat[0, j : j + 1, :] = m_loc[:, RUN * j : RUN * (j + 1)]
        stat[0, 4 + j : 5 + j, :] = s_loc[:, RUN * j : RUN * (j + 1)]
    stats = {p: rcopy(stat.at[0], stat.at[inverse[p]], stat_ss.at[p], stat_rs.at[inverse[p]], group[p]) for p in group}
    for p in (ZXM, ZXP, ZN, XM, XP):
        stats[p].start()
    for cp in (*over_z, *pass_on, on_up, on_down, *sib_late):
        cp.wait_send()
    for p in group:
        rcopy(stat.at[0], stat.at[p], stat_ss.at[p], stat_rs.at[p], group[p]).wait_recv()
    elsewhere = (
        (((XP, 1), (XM, 1)), ((ZN, 2), (ZN, 2)), ((ZXP, 3), (ZXM, 3))),
        (((XM, 0), (XP, 0)), ((ZXM, 2), (ZXP, 2)), ((ZN, 3), (ZN, 3))),
        (((ZN, 0), (ZN, 0)), ((XP, 3), (XM, 3)), ((ZXP, 1), (ZXM, 1))),
        (((ZXM, 0), (ZXP, 0)), ((XM, 2), (XP, 2)), ((ZN, 1), (ZN, 1))),
    )
    for j in range(4):

        def line(at, i):
            return stat[at[0], i + at[1] : i + at[1] + 1, :]

        m = [stat[0, j : j + 1, :]] + [halves(line(lo, 0), line(hi, 0)) for lo, hi in elsewhere[j]]
        s = [stat[0, 4 + j : 5 + j, :]] + [halves(line(lo, 4), line(hi, 4)) for lo, hi in elsewhere[j]]
        top = jnp.maximum(jnp.maximum(m[0], m[1]), jnp.maximum(m[2], m[3]))
        total = sum(s[i] * jnp.exp(m[i] - top) for i in range(4))
        log_total = top + jnp.log(total)
        if j == 0:
            logt_v[...] = log_total
            logt_out = pltpu.make_async_copy(logt_v, logt_hbm, o_sem.at[1])
            logt_out.start()
        cols = slice(RUN * j, RUN * (j + 1))
        fac[:, cols] = weights[j] * jnp.exp(mch[:, cols] - log_total)

    def mass_step(i, carry):
        f = fac[pl.ds(i, 1), :]
        rows = pl.ds(pl.multiple_of(i * MCH, MCH), MCH)
        acc = jnp.zeros((MCH, RUN), F32)
        for j in range(4):
            cols = slice(RUN * j, RUN * (j + 1))
            acc = acc + scores[rows, cols] * f[:, cols]
        terms[i] = jnp.sum(acc.T, axis=0, keepdims=True)
        return carry

    lax.fori_loop(0, 4, mass_step, 0)
    mp[0, :, 0:512] = terms[0]
    mp[0, :, 512:768] = terms[1][:, :256]
    mp[0, :, 768:1024] = terms[3][:, :256]
    mp[1, :, 0:256] = terms[1][:, 256:]
    mp[1, :, 256:768] = terms[2]
    mp[1, :, 768:1024] = terms[3][:, 256:]

    to_sib_mass = rcopy(mp.at[1], sib_in, m1_ss, m1_rs, sibling)
    to_sib_mass.start()
    to_sib_mass.wait_recv()
    both = mp[0] + sib_in[...]
    for i in range(2 * DP):
        ms[i, :, :PART] = both[:, PART * i : PART * (i + 1)]

    for i, o in enumerate(owners):
        at, dev = owner(*o)
        rcopy(ms.at[at], mr.at[i], m2_ss, m2_rs, dev).start()
    own_mass = pltpu.make_async_copy(ms.at[owner(0, 0, 0)[0]], mr.at[2 * DP - 1], o_sem.at[2])
    own_mass.start()
    for cp in [to_sib_mass, *stats.values()]:
        cp.wait_send()
    logt_out.wait()
    own_mass.wait()
    lines = pl.ds(0, 2 * DP - 1)
    rcopy(ms.at[lines], mr.at[lines], m2_ss, m2_rs, row_peer(1)).wait()


def hand_on(cent, logt, terms, cent_out, logt_out, mass_out):
    cent_out[...] = cent[...]
    logt_out[...] = logt[...]
    mass_out[...] = jnp.sum(terms[...], axis=0)[:, :PART]


def per_device(embeddings, assignments, parents, starting_coarse_label):
    vmem = pl.BlockSpec(memory_space=pltpu.VMEM)
    hbm = pl.BlockSpec(memory_space=pltpu.HBM)
    anywhere = pl.BlockSpec(memory_space=pl.ANY)
    dma = pltpu.SemaphoreType.DMA
    operands = (assignments.reshape(32, RUN), starting_coarse_label.reshape(1, RUN), embeddings, parents)
    cent, logt, terms = pl.pallas_call(
        kernel,
        out_shape=(
            jax.ShapeDtypeStruct((RUN, W), BF16),
            jax.ShapeDtypeStruct((1, RUN), F32),
            jax.ShapeDtypeStruct((2 * DP, 1, RUN), F32),
        ),
        in_specs=[hbm, hbm, hbm, hbm],
        out_specs=(anywhere, anywhere, anywhere),
        scratch_shapes=[
            pltpu.VMEM((32, RUN), jnp.int32),
            pltpu.VMEM((1, RUN), jnp.int32),
            pltpu.VMEM((NTILE, ROWS, TILE), BF16),
            pltpu.VMEM((SLOTS, ROWS), BF16),
            pltpu.VMEM((16, ROWS), BF16),
            pltpu.VMEM((32, RUN), jnp.int32),
            pltpu.VMEM((DP, CAP, W), BF16),
            pltpu.VMEM((DP, CAP, W), BF16),
            pltpu.VMEM((DP, 1, SLOTS), F32),
            pltpu.VMEM((DP, 1, SLOTS), F32),
            pltpu.VMEM((EARLY + LATE, W), BF16),
            pltpu.VMEM((4, RUN, W), BF16),
            pltpu.VMEM((6, 8, RUN), F32),
            pltpu.VMEM((EARLY + LATE, 4 * RUN), F32),
            pltpu.VMEM((4, 4 * RUN), F32),
            pltpu.VMEM((4, 4 * RUN), F32),
            pltpu.VMEM((6, 8, RUN), F32),
            pltpu.VMEM((4, 4 * RUN), F32),
            pltpu.VMEM((4, 1, MCH), F32),
            pltpu.VMEM((2, 1, 1024), F32),
            pltpu.VMEM((1, 1024), F32),
            pltpu.VMEM((2 * DP, 1, RUN), F32),
            pltpu.VMEM((1, RUN), F32),
            dma((NTILE,)),
            dma((2,)),
            dma((len(RANGES),)),
            dma((len(RANGES),)),
            dma,
            dma,
            dma((12,)),
            dma((12,)),
            dma((10,)),
            dma((10,)),
            dma((6,)),
            dma((6,)),
            dma((6,)),
            dma((6,)),
            dma,
            dma,
            dma,
            dma,
            dma((3,)),
            dma((2,)),
        ],
        compiler_params=pltpu.CompilerParams(collective_id=0, has_side_effects=True, vmem_limit_bytes=52 << 20),
        name="handover",
    )(
        *(pltpu.with_memory_space_constraint(v, pltpu.HBM) for v in operands),
    )
    cent, logt, mass = pl.pallas_call(
        hand_on,
        out_shape=(
            jax.ShapeDtypeStruct((RUN, W), BF16),
            jax.ShapeDtypeStruct((1, RUN), F32),
            jax.ShapeDtypeStruct((1, PART), F32),
        ),
        in_specs=[vmem, vmem, vmem],
        out_specs=(vmem, vmem, vmem),
        compiler_params=pltpu.CompilerParams(vmem_limit_bytes=2 << 20),
        name="finish",
    )(cent, logt, terms)
    return cent, logt.reshape(RUN), mass.reshape(PART)


def solution(mesh):
    return jax.shard_map(
        per_device,
        mesh=mesh,
        in_specs=(P("dp", None), P("dp"), P("cent", None), P(("cent", "dp"))),
        out_specs=(P(("cent", "dp"), None), P(("cent", "dp")), P(("cent", "dp"))),
        check_vma=False,
    )
```

```python
import jax
import jax.numpy as jnp
from jax import lax
from jax.experimental import pallas as pl
from jax.experimental.pallas import tpu as pltpu
from jax.sharding import PartitionSpec as P

MESH = pl.DeviceIdType.MESH
F32 = jnp.float32
BF16 = jnp.bfloat16

W = 1536
RUN = 128
CAP = 48
DP = 8
SLOTS = DP * CAP
TILE = 256
COLS = W // 2
NTILE = COLS // TILE
ROWS = 4096
SLAB = 512
PART = 64
EARLY, LATE = 1536, 512
BLK = 128
MCH = 512
PIECES = (0, 2, 1, 3)
INV_SOFT = 1.0 / 0.5
REWARD = 1.5

RANGES = ((0, 256), (256, 512))
SEND_AFTER = (0, 2)
FAR_FIRST = (5, 3, 4, 6, 2, 7, 1)


def kernel(
    a_hbm, label_hbm, e_hbm, p_hbm,
    cent_hbm, logt_hbm, mr,
    a_v, label_v, e_v, oht, place, slot_v, send, recv, id_send, id_recv, par, cb, meta, scores, mch, sch, stat, fac, terms, mp, sib_in, ms, logt_v,
    e_sem, p_sem, row_ss, row_rs, sib_ss, sib_rs, id_ss, id_rs, par_ss, par_rs, cb_ss, cb_rs, meta_ss, meta_rs, stat_ss, stat_rs,
    m1_ss, m1_rs, m2_ss, m2_rs, o_sem, in_sem,
):
    d = lax.axis_index("dp")
    c = lax.axis_index("cent")
    zlo = d % 2
    zhi = c // 8
    y = (c // 2) % 4
    k = c % 2

    def cent_of(zh, yy, kk):
        return zh * 8 + yy * 2 + kk

    yp, ym, y2 = (y + 1) % 4, (y + 3) % 4, (y + 2) % 4
    x = d // 2
    q = x % 2
    xp, xm = (x + 1) % 4, (x + 3) % 4
    other_z = cent_of(1 - zhi, y, k)
    ZN, XM, XP, ZXM, ZXP = 1, 2, 3, 4, 5
    group = {
        ZN: (x * 2 + 1 - zlo, other_z),
        XM: (xm * 2 + zlo, c),
        XP: (xp * 2 + zlo, c),
        ZXM: (xm * 2 + 1 - zlo, other_z),
        ZXP: (xp * 2 + 1 - zlo, other_z),
    }
    inverse = {ZN: ZN, XM: XP, XP: XM, ZXM: ZXP, ZXP: ZXM}
    sibling = (d, cent_of(zhi, y, 1 - k))
    up = (d, cent_of(zhi, yp, k))
    down = (d, cent_of(zhi, ym, k))
    y_of = (y, ym, yp, y2)

    def owner(t, ra, rb):
        a, b = (x // 2 + ra) % 2, (zlo + rb) % 2
        return 4 * t + 2 * a + b, ((2 * a + q) * 2 + b, cent_of(zhi, y_of[t], k))

    owners = [(t, ra, rb) for t in (3, 2, 1, 0) for ra in (1, 0) for rb in (1, 0) if (t, ra, rb) != (0, 0, 0)]

    def row_peer(r):
        return ((d + r) % DP, c)

    def rcopy(src, dst, ss, rs, dev):
        return pltpu.make_async_remote_copy(
            src_ref=src, dst_ref=dst, send_sem=ss, recv_sem=rs, device_id=dev, device_id_type=MESH
        )

    load_a = pltpu.make_async_copy(a_hbm, a_v, in_sem.at[0])
    load_label = pltpu.make_async_copy(label_hbm, label_v, in_sem.at[1])
    e_copies = [
        pltpu.make_async_copy(
            e_hbm.at[:, pl.ds(pl.multiple_of(COLS * k + TILE * n, TILE), TILE)], e_v.at[n], e_sem.at[n]
        )
        for n in range(NTILE)
    ]
    def mine(a):
        return p_hbm.at[pl.ds(pl.multiple_of(2 * BLK * a + BLK * q, BLK), BLK)]

    def place_of(core, t, a=0, n=1):
        start = (EARLY + 256 * core if t == 3 else 768 * core + 256 * t) + BLK * a
        return par.at[pl.ds(start, BLK * n)]

    own_par = [pltpu.make_async_copy(mine(a), place_of(0, 0, a), p_sem.at[a]) for a in range(2)]
    load_a.start()
    e_copies[0].start()

    barrier = pltpu.get_barrier_semaphore()
    partners = [row_peer(r) for r in range(1, DP)] + [group[ZN], group[ZXM], group[ZXP], sibling]
    partners += [((d + r) % DP, cent_of(zhi, y, 1 - k)) for r in range(1, DP)]
    partners += [owner(*o)[1] for o in owners if o[0] != 0]
    for dev in partners:
        pl.semaphore_signal(barrier, inc=1, device_id=dev, device_id_type=MESH)

    e_copies[1].start()
    load_label.start()
    load_a.wait()

    a = a_v[...]
    run_id = lax.broadcasted_iota(jnp.int32, (32, 8, RUN), 1)
    upper = (
        lax.broadcasted_iota(jnp.int32, (RUN, RUN), 0) < lax.broadcasted_iota(jnp.int32, (RUN, RUN), 1)
    ).astype(F32).astype(BF16)
    ri = lax.broadcasted_iota(jnp.int32, (256, 256), 0)
    ci = lax.broadcasted_iota(jnp.int32, (256, 256), 1)
    before = (((ri & 7) == (ci & 7)) & (ci < ri)).astype(F32).astype(BF16)
    base = ((lax.broadcasted_iota(jnp.int32, (256, RUN), 0) & 7) * CAP + 1).astype(F32)
    for stage in range(2):
        rel = lax.shift_right_logical(a, 7) - cent_of(zhi, y, stage) * DP
        member = (rel[:, None, :] == run_id).astype(F32).reshape(256, RUN)
        member_b = member.astype(BF16)
        within = jnp.dot(member_b, upper, preferred_element_type=F32)
        earlier = jnp.dot(before, member_b, preferred_element_type=F32).astype(BF16)
        ahead = jnp.dot(earlier, jnp.ones((RUN, RUN), BF16), preferred_element_type=F32)
        slot = jnp.sum((member * (within + ahead + base)).reshape(32, 8, RUN), axis=1) - 1.0
        slot_v[stage] = slot.astype(jnp.int32)
    spot = ((a & (RUN - 1)) + 1).astype(F32)
    for b in range(ROWS // RUN):
        place[:, RUN * b : RUN * (b + 1)] = jnp.broadcast_to(spot[b : b + 1, :], (16, RUN)).astype(BF16)

    def par_copy(src, dst, idx, dev):
        return rcopy(src, dst, par_ss.at[idx], par_rs.at[idx], dev)

    to_up = [par_copy(mine(a), place_of(0, 1, a), a, up) for a in range(2)]
    to_down = [par_copy(mine(a), place_of(0, 2, a), 2 + a, down) for a in range(2)]
    on_up = par_copy(place_of(0, 1, 0), place_of(0, 3, 0), 4, up)
    on_down = par_copy(place_of(0, 2, 1), place_of(0, 3, 1), 5, down)
    to_sib = [par_copy(mine(a), place_of(1, 0, a), 6 + a, sibling) for a in range(2)]
    sib_early = [par_copy(place_of(0, t, 0, 2), place_of(1, t, 0, 2), 7 + t, sibling) for t in (1, 2)]
    sib_late = [par_copy(place_of(0, 3, a), place_of(1, 3, a), 10 + a, sibling) for a in range(2)]

    def build(stage):
        def block(b, carry):
            cols = pl.ds(pl.multiple_of(b * RUN, RUN), RUN)
            line = slot_v[stage, pl.ds(b, 1), :]
            oht[stage, :, cols] = (lax.broadcasted_iota(jnp.int32, (SLOTS, RUN), 0) == line).astype(F32).astype(BF16)
            return carry

        lax.fori_loop(0, ROWS // RUN, block, 0)

    build(0)

    for cp in e_copies[2:]:
        cp.start()
    pl.semaphore_wait(barrier, len(partners))
    for cp in (to_up[0], to_down[1], to_up[1], to_down[0]):
        cp.start()

    def there(start, size):
        return pl.ds(pl.multiple_of(COLS * k + start, TILE), size)

    def row_copy(r, stage, g):
        start, size = RANGES[g]
        to = (d + r) % DP
        return rcopy(
            send.at[stage, to, :, pl.ds(start, size)],
            recv.at[d, :, there(start, size)],
            row_ss.at[stage],
            row_rs,
            (to, cent_of(zhi, y, stage)),
        )

    peers = pl.ds(0, DP - 1)
    rows_in = rcopy(recv.at[peers], recv.at[peers], row_ss.at[0], row_rs, row_peer(1))
    rows_out = [rcopy(send.at[i, peers], send.at[i, peers], row_ss.at[i], row_rs, row_peer(1)) for i in range(2)]
    rows_sib = rcopy(send.at[1 - k, d], recv.at[d, :, there(0, COLS)], sib_ss, sib_rs, sibling)
    id_total = rcopy(id_send.at[peers], id_recv.at[peers], id_ss, id_rs, row_peer(1))

    for stage in range(2):
        for n in range(NTILE):
            if stage == 0:
                e_copies[n].wait()
            part = jnp.dot(oht[stage], e_v[n], preferred_element_type=F32)
            send[stage, :, :, TILE * n : TILE * (n + 1)] = part.astype(BF16).reshape(DP, CAP, TILE)
            if n in SEND_AFTER:
                for r in FAR_FIRST:
                    row_copy(r, stage, SEND_AFTER.index(n)).start()
        if stage == 0:
            for cp in (*own_par, *to_sib):
                cp.start()
            build(1)
            spots = lax.dot_general(place[...], oht[k], (((1,), (1,)), ((), ())), preferred_element_type=F32)[:8]
            lane = lax.broadcasted_iota(jnp.int32, (DP, SLOTS), 1)
            mine_at = jnp.where(lane // CAP == lax.broadcasted_iota(jnp.int32, (DP, SLOTS), 0), spots, 0.0).astype(BF16)
            lo = lax.broadcasted_iota(jnp.int32, (SLOTS, SLOTS), 0)
            hi = lax.broadcasted_iota(jnp.int32, (SLOTS, SLOTS), 1)
            shift = ((lo % CAP == hi % CAP) & (hi // CAP == d)).astype(F32).astype(BF16)
            moved = jnp.dot(mine_at, shift, preferred_element_type=F32)
            for i in range(DP):
                id_send[i] = moved[i : i + 1, :]
            for r in FAR_FIRST:
                dev = row_peer(r)
                rcopy(id_send.at[dev[0]], id_recv.at[d], id_ss, id_rs, dev).start()
    rows_sib.start()
    recv[d, :, there(0, COLS)] = send[k, d]
    id_recv[d] = id_send[d]
    ms[...] = jnp.zeros_like(ms)
    to_up[0].wait_recv()
    on_up.start()
    to_down[1].wait_recv()
    on_down.start()

    id_total.wait_recv()
    ids = jnp.sum(id_recv[...], axis=0).astype(jnp.int32) - 1
    onehot = (lax.broadcasted_iota(jnp.int32, (RUN, SLOTS), 0) == ids).astype(F32)
    counts_col = jnp.sum(onehot, axis=1, keepdims=True)
    onehot = onehot.astype(BF16)
    counts_row = lax.dot_general(jnp.ones((16, SLOTS), BF16), onehot, (((1,), (1,)), ((), ())), preferred_element_type=F32)[:1]
    rows_in.wait_recv()
    rows_sib.wait_recv()
    sums = jnp.dot(onehot, recv[...].reshape(SLOTS, W), preferred_element_type=F32)
    mean = sums / jnp.maximum(counts_col, 1.0)
    scale = jnp.sqrt(jnp.sum(mean * mean, axis=1, keepdims=True) + 1e-06)
    normed = (mean / scale).astype(BF16)
    cb[0] = normed
    cent_out = pltpu.make_async_copy(cb.at[0], cent_hbm, o_sem.at[0])
    cent_out.start()
    load_label.wait()
    meta[0, 0:1, :] = counts_row.astype(BF16).astype(F32)
    meta[0, 1:2, :] = label_v[...].astype(F32)
    meta[0, 2:8, :] = jnp.zeros((6, RUN), F32)

    def cent_copy(src, dst, start, size, idx, dev):
        rows = pl.ds(start, size)
        return rcopy(cb.at[src, rows], cb.at[dst, rows], cb_ss.at[idx], cb_rs.at[idx], dev)

    over_z = [cent_copy(0, 2, 32 * i, 32, i, group[ZN]) for i in range(4)]
    over_x = [cent_copy(0, 1, 64 * h, 64, 4 + h, group[(XP, XM)[h]]) for h in range(2)]
    pass_on = [cent_copy(2, 3, 32 * i, 32, 6 + i, group[(XP, XM)[i // 2]]) for i in range(4)]
    over_z[PIECES[0]].start()
    for cp in over_x:
        cp.start()
    for i in PIECES[1:]:
        over_z[i].start()
    metas = {p: rcopy(meta.at[0], meta.at[inverse[p]], meta_ss.at[p], meta_rs.at[inverse[p]], group[p]) for p in group}
    for p in (ZXM, ZXP, ZN, XM, XP):
        metas[p].start()

    def arrived(p):
        return rcopy(meta.at[0], meta.at[p], meta_ss.at[p], meta_rs.at[p], group[p])

    for cp in (*rows_out, rows_sib):
        cp.wait_send()
    id_total.wait_send()
    to_up[1].wait_recv()
    sib_early[0].start()
    to_down[0].wait_recv()
    sib_early[1].start()
    for i in PIECES:
        over_z[i].wait_recv()
        pass_on[i].start()
    on_up.wait_recv()
    sib_late[0].start()
    on_down.wait_recv()
    sib_late[1].start()
    for cp in own_par:
        cp.wait()
    for cp in (*to_sib, *over_x, *sib_early):
        cp.wait_recv()
    for p in group:
        arrived(p).wait_recv()

    low_lanes = lax.broadcasted_iota(jnp.int32, (1, RUN), 1) < RUN // 2

    def halves(low, high):
        return jnp.where(low_lanes, low, high)

    def meta_line(i):
        return [
            meta[0, i : i + 1, :],
            halves(meta[XM, i : i + 1, :], meta[XP, i : i + 1, :]),
            meta[ZN, i : i + 1, :],
            halves(meta[ZXM, i : i + 1, :], meta[ZXP, i : i + 1, :]),
        ]

    weights, labels = meta_line(0), meta_line(1)

    firsts = [
        cent_of(zhi, y_of[t], core) * SLAB + 2 * BLK * a + BLK * q
        for times in ((0, 1, 2), (3,))
        for core in (k, 1 - k)
        for t in times
        for a in range(2)
    ]

    def score(pair, size, first_step, steps):
        cols = slice(2 * RUN * pair, 2 * RUN * (pair + 1))
        label = jnp.concatenate([labels[2 * pair], labels[2 * pair + 1]], axis=1).astype(jnp.int32)
        per = size // BLK

        def step(i, carry):
            rows = pl.ds(pl.multiple_of(i * size, size), size)
            block = cb[2 * pair : 2 * pair + 2].reshape(2 * RUN, W)
            s = lax.dot_general(par[rows, :], block, (((1,), (1,)), ((), ())), preferred_element_type=F32)
            line = lax.broadcasted_iota(jnp.int32, (BLK, 2 * RUN), 0)
            parts = []
            for b in range(per):
                first = firsts[per * first_step + b]
                for other in range(first_step + 1, first_step + steps):
                    first = jnp.where(i == other, firsts[per * other + b], first)
                bonus = jnp.where(line == label - first, REWARD, 0.0)
                parts.append(s[BLK * b : BLK * (b + 1)] * INV_SOFT + bonus)
            s = jnp.concatenate(parts, axis=0)
            top = jnp.max(s, axis=0, keepdims=True)
            e = jnp.exp(s - top)
            scores[rows, cols] = e
            total = jnp.sum(e, axis=0, keepdims=True)
            for h in range(size // MCH):
                at = pl.ds(i * (size // MCH) + h, 1)
                mch[at, cols] = top
                sch[at, cols] = total if h == 0 else jnp.zeros_like(total)
            return carry

        lax.fori_loop(first_step, first_step + steps, step, 0)

    score(0, MCH, 0, 3)
    for cp in (*to_up, *to_down, *to_sib, *sib_early, *metas.values(), *over_x):
        cp.wait_send()
    cent_out.wait()
    for cp in sib_late:
        cp.wait_recv()
    score(0, MCH, 3, 1)
    for cp in pass_on:
        cp.wait_recv()
    score(1, 2 * MCH, 0, 2)

    m_loc = jnp.max(mch[...], axis=0, keepdims=True)
    s_loc = jnp.sum(sch[...] * jnp.exp(mch[...] - m_loc), axis=0, keepdims=True)
    for j in range(4):
        stat[0, j : j + 1, :] = m_loc[:, RUN * j : RUN * (j + 1)]
        stat[0, 4 + j : 5 + j, :] = s_loc[:, RUN * j : RUN * (j + 1)]
    stats = {p: rcopy(stat.at[0], stat.at[inverse[p]], stat_ss.at[p], stat_rs.at[inverse[p]], group[p]) for p in group}
    for p in (ZXM, ZXP, ZN, XM, XP):
        stats[p].start()
    for cp in (*over_z, *pass_on, on_up, on_down, *sib_late):
        cp.wait_send()
    for p in group:
        rcopy(stat.at[0], stat.at[p], stat_ss.at[p], stat_rs.at[p], group[p]).wait_recv()
    elsewhere = (
        (((XP, 1), (XM, 1)), ((ZN, 2), (ZN, 2)), ((ZXP, 3), (ZXM, 3))),
        (((XM, 0), (XP, 0)), ((ZXM, 2), (ZXP, 2)), ((ZN, 3), (ZN, 3))),
        (((ZN, 0), (ZN, 0)), ((XP, 3), (XM, 3)), ((ZXP, 1), (ZXM, 1))),
        (((ZXM, 0), (ZXP, 0)), ((XM, 2), (XP, 2)), ((ZN, 1), (ZN, 1))),
    )
    for j in range(4):

        def line(at, i):
            return stat[at[0], i + at[1] : i + at[1] + 1, :]

        m = [stat[0, j : j + 1, :]] + [halves(line(lo, 0), line(hi, 0)) for lo, hi in elsewhere[j]]
        s = [stat[0, 4 + j : 5 + j, :]] + [halves(line(lo, 4), line(hi, 4)) for lo, hi in elsewhere[j]]
        top = jnp.maximum(jnp.maximum(m[0], m[1]), jnp.maximum(m[2], m[3]))
        total = sum(s[i] * jnp.exp(m[i] - top) for i in range(4))
        log_total = top + jnp.log(total)
        if j == 0:
            logt_v[...] = log_total
            logt_out = pltpu.make_async_copy(logt_v, logt_hbm, o_sem.at[1])
            logt_out.start()
        cols = slice(RUN * j, RUN * (j + 1))
        fac[:, cols] = weights[j] * jnp.exp(mch[:, cols] - log_total)

    def mass_step(i, carry):
        f = fac[pl.ds(i, 1), :]
        rows = pl.ds(pl.multiple_of(i * MCH, MCH), MCH)
        acc = jnp.zeros((MCH, RUN), F32)
        for j in range(4):
            cols = slice(RUN * j, RUN * (j + 1))
            acc = acc + scores[rows, cols] * f[:, cols]
        terms[i] = jnp.sum(acc.T, axis=0, keepdims=True)
        return carry

    lax.fori_loop(0, 4, mass_step, 0)
    mp[0, :, 0:512] = terms[0]
    mp[0, :, 512:768] = terms[1][:, :256]
    mp[0, :, 768:1024] = terms[3][:, :256]
    mp[1, :, 0:256] = terms[1][:, 256:]
    mp[1, :, 256:768] = terms[2]
    mp[1, :, 768:1024] = terms[3][:, 256:]

    to_sib_mass = rcopy(mp.at[1], sib_in, m1_ss, m1_rs, sibling)
    to_sib_mass.start()
    to_sib_mass.wait_recv()
    both = mp[0] + sib_in[...]
    for i in range(2 * DP):
        ms[i, :, :PART] = both[:, PART * i : PART * (i + 1)]

    for i, o in enumerate(owners):
        at, dev = owner(*o)
        rcopy(ms.at[at], mr.at[i], m2_ss, m2_rs, dev).start()
    own_mass = pltpu.make_async_copy(ms.at[owner(0, 0, 0)[0]], mr.at[2 * DP - 1], o_sem.at[2])
    own_mass.start()
    for cp in [to_sib_mass, *stats.values()]:
        cp.wait_send()
    logt_out.wait()
    own_mass.wait()
    lines = pl.ds(0, 2 * DP - 1)
    rcopy(ms.at[lines], mr.at[lines], m2_ss, m2_rs, row_peer(1)).wait()


def hand_on(cent, logt, terms, cent_out, logt_out, mass_out):
    cent_out[...] = cent[...]
    logt_out[...] = logt[...]
    mass_out[...] = jnp.sum(terms[...], axis=0)[:, :PART]


def per_device(embeddings, assignments, parents, starting_coarse_label):
    vmem = pl.BlockSpec(memory_space=pltpu.VMEM)
    hbm = pl.BlockSpec(memory_space=pltpu.HBM)
    anywhere = pl.BlockSpec(memory_space=pl.ANY)
    dma = pltpu.SemaphoreType.DMA
    operands = (assignments.reshape(32, RUN), starting_coarse_label.reshape(1, RUN), embeddings, parents)
    cent, logt, terms = pl.pallas_call(
        kernel,
        out_shape=(
            jax.ShapeDtypeStruct((RUN, W), BF16),
            jax.ShapeDtypeStruct((1, RUN), F32),
            jax.ShapeDtypeStruct((2 * DP, 1, RUN), F32),
        ),
        in_specs=[hbm, hbm, hbm, hbm],
        out_specs=(anywhere, anywhere, anywhere),
        scratch_shapes=[
            pltpu.VMEM((32, RUN), jnp.int32),
            pltpu.VMEM((1, RUN), jnp.int32),
            pltpu.VMEM((NTILE, ROWS, TILE), BF16),
            pltpu.VMEM((2, SLOTS, ROWS), BF16),
            pltpu.VMEM((16, ROWS), BF16),
            pltpu.VMEM((2, 32, RUN), jnp.int32),
            pltpu.VMEM((2, DP, CAP, COLS), BF16),
            pltpu.VMEM((DP, CAP, W), BF16),
            pltpu.VMEM((DP, 1, SLOTS), F32),
            pltpu.VMEM((DP, 1, SLOTS), F32),
            pltpu.VMEM((EARLY + LATE, W), BF16),
            pltpu.VMEM((4, RUN, W), BF16),
            pltpu.VMEM((6, 8, RUN), F32),
            pltpu.VMEM((EARLY + LATE, 4 * RUN), F32),
            pltpu.VMEM((4, 4 * RUN), F32),
            pltpu.VMEM((4, 4 * RUN), F32),
            pltpu.VMEM((6, 8, RUN), F32),
            pltpu.VMEM((4, 4 * RUN), F32),
            pltpu.VMEM((4, 1, MCH), F32),
            pltpu.VMEM((2, 1, 1024), F32),
            pltpu.VMEM((1, 1024), F32),
            pltpu.VMEM((2 * DP, 1, RUN), F32),
            pltpu.VMEM((1, RUN), F32),
            dma((NTILE,)),
            dma((2,)),
            dma((2,)),
            dma,
            dma,
            dma,
            dma,
            dma,
            dma((12,)),
            dma((12,)),
            dma((10,)),
            dma((10,)),
            dma((6,)),
            dma((6,)),
            dma((6,)),
            dma((6,)),
            dma,
            dma,
            dma,
            dma,
            dma((3,)),
            dma((2,)),
        ],
        compiler_params=pltpu.CompilerParams(collective_id=0, has_side_effects=True, vmem_limit_bytes=52 << 20),
        name="handover",
    )(
        *(pltpu.with_memory_space_constraint(v, pltpu.HBM) for v in operands),
    )
    cent, logt, mass = pl.pallas_call(
        hand_on,
        out_shape=(
            jax.ShapeDtypeStruct((RUN, W), BF16),
            jax.ShapeDtypeStruct((1, RUN), F32),
            jax.ShapeDtypeStruct((1, PART), F32),
        ),
        in_specs=[vmem, vmem, vmem],
        out_specs=(vmem, vmem, vmem),
        compiler_params=pltpu.CompilerParams(vmem_limit_bytes=2 << 20),
        name="finish",
    )(cent, logt, terms)
    return cent, logt.reshape(RUN), mass.reshape(PART)


def solution(mesh):
    return jax.shard_map(
        per_device,
        mesh=mesh,
        in_specs=(P("dp", None), P("dp"), P("cent", None), P(("cent", "dp"))),
        out_specs=(P(("cent", "dp"), None), P(("cent", "dp")), P(("cent", "dp"))),
        check_vma=False,
    )
```

```python
import jax
import jax.numpy as jnp
from jax import lax
from jax.experimental import pallas as pl
from jax.experimental.pallas import tpu as pltpu
from jax.sharding import PartitionSpec as P

MESH = pl.DeviceIdType.MESH
F32 = jnp.float32
BF16 = jnp.bfloat16

W = 1536
RUN = 128
CAP = 48
DP = 8
SLOTS = DP * CAP
TILE = 256
COLS = W // 2
NTILE = COLS // TILE
ROWS = 4096
SLAB = 512
PART = 64
EARLY, LATE = 1536, 512
BLK = 128
MCH = 512
PIECES = (0, 2, 1, 3)
INV_SOFT = 1.0 / 0.5
REWARD = 1.5

RANGES = ((0, 256), (256, 512))
SEND_AFTER = (0, 2)
FAR_FIRST = (5, 3, 4, 6, 2, 7, 1)


def kernel(
    a_hbm, label_hbm, e_hbm, p_hbm,
    cent_hbm, logt_hbm, mr,
    a_v, label_v, e_v, oht, place, slot_v, send, recv, id_send, id_recv, par, cb, meta, scores, mch, sch, stat, fac, terms, mp, sib_in, ms, logt_v,
    e_sem, p_sem, row_ss, row_rs, sib_ss, sib_rs, id_ss, id_rs, par_ss, par_rs, cb_ss, cb_rs, meta_ss, meta_rs, stat_ss, stat_rs,
    m1_ss, m1_rs, m2_ss, m2_rs, o_sem, in_sem,
):
    d = lax.axis_index("dp")
    c = lax.axis_index("cent")
    zlo = d % 2
    zhi = c // 8
    y = (c // 2) % 4
    k = c % 2

    def cent_of(zh, yy, kk):
        return zh * 8 + yy * 2 + kk

    yp, ym, y2 = (y + 1) % 4, (y + 3) % 4, (y + 2) % 4
    x = d // 2
    q = x % 2
    xp, xm = (x + 1) % 4, (x + 3) % 4
    other_z = cent_of(1 - zhi, y, k)
    ZN, XM, XP, ZXM, ZXP = 1, 2, 3, 4, 5
    group = {
        ZN: (x * 2 + 1 - zlo, other_z),
        XM: (xm * 2 + zlo, c),
        XP: (xp * 2 + zlo, c),
        ZXM: (xm * 2 + 1 - zlo, other_z),
        ZXP: (xp * 2 + 1 - zlo, other_z),
    }
    inverse = {ZN: ZN, XM: XP, XP: XM, ZXM: ZXP, ZXP: ZXM}
    sibling = (d, cent_of(zhi, y, 1 - k))
    up = (d, cent_of(zhi, yp, k))
    down = (d, cent_of(zhi, ym, k))
    y_of = (y, ym, yp, y2)

    def owner(t, ra, rb):
        a, b = (x // 2 + ra) % 2, (zlo + rb) % 2
        return 4 * t + 2 * a + b, ((2 * a + q) * 2 + b, cent_of(zhi, y_of[t], k))

    owners = [(t, ra, rb) for t in (3, 2, 1, 0) for ra in (1, 0) for rb in (1, 0) if (t, ra, rb) != (0, 0, 0)]

    def row_peer(r):
        return ((d + r) % DP, c)

    def rcopy(src, dst, ss, rs, dev):
        return pltpu.make_async_remote_copy(
            src_ref=src, dst_ref=dst, send_sem=ss, recv_sem=rs, device_id=dev, device_id_type=MESH
        )

    load_a = pltpu.make_async_copy(a_hbm, a_v, in_sem.at[0])
    load_label = pltpu.make_async_copy(label_hbm, label_v, in_sem.at[1])
    e_copies = [
        pltpu.make_async_copy(
            e_hbm.at[:, pl.ds(pl.multiple_of(COLS * k + TILE * n, TILE), TILE)], e_v.at[n], e_sem.at[n]
        )
        for n in range(NTILE)
    ]
    def mine(a):
        return p_hbm.at[pl.ds(pl.multiple_of(2 * BLK * a + BLK * q, BLK), BLK)]

    def place_of(core, t, a=0, n=1):
        start = (EARLY + 256 * core if t == 3 else 768 * core + 256 * t) + BLK * a
        return par.at[pl.ds(start, BLK * n)]

    own_par = [pltpu.make_async_copy(mine(a), place_of(0, 0, a), p_sem.at[a]) for a in range(2)]
    load_a.start()
    e_copies[0].start()

    barrier = pltpu.get_barrier_semaphore()
    partners = [row_peer(r) for r in range(1, DP)] + [group[ZN], group[ZXM], group[ZXP], sibling]
    partners += [((d + r) % DP, cent_of(zhi, y, 1 - k)) for r in range(1, DP)]
    partners += [owner(*o)[1] for o in owners if o[0] != 0]
    for dev in partners:
        pl.semaphore_signal(barrier, inc=1, device_id=dev, device_id_type=MESH)

    e_copies[1].start()
    load_label.start()
    load_a.wait()

    a = a_v[...]
    run_id = lax.broadcasted_iota(jnp.int32, (32, 8, RUN), 1)
    upper = (
        lax.broadcasted_iota(jnp.int32, (RUN, RUN), 0) < lax.broadcasted_iota(jnp.int32, (RUN, RUN), 1)
    ).astype(F32).astype(BF16)
    ri = lax.broadcasted_iota(jnp.int32, (256, 256), 0)
    ci = lax.broadcasted_iota(jnp.int32, (256, 256), 1)
    before = (((ri & 7) == (ci & 7)) & (ci < ri)).astype(F32).astype(BF16)
    base = ((lax.broadcasted_iota(jnp.int32, (256, RUN), 0) & 7) * CAP + 1).astype(F32)
    def find_slots(stage):
        rel = lax.shift_right_logical(a, 7) - cent_of(zhi, y, stage) * DP
        member = (rel[:, None, :] == run_id).astype(F32).reshape(256, RUN)
        member_b = member.astype(BF16)
        within = jnp.dot(member_b, upper, preferred_element_type=F32)
        earlier = jnp.dot(before, member_b, preferred_element_type=F32).astype(BF16)
        ahead = jnp.dot(earlier, jnp.ones((RUN, RUN), BF16), preferred_element_type=F32)
        slot = jnp.sum((member * (within + ahead + base)).reshape(32, 8, RUN), axis=1) - 1.0
        slot_v[stage] = slot.astype(jnp.int32)

    find_slots(0)

    def par_copy(src, dst, idx, dev):
        return rcopy(src, dst, par_ss.at[idx], par_rs.at[idx], dev)

    to_up = [par_copy(mine(a), place_of(0, 1, a), a, up) for a in range(2)]
    to_down = [par_copy(mine(a), place_of(0, 2, a), 2 + a, down) for a in range(2)]
    on_up = par_copy(place_of(0, 1, 0), place_of(0, 3, 0), 4, up)
    on_down = par_copy(place_of(0, 2, 1), place_of(0, 3, 1), 5, down)
    to_sib = [par_copy(mine(a), place_of(1, 0, a), 6 + a, sibling) for a in range(2)]
    sib_early = [par_copy(place_of(0, t, 0, 2), place_of(1, t, 0, 2), 7 + t, sibling) for t in (1, 2)]
    sib_late = [par_copy(place_of(0, 3, a), place_of(1, 3, a), 10 + a, sibling) for a in range(2)]

    def build(stage):
        def block(b, carry):
            cols = pl.ds(pl.multiple_of(b * RUN, RUN), RUN)
            line = slot_v[stage, pl.ds(b, 1), :]
            oht[stage, :, cols] = (lax.broadcasted_iota(jnp.int32, (SLOTS, RUN), 0) == line).astype(F32).astype(BF16)
            return carry

        lax.fori_loop(0, ROWS // RUN, block, 0)

    pl.semaphore_wait(barrier, len(partners))
    for cp in (to_up[0], to_down[1], to_up[1], to_down[0]):
        cp.start()
    build(0)

    for cp in e_copies[2:]:
        cp.start()

    def there(start, size):
        return pl.ds(pl.multiple_of(COLS * k + start, TILE), size)

    def row_copy(r, stage, g):
        start, size = RANGES[g]
        to = (d + r) % DP
        return rcopy(
            send.at[stage, to, :, pl.ds(start, size)],
            recv.at[d, :, there(start, size)],
            row_ss.at[stage],
            row_rs,
            (to, cent_of(zhi, y, stage)),
        )

    peers = pl.ds(0, DP - 1)
    rows_in = rcopy(recv.at[peers], recv.at[peers], row_ss.at[0], row_rs, row_peer(1))
    rows_out = [rcopy(send.at[i, peers], send.at[i, peers], row_ss.at[i], row_rs, row_peer(1)) for i in range(2)]
    rows_sib = rcopy(send.at[1 - k, d], recv.at[d, :, there(0, COLS)], sib_ss, sib_rs, sibling)
    id_total = rcopy(id_send.at[peers], id_recv.at[peers], id_ss, id_rs, row_peer(1))

    for stage in range(2):
        for n in range(NTILE):
            if stage == 0:
                e_copies[n].wait()
            part = jnp.dot(oht[stage], e_v[n], preferred_element_type=F32)
            send[stage, :, :, TILE * n : TILE * (n + 1)] = part.astype(BF16).reshape(DP, CAP, TILE)
            if n in SEND_AFTER:
                for r in FAR_FIRST:
                    row_copy(r, stage, SEND_AFTER.index(n)).start()
        if stage == 0:
            for cp in (*own_par, *to_sib):
                cp.start()
            find_slots(1)
            build(1)
            spot = ((a & (RUN - 1)) + 1).astype(F32)
            for b in range(ROWS // RUN):
                place[:, RUN * b : RUN * (b + 1)] = jnp.broadcast_to(spot[b : b + 1, :], (16, RUN)).astype(BF16)
            spots = lax.dot_general(place[...], oht[k], (((1,), (1,)), ((), ())), preferred_element_type=F32)[:8]
            lane = lax.broadcasted_iota(jnp.int32, (DP, SLOTS), 1)
            mine_at = jnp.where(lane // CAP == lax.broadcasted_iota(jnp.int32, (DP, SLOTS), 0), spots, 0.0).astype(BF16)
            lo = lax.broadcasted_iota(jnp.int32, (SLOTS, SLOTS), 0)
            hi = lax.broadcasted_iota(jnp.int32, (SLOTS, SLOTS), 1)
            shift = ((lo % CAP == hi % CAP) & (hi // CAP == d)).astype(F32).astype(BF16)
            moved = jnp.dot(mine_at, shift, preferred_element_type=F32)
            for i in range(DP):
                id_send[i] = moved[i : i + 1, :]
            for r in FAR_FIRST:
                dev = row_peer(r)
                rcopy(id_send.at[dev[0]], id_recv.at[d], id_ss, id_rs, dev).start()
    rows_sib.start()
    recv[d, :, there(0, COLS)] = send[k, d]
    id_recv[d] = id_send[d]
    ms[...] = jnp.zeros_like(ms)
    to_up[0].wait_recv()
    on_up.start()
    to_down[1].wait_recv()
    on_down.start()

    id_total.wait_recv()
    ids = jnp.sum(id_recv[...], axis=0).astype(jnp.int32) - 1
    onehot = (lax.broadcasted_iota(jnp.int32, (RUN, SLOTS), 0) == ids).astype(F32)
    counts_col = jnp.sum(onehot, axis=1, keepdims=True)
    onehot = onehot.astype(BF16)
    counts_row = lax.dot_general(jnp.ones((16, SLOTS), BF16), onehot, (((1,), (1,)), ((), ())), preferred_element_type=F32)[:1]
    rows_in.wait_recv()
    rows_sib.wait_recv()
    sums = jnp.dot(onehot, recv[...].reshape(SLOTS, W), preferred_element_type=F32)
    mean = sums / jnp.maximum(counts_col, 1.0)
    scale = jnp.sqrt(jnp.sum(mean * mean, axis=1, keepdims=True) + 1e-06)
    normed = (mean / scale).astype(BF16)
    cb[0] = normed
    cent_out = pltpu.make_async_copy(cb.at[0], cent_hbm, o_sem.at[0])
    cent_out.start()
    load_label.wait()
    meta[0, 0:1, :] = counts_row.astype(BF16).astype(F32)
    meta[0, 1:2, :] = label_v[...].astype(F32)
    meta[0, 2:8, :] = jnp.zeros((6, RUN), F32)

    def cent_copy(src, dst, start, size, idx, dev):
        rows = pl.ds(start, size)
        return rcopy(cb.at[src, rows], cb.at[dst, rows], cb_ss.at[idx], cb_rs.at[idx], dev)

    over_z = [cent_copy(0, 2, 32 * i, 32, i, group[ZN]) for i in range(4)]
    over_x = [cent_copy(0, 1, 64 * h, 64, 4 + h, group[(XP, XM)[h]]) for h in range(2)]
    pass_on = [cent_copy(2, 3, 32 * i, 32, 6 + i, group[(XP, XM)[i // 2]]) for i in range(4)]
    over_z[PIECES[0]].start()
    for cp in over_x:
        cp.start()
    for i in PIECES[1:]:
        over_z[i].start()
    metas = {p: rcopy(meta.at[0], meta.at[inverse[p]], meta_ss.at[p], meta_rs.at[inverse[p]], group[p]) for p in group}
    for p in (ZXM, ZXP, ZN, XM, XP):
        metas[p].start()

    def arrived(p):
        return rcopy(meta.at[0], meta.at[p], meta_ss.at[p], meta_rs.at[p], group[p])

    for cp in (*rows_out, rows_sib):
        cp.wait_send()
    id_total.wait_send()
    to_up[1].wait_recv()
    sib_early[0].start()
    to_down[0].wait_recv()
    sib_early[1].start()
    for i in PIECES:
        over_z[i].wait_recv()
        pass_on[i].start()
    on_up.wait_recv()
    sib_late[0].start()
    on_down.wait_recv()
    sib_late[1].start()
    for cp in own_par:
        cp.wait()
    for cp in (*to_sib, *over_x, *sib_early):
        cp.wait_recv()
    for p in group:
        arrived(p).wait_recv()

    low_lanes = lax.broadcasted_iota(jnp.int32, (1, RUN), 1) < RUN // 2

    def halves(low, high):
        return jnp.where(low_lanes, low, high)

    def meta_line(i):
        return [
            meta[0, i : i + 1, :],
            halves(meta[XM, i : i + 1, :], meta[XP, i : i + 1, :]),
            meta[ZN, i : i + 1, :],
            halves(meta[ZXM, i : i + 1, :], meta[ZXP, i : i + 1, :]),
        ]

    weights, labels = meta_line(0), meta_line(1)

    firsts = [
        cent_of(zhi, y_of[t], core) * SLAB + 2 * BLK * a + BLK * q
        for times in ((0, 1, 2), (3,))
        for core in (k, 1 - k)
        for t in times
        for a in range(2)
    ]

    def score(pair, size, first_step, steps):
        cols = slice(2 * RUN * pair, 2 * RUN * (pair + 1))
        label = jnp.concatenate([labels[2 * pair], labels[2 * pair + 1]], axis=1).astype(jnp.int32)
        per = size // BLK

        def step(i, carry):
            rows = pl.ds(pl.multiple_of(i * size, size), size)
            block = cb[2 * pair : 2 * pair + 2].reshape(2 * RUN, W)
            s = lax.dot_general(par[rows, :], block, (((1,), (1,)), ((), ())), preferred_element_type=F32)
            line = lax.broadcasted_iota(jnp.int32, (BLK, 2 * RUN), 0)
            parts = []
            for b in range(per):
                first = firsts[per * first_step + b]
                for other in range(first_step + 1, first_step + steps):
                    first = jnp.where(i == other, firsts[per * other + b], first)
                bonus = jnp.where(line == label - first, REWARD, 0.0)
                parts.append(s[BLK * b : BLK * (b + 1)] * INV_SOFT + bonus)
            s = jnp.concatenate(parts, axis=0)
            top = jnp.max(s, axis=0, keepdims=True)
            e = jnp.exp(s - top)
            scores[rows, cols] = e
            total = jnp.sum(e, axis=0, keepdims=True)
            for h in range(size // MCH):
                at = pl.ds(i * (size // MCH) + h, 1)
                mch[at, cols] = top
                sch[at, cols] = total if h == 0 else jnp.zeros_like(total)
            return carry

        lax.fori_loop(first_step, first_step + steps, step, 0)

    score(0, MCH, 0, 3)
    for cp in (*to_up, *to_down, *to_sib, *sib_early, *metas.values(), *over_x):
        cp.wait_send()
    cent_out.wait()
    for cp in sib_late:
        cp.wait_recv()
    score(0, MCH, 3, 1)
    for cp in pass_on:
        cp.wait_recv()
    score(1, 2 * MCH, 0, 2)

    m_loc = jnp.max(mch[...], axis=0, keepdims=True)
    s_loc = jnp.sum(sch[...] * jnp.exp(mch[...] - m_loc), axis=0, keepdims=True)
    for j in range(4):
        stat[0, j : j + 1, :] = m_loc[:, RUN * j : RUN * (j + 1)]
        stat[0, 4 + j : 5 + j, :] = s_loc[:, RUN * j : RUN * (j + 1)]
    stats = {p: rcopy(stat.at[0], stat.at[inverse[p]], stat_ss.at[p], stat_rs.at[inverse[p]], group[p]) for p in group}
    for p in (ZXM, ZXP, ZN, XM, XP):
        stats[p].start()
    for cp in (*over_z, *pass_on, on_up, on_down, *sib_late):
        cp.wait_send()
    for p in group:
        rcopy(stat.at[0], stat.at[p], stat_ss.at[p], stat_rs.at[p], group[p]).wait_recv()
    elsewhere = (
        (((XP, 1), (XM, 1)), ((ZN, 2), (ZN, 2)), ((ZXP, 3), (ZXM, 3))),
        (((XM, 0), (XP, 0)), ((ZXM, 2), (ZXP, 2)), ((ZN, 3), (ZN, 3))),
        (((ZN, 0), (ZN, 0)), ((XP, 3), (XM, 3)), ((ZXP, 1), (ZXM, 1))),
        (((ZXM, 0), (ZXP, 0)), ((XM, 2), (XP, 2)), ((ZN, 1), (ZN, 1))),
    )
    for j in range(4):

        def line(at, i):
            return stat[at[0], i + at[1] : i + at[1] + 1, :]

        m = [stat[0, j : j + 1, :]] + [halves(line(lo, 0), line(hi, 0)) for lo, hi in elsewhere[j]]
        s = [stat[0, 4 + j : 5 + j, :]] + [halves(line(lo, 4), line(hi, 4)) for lo, hi in elsewhere[j]]
        top = jnp.maximum(jnp.maximum(m[0], m[1]), jnp.maximum(m[2], m[3]))
        total = sum(s[i] * jnp.exp(m[i] - top) for i in range(4))
        log_total = top + jnp.log(total)
        if j == 0:
            logt_v[...] = log_total
            logt_out = pltpu.make_async_copy(logt_v, logt_hbm, o_sem.at[1])
            logt_out.start()
        cols = slice(RUN * j, RUN * (j + 1))
        fac[:, cols] = weights[j] * jnp.exp(mch[:, cols] - log_total)

    def mass_step(i, carry):
        f = fac[pl.ds(i, 1), :]
        rows = pl.ds(pl.multiple_of(i * MCH, MCH), MCH)
        acc = jnp.zeros((MCH, RUN), F32)
        for j in range(4):
            cols = slice(RUN * j, RUN * (j + 1))
            acc = acc + scores[rows, cols] * f[:, cols]
        terms[i] = jnp.sum(acc.T, axis=0, keepdims=True)
        return carry

    lax.fori_loop(0, 4, mass_step, 0)
    mp[0, :, 0:512] = terms[0]
    mp[0, :, 512:768] = terms[1][:, :256]
    mp[0, :, 768:1024] = terms[3][:, :256]
    mp[1, :, 0:256] = terms[1][:, 256:]
    mp[1, :, 256:768] = terms[2]
    mp[1, :, 768:1024] = terms[3][:, 256:]

    to_sib_mass = rcopy(mp.at[1], sib_in, m1_ss, m1_rs, sibling)
    to_sib_mass.start()
    to_sib_mass.wait_recv()
    both = mp[0] + sib_in[...]
    for i in range(2 * DP):
        ms[i, :, :PART] = both[:, PART * i : PART * (i + 1)]

    for i, o in enumerate(owners):
        at, dev = owner(*o)
        rcopy(ms.at[at], mr.at[i], m2_ss, m2_rs, dev).start()
    own_mass = pltpu.make_async_copy(ms.at[owner(0, 0, 0)[0]], mr.at[2 * DP - 1], o_sem.at[2])
    own_mass.start()
    for cp in [to_sib_mass, *stats.values()]:
        cp.wait_send()
    logt_out.wait()
    own_mass.wait()
    lines = pl.ds(0, 2 * DP - 1)
    rcopy(ms.at[lines], mr.at[lines], m2_ss, m2_rs, row_peer(1)).wait()


def hand_on(cent, logt, terms, cent_out, logt_out, mass_out):
    cent_out[...] = cent[...]
    logt_out[...] = logt[...]
    mass_out[...] = jnp.sum(terms[...], axis=0)[:, :PART]


def per_device(embeddings, assignments, parents, starting_coarse_label):
    vmem = pl.BlockSpec(memory_space=pltpu.VMEM)
    hbm = pl.BlockSpec(memory_space=pltpu.HBM)
    anywhere = pl.BlockSpec(memory_space=pl.ANY)
    dma = pltpu.SemaphoreType.DMA
    operands = (assignments.reshape(32, RUN), starting_coarse_label.reshape(1, RUN), embeddings, parents)
    cent, logt, terms = pl.pallas_call(
        kernel,
        out_shape=(
            jax.ShapeDtypeStruct((RUN, W), BF16),
            jax.ShapeDtypeStruct((1, RUN), F32),
            jax.ShapeDtypeStruct((2 * DP, 1, RUN), F32),
        ),
        in_specs=[hbm, hbm, hbm, hbm],
        out_specs=(anywhere, anywhere, anywhere),
        scratch_shapes=[
            pltpu.VMEM((32, RUN), jnp.int32),
            pltpu.VMEM((1, RUN), jnp.int32),
            pltpu.VMEM((NTILE, ROWS, TILE), BF16),
            pltpu.VMEM((2, SLOTS, ROWS), BF16),
            pltpu.VMEM((16, ROWS), BF16),
            pltpu.VMEM((2, 32, RUN), jnp.int32),
            pltpu.VMEM((2, DP, CAP, COLS), BF16),
            pltpu.VMEM((DP, CAP, W), BF16),
            pltpu.VMEM((DP, 1, SLOTS), F32),
            pltpu.VMEM((DP, 1, SLOTS), F32),
            pltpu.VMEM((EARLY + LATE, W), BF16),
            pltpu.VMEM((4, RUN, W), BF16),
            pltpu.VMEM((6, 8, RUN), F32),
            pltpu.VMEM((EARLY + LATE, 4 * RUN), F32),
            pltpu.VMEM((4, 4 * RUN), F32),
            pltpu.VMEM((4, 4 * RUN), F32),
            pltpu.VMEM((6, 8, RUN), F32),
            pltpu.VMEM((4, 4 * RUN), F32),
            pltpu.VMEM((4, 1, MCH), F32),
            pltpu.VMEM((2, 1, 1024), F32),
            pltpu.VMEM((1, 1024), F32),
            pltpu.VMEM((2 * DP, 1, RUN), F32),
            pltpu.VMEM((1, RUN), F32),
            dma((NTILE,)),
            dma((2,)),
            dma((2,)),
            dma,
            dma,
            dma,
            dma,
            dma,
            dma((12,)),
            dma((12,)),
            dma((10,)),
            dma((10,)),
            dma((6,)),
            dma((6,)),
            dma((6,)),
            dma((6,)),
            dma,
            dma,
            dma,
            dma,
            dma((3,)),
            dma((2,)),
        ],
        compiler_params=pltpu.CompilerParams(collective_id=0, has_side_effects=True, vmem_limit_bytes=52 << 20),
        name="handover",
    )(
        *(pltpu.with_memory_space_constraint(v, pltpu.HBM) for v in operands),
    )
    cent, logt, mass = pl.pallas_call(
        hand_on,
        out_shape=(
            jax.ShapeDtypeStruct((RUN, W), BF16),
            jax.ShapeDtypeStruct((1, RUN), F32),
            jax.ShapeDtypeStruct((1, PART), F32),
        ),
        in_specs=[vmem, vmem, vmem],
        out_specs=(vmem, vmem, vmem),
        compiler_params=pltpu.CompilerParams(vmem_limit_bytes=2 << 20),
        name="finish",
    )(cent, logt, terms)
    return cent, logt.reshape(RUN), mass.reshape(PART)


def solution(mesh):
    return jax.shard_map(
        per_device,
        mesh=mesh,
        in_specs=(P("dp", None), P("dp"), P("cent", None), P(("cent", "dp"))),
        out_specs=(P(("cent", "dp"), None), P(("cent", "dp")), P(("cent", "dp"))),
        check_vma=False,
    )
```

```python
import jax
import jax.numpy as jnp
from jax import lax
from jax.experimental import pallas as pl
from jax.experimental.pallas import tpu as pltpu
from jax.sharding import PartitionSpec as P

MESH = pl.DeviceIdType.MESH
F32 = jnp.float32
BF16 = jnp.bfloat16

W = 1536
RUN = 128
CAP = 48
DP = 8
SLOTS = DP * CAP
TILE = 256
COLS = W // 2
NTILE = COLS // TILE
ROWS = 4096
SLAB = 512
PART = 64
EARLY, LATE = 1536, 512
BLK = 128
MCH = 512
PIECES = (0, 2, 1, 3)
INV_SOFT = 1.0 / 0.5
REWARD = 1.5

RANGES = ((0, 256), (256, 512))
SEND_AFTER = (0, 2)
FAR_FIRST = (5, 3, 4, 6, 2, 7, 1)


def kernel(
    a_hbm, label_hbm, e_hbm, p_hbm,
    cent_hbm, logt_hbm, mr,
    a_v, label_v, e_v, oht, place, slot_v, send, recv, id_send, id_recv, par, cb, meta, scores, mch, sch, stat, fac, terms, mp, sib_in, ms, logt_v,
    e_sem, p_sem, row_ss, row_rs, sib_ss, sib_rs, id_ss, id_rs, par_ss, par_rs, cb_ss, cb_rs, meta_ss, meta_rs, stat_ss, stat_rs,
    m1_ss, m1_rs, m2_ss, m2_rs, o_sem, in_sem,
):
    d = lax.axis_index("dp")
    c = lax.axis_index("cent")
    zlo = d % 2
    zhi = c // 8
    y = (c // 2) % 4
    k = c % 2

    def cent_of(zh, yy, kk):
        return zh * 8 + yy * 2 + kk

    yp, ym, y2 = (y + 1) % 4, (y + 3) % 4, (y + 2) % 4
    x = d // 2
    q = x % 2
    xp, xm = (x + 1) % 4, (x + 3) % 4
    other_z = cent_of(1 - zhi, y, k)
    ZN, XM, XP, ZXM, ZXP = 1, 2, 3, 4, 5
    group = {
        ZN: (x * 2 + 1 - zlo, other_z),
        XM: (xm * 2 + zlo, c),
        XP: (xp * 2 + zlo, c),
        ZXM: (xm * 2 + 1 - zlo, other_z),
        ZXP: (xp * 2 + 1 - zlo, other_z),
    }
    inverse = {ZN: ZN, XM: XP, XP: XM, ZXM: ZXP, ZXP: ZXM}
    sibling = (d, cent_of(zhi, y, 1 - k))
    up = (d, cent_of(zhi, yp, k))
    down = (d, cent_of(zhi, ym, k))
    y_of = (y, ym, yp, y2)

    def owner(t, ra, rb):
        a, b = (x // 2 + ra) % 2, (zlo + rb) % 2
        return 4 * t + 2 * a + b, ((2 * a + q) * 2 + b, cent_of(zhi, y_of[t], k))

    owners = [(t, ra, rb) for t in (3, 2, 1, 0) for ra in (1, 0) for rb in (1, 0) if (t, ra, rb) != (0, 0, 0)]

    def row_peer(r):
        return ((d + r) % DP, c)

    def rcopy(src, dst, ss, rs, dev):
        return pltpu.make_async_remote_copy(
            src_ref=src, dst_ref=dst, send_sem=ss, recv_sem=rs, device_id=dev, device_id_type=MESH
        )

    load_a = pltpu.make_async_copy(a_hbm, a_v, in_sem.at[0])
    load_label = pltpu.make_async_copy(label_hbm, label_v, in_sem.at[1])
    e_copies = [
        pltpu.make_async_copy(
            e_hbm.at[:, pl.ds(pl.multiple_of(COLS * k + TILE * n, TILE), TILE)], e_v.at[n], e_sem.at[n]
        )
        for n in range(NTILE)
    ]
    def mine(a):
        return p_hbm.at[pl.ds(pl.multiple_of(2 * BLK * a + BLK * q, BLK), BLK)]

    def place_of(core, t, a=0, n=1):
        start = (EARLY + 256 * core if t == 3 else 768 * core + 256 * t) + BLK * a
        return par.at[pl.ds(start, BLK * n)]

    own_par = [pltpu.make_async_copy(mine(a), place_of(0, 0, a), p_sem.at[a]) for a in range(2)]
    load_a.start()
    e_copies[0].start()

    barrier = pltpu.get_barrier_semaphore()
    partners = [row_peer(r) for r in range(1, DP)] + [group[ZN], group[ZXM], group[ZXP], sibling]
    partners += [((d + r) % DP, cent_of(zhi, y, 1 - k)) for r in range(1, DP)]
    partners += [owner(*o)[1] for o in owners if o[0] != 0]
    for dev in partners:
        pl.semaphore_signal(barrier, inc=1, device_id=dev, device_id_type=MESH)

    e_copies[1].start()
    load_label.start()
    load_a.wait()

    a = a_v[...]
    run_id = lax.broadcasted_iota(jnp.int32, (32, 8, RUN), 1)
    upper = (
        lax.broadcasted_iota(jnp.int32, (RUN, RUN), 0) < lax.broadcasted_iota(jnp.int32, (RUN, RUN), 1)
    ).astype(F32).astype(BF16)
    ri = lax.broadcasted_iota(jnp.int32, (256, 256), 0)
    ci = lax.broadcasted_iota(jnp.int32, (256, 256), 1)
    before = (((ri & 7) == (ci & 7)) & (ci < ri)).astype(F32).astype(BF16)
    base = ((lax.broadcasted_iota(jnp.int32, (256, RUN), 0) & 7) * CAP + 1).astype(F32)
    for stage in range(2):
        rel = lax.shift_right_logical(a, 7) - cent_of(zhi, y, stage) * DP
        member = (rel[:, None, :] == run_id).astype(F32).reshape(256, RUN)
        member_b = member.astype(BF16)
        within = jnp.dot(member_b, upper, preferred_element_type=F32)
        earlier = jnp.dot(before, member_b, preferred_element_type=F32).astype(BF16)
        ahead = jnp.dot(earlier, jnp.ones((RUN, RUN), BF16), preferred_element_type=F32)
        slot = jnp.sum((member * (within + ahead + base)).reshape(32, 8, RUN), axis=1) - 1.0
        slot_v[stage] = slot.astype(jnp.int32)
    spot = ((a & (RUN - 1)) + 1).astype(F32)
    for b in range(ROWS // RUN):
        place[:, RUN * b : RUN * (b + 1)] = jnp.broadcast_to(spot[b : b + 1, :], (16, RUN)).astype(BF16)

    def par_copy(src, dst, idx, dev):
        return rcopy(src, dst, par_ss.at[idx], par_rs.at[idx], dev)

    to_up = [par_copy(mine(a), place_of(0, 1, a), a, up) for a in range(2)]
    to_down = [par_copy(mine(a), place_of(0, 2, a), 2 + a, down) for a in range(2)]
    on_up = par_copy(place_of(0, 1, 0), place_of(0, 3, 0), 4, up)
    on_down = par_copy(place_of(0, 2, 1), place_of(0, 3, 1), 5, down)
    to_sib = [par_copy(mine(a), place_of(1, 0, a), 6 + a, sibling) for a in range(2)]
    sib_early = [par_copy(place_of(0, t, 0, 2), place_of(1, t, 0, 2), 7 + t, sibling) for t in (1, 2)]
    sib_late = [par_copy(place_of(0, 3, a), place_of(1, 3, a), 10 + a, sibling) for a in range(2)]

    def build(stage):
        def block(b, carry):
            cols = pl.ds(pl.multiple_of(b * RUN, RUN), RUN)
            line = slot_v[stage, pl.ds(b, 1), :]
            oht[stage, :, cols] = (lax.broadcasted_iota(jnp.int32, (SLOTS, RUN), 0) == line).astype(F32).astype(BF16)
            return carry

        lax.fori_loop(0, ROWS // RUN, block, 0)

    build(0)

    for cp in e_copies[2:]:
        cp.start()
    pl.semaphore_wait(barrier, len(partners))
    for cp in (to_up[0], to_down[1], to_up[1], to_down[0]):
        cp.start()

    def there(start, size):
        return pl.ds(pl.multiple_of(COLS * k + start, TILE), size)

    def row_copy(r, stage, g):
        start, size = RANGES[g]
        to = (d + r) % DP
        return rcopy(
            send.at[stage, to, :, pl.ds(start, size)],
            recv.at[d, :, there(start, size)],
            row_ss.at[stage],
            row_rs,
            (to, cent_of(zhi, y, stage)),
        )

    peers = pl.ds(0, DP - 1)
    rows_in = rcopy(recv.at[peers], recv.at[peers], row_ss.at[0], row_rs, row_peer(1))
    rows_out = [rcopy(send.at[i, peers], send.at[i, peers], row_ss.at[i], row_rs, row_peer(1)) for i in range(2)]
    rows_sib = rcopy(send.at[1 - k, d], recv.at[d, :, there(0, COLS)], sib_ss, sib_rs, sibling)
    id_total = rcopy(id_send.at[peers], id_recv.at[peers], id_ss, id_rs, row_peer(1))

    for stage in range(2):
        for n in range(NTILE):
            if stage == 0:
                e_copies[n].wait()
            part = jnp.dot(oht[stage], e_v[n], preferred_element_type=F32)
            send[stage, :, :, TILE * n : TILE * (n + 1)] = part.astype(BF16).reshape(DP, CAP, TILE)
            if n in SEND_AFTER:
                for r in FAR_FIRST:
                    row_copy(r, stage, SEND_AFTER.index(n)).start()
        if stage == 0:
            for cp in (*own_par, *to_sib):
                cp.start()
            build(1)
            spots = lax.dot_general(place[...], oht[k], (((1,), (1,)), ((), ())), preferred_element_type=F32)[:8]
            lane = lax.broadcasted_iota(jnp.int32, (DP, SLOTS), 1)
            mine_at = jnp.where(lane // CAP == lax.broadcasted_iota(jnp.int32, (DP, SLOTS), 0), spots, 0.0).astype(BF16)
            lo = lax.broadcasted_iota(jnp.int32, (SLOTS, SLOTS), 0)
            hi = lax.broadcasted_iota(jnp.int32, (SLOTS, SLOTS), 1)
            shift = ((lo % CAP == hi % CAP) & (hi // CAP == d)).astype(F32).astype(BF16)
            moved = jnp.dot(mine_at, shift, preferred_element_type=F32)
            for i in range(DP):
                id_send[i] = moved[i : i + 1, :]
            for r in FAR_FIRST:
                dev = row_peer(r)
                rcopy(id_send.at[dev[0]], id_recv.at[d], id_ss, id_rs, dev).start()
    rows_sib.start()
    recv[d, :, there(0, COLS)] = send[k, d]
    id_recv[d] = id_send[d]
    ms[...] = jnp.zeros_like(ms)
    to_up[0].wait_recv()
    on_up.start()
    to_down[1].wait_recv()
    on_down.start()

    id_total.wait_recv()
    ids = jnp.sum(id_recv[...], axis=0).astype(jnp.int32) - 1
    onehot = (lax.broadcasted_iota(jnp.int32, (RUN, SLOTS), 0) == ids).astype(F32)
    counts_col = jnp.sum(onehot, axis=1, keepdims=True)
    onehot = onehot.astype(BF16)
    counts_row = lax.dot_general(jnp.ones((16, SLOTS), BF16), onehot, (((1,), (1,)), ((), ())), preferred_element_type=F32)[:1]
    rows_in.wait_recv()
    rows_sib.wait_recv()
    sums = jnp.dot(onehot, recv[...].reshape(SLOTS, W), preferred_element_type=F32)
    mean = sums / jnp.maximum(counts_col, 1.0)
    scale = jnp.sqrt(jnp.sum(mean * mean, axis=1, keepdims=True) + 1e-06)
    normed = (mean / scale).astype(BF16)
    cb[0] = normed
    cent_out = pltpu.make_async_copy(cb.at[0], cent_hbm, o_sem.at[0])
    cent_out.start()
    load_label.wait()
    meta[0, 0:1, :] = counts_row.astype(BF16).astype(F32)
    meta[0, 1:2, :] = label_v[...].astype(F32)
    meta[0, 2:8, :] = jnp.zeros((6, RUN), F32)

    def cent_copy(src, dst, start, size, idx, dev):
        rows = pl.ds(start, size)
        return rcopy(cb.at[src, rows], cb.at[dst, rows], cb_ss.at[idx], cb_rs.at[idx], dev)

    over_z = [cent_copy(0, 2, 32 * i, 32, i, group[ZN]) for i in range(4)]
    over_x = [cent_copy(0, 1, 64 * h, 64, 4 + h, group[(XP, XM)[h]]) for h in range(2)]
    pass_on = [cent_copy(2, 3, 32 * i, 32, 6 + i, group[(XP, XM)[i // 2]]) for i in range(4)]
    over_z[PIECES[0]].start()
    for cp in over_x:
        cp.start()
    for i in PIECES[1:]:
        over_z[i].start()
    metas = {p: rcopy(meta.at[0], meta.at[inverse[p]], meta_ss.at[p], meta_rs.at[inverse[p]], group[p]) for p in group}
    for p in (ZXM, ZXP, ZN, XM, XP):
        metas[p].start()

    def arrived(p):
        return rcopy(meta.at[0], meta.at[p], meta_ss.at[p], meta_rs.at[p], group[p])

    for cp in (*rows_out, rows_sib):
        cp.wait_send()
    id_total.wait_send()
    to_up[1].wait_recv()
    sib_early[0].start()
    to_down[0].wait_recv()
    sib_early[1].start()
    for i in PIECES:
        over_z[i].wait_recv()
        pass_on[i].start()
    for cp in own_par:
        cp.wait()
    for cp in (*to_sib, *over_x, *sib_early):
        cp.wait_recv()
    for p in group:
        arrived(p).wait_recv()

    low_lanes = lax.broadcasted_iota(jnp.int32, (1, RUN), 1) < RUN // 2

    def halves(low, high):
        return jnp.where(low_lanes, low, high)

    def meta_line(i):
        return [
            meta[0, i : i + 1, :],
            halves(meta[XM, i : i + 1, :], meta[XP, i : i + 1, :]),
            meta[ZN, i : i + 1, :],
            halves(meta[ZXM, i : i + 1, :], meta[ZXP, i : i + 1, :]),
        ]

    weights, labels = meta_line(0), meta_line(1)

    firsts = [
        cent_of(zhi, y_of[t], core) * SLAB + 2 * BLK * a + BLK * q
        for times in ((0, 1, 2), (3,))
        for core in (k, 1 - k)
        for t in times
        for a in range(2)
    ]

    def score(pair, size, first_step, steps):
        cols = slice(2 * RUN * pair, 2 * RUN * (pair + 1))
        label = jnp.concatenate([labels[2 * pair], labels[2 * pair + 1]], axis=1).astype(jnp.int32)
        per = size // BLK

        def step(i, carry):
            rows = pl.ds(pl.multiple_of(i * size, size), size)
            block = cb[2 * pair : 2 * pair + 2].reshape(2 * RUN, W)
            s = lax.dot_general(par[rows, :], block, (((1,), (1,)), ((), ())), preferred_element_type=F32)
            line = lax.broadcasted_iota(jnp.int32, (BLK, 2 * RUN), 0)
            parts = []
            for b in range(per):
                first = firsts[per * first_step + b]
                for other in range(first_step + 1, first_step + steps):
                    first = jnp.where(i == other, firsts[per * other + b], first)
                bonus = jnp.where(line == label - first, REWARD, 0.0)
                parts.append(s[BLK * b : BLK * (b + 1)] * INV_SOFT + bonus)
            s = jnp.concatenate(parts, axis=0)
            top = jnp.max(s, axis=0, keepdims=True)
            e = jnp.exp(s - top)
            scores[rows, cols] = e
            total = jnp.sum(e, axis=0, keepdims=True)
            for h in range(size // MCH):
                at = pl.ds(i * (size // MCH) + h, 1)
                mch[at, cols] = top
                sch[at, cols] = total if h == 0 else jnp.zeros_like(total)
            return carry

        lax.fori_loop(first_step, first_step + steps, step, 0)

    score(0, 2 * MCH, 0, 1)
    score(0, MCH, 2, 1)
    on_up.wait_recv()
    sib_late[0].start()
    on_down.wait_recv()
    sib_late[1].start()
    for cp in pass_on:
        cp.wait_recv()
    score(1, 2 * MCH, 0, 1)
    score(1, MCH, 2, 1)
    for cp in (*to_up, *to_down, *to_sib, *sib_early, *metas.values(), *over_x):
        cp.wait_send()
    cent_out.wait()
    for cp in sib_late:
        cp.wait_recv()
    score(0, MCH, 3, 1)
    score(1, MCH, 3, 1)

    m_loc = jnp.max(mch[...], axis=0, keepdims=True)
    s_loc = jnp.sum(sch[...] * jnp.exp(mch[...] - m_loc), axis=0, keepdims=True)
    for j in range(4):
        stat[0, j : j + 1, :] = m_loc[:, RUN * j : RUN * (j + 1)]
        stat[0, 4 + j : 5 + j, :] = s_loc[:, RUN * j : RUN * (j + 1)]
    stats = {p: rcopy(stat.at[0], stat.at[inverse[p]], stat_ss.at[p], stat_rs.at[inverse[p]], group[p]) for p in group}
    for p in (ZXM, ZXP, ZN, XM, XP):
        stats[p].start()
    for cp in (*over_z, *pass_on, on_up, on_down, *sib_late):
        cp.wait_send()
    for p in group:
        rcopy(stat.at[0], stat.at[p], stat_ss.at[p], stat_rs.at[p], group[p]).wait_recv()
    elsewhere = (
        (((XP, 1), (XM, 1)), ((ZN, 2), (ZN, 2)), ((ZXP, 3), (ZXM, 3))),
        (((XM, 0), (XP, 0)), ((ZXM, 2), (ZXP, 2)), ((ZN, 3), (ZN, 3))),
        (((ZN, 0), (ZN, 0)), ((XP, 3), (XM, 3)), ((ZXP, 1), (ZXM, 1))),
        (((ZXM, 0), (ZXP, 0)), ((XM, 2), (XP, 2)), ((ZN, 1), (ZN, 1))),
    )
    for j in range(4):

        def line(at, i):
            return stat[at[0], i + at[1] : i + at[1] + 1, :]

        m = [stat[0, j : j + 1, :]] + [halves(line(lo, 0), line(hi, 0)) for lo, hi in elsewhere[j]]
        s = [stat[0, 4 + j : 5 + j, :]] + [halves(line(lo, 4), line(hi, 4)) for lo, hi in elsewhere[j]]
        top = jnp.maximum(jnp.maximum(m[0], m[1]), jnp.maximum(m[2], m[3]))
        total = sum(s[i] * jnp.exp(m[i] - top) for i in range(4))
        log_total = top + jnp.log(total)
        if j == 0:
            logt_v[...] = log_total
            logt_out = pltpu.make_async_copy(logt_v, logt_hbm, o_sem.at[1])
            logt_out.start()
        cols = slice(RUN * j, RUN * (j + 1))
        fac[:, cols] = weights[j] * jnp.exp(mch[:, cols] - log_total)

    def mass_step(i, carry):
        f = fac[pl.ds(i, 1), :]
        rows = pl.ds(pl.multiple_of(i * MCH, MCH), MCH)
        acc = jnp.zeros((MCH, RUN), F32)
        for j in range(4):
            cols = slice(RUN * j, RUN * (j + 1))
            acc = acc + scores[rows, cols] * f[:, cols]
        terms[i] = jnp.sum(acc.T, axis=0, keepdims=True)
        return carry

    lax.fori_loop(0, 4, mass_step, 0)
    mp[0, :, 0:512] = terms[0]
    mp[0, :, 512:768] = terms[1][:, :256]
    mp[0, :, 768:1024] = terms[3][:, :256]
    mp[1, :, 0:256] = terms[1][:, 256:]
    mp[1, :, 256:768] = terms[2]
    mp[1, :, 768:1024] = terms[3][:, 256:]

    to_sib_mass = rcopy(mp.at[1], sib_in, m1_ss, m1_rs, sibling)
    to_sib_mass.start()
    to_sib_mass.wait_recv()
    both = mp[0] + sib_in[...]
    for i in range(2 * DP):
        ms[i, :, :PART] = both[:, PART * i : PART * (i + 1)]

    for i, o in enumerate(owners):
        at, dev = owner(*o)
        rcopy(ms.at[at], mr.at[i], m2_ss, m2_rs, dev).start()
    own_mass = pltpu.make_async_copy(ms.at[owner(0, 0, 0)[0]], mr.at[2 * DP - 1], o_sem.at[2])
    own_mass.start()
    for cp in [to_sib_mass, *stats.values()]:
        cp.wait_send()
    logt_out.wait()
    own_mass.wait()
    lines = pl.ds(0, 2 * DP - 1)
    rcopy(ms.at[lines], mr.at[lines], m2_ss, m2_rs, row_peer(1)).wait()


def hand_on(cent, logt, terms, cent_out, logt_out, mass_out):
    cent_out[...] = cent[...]
    logt_out[...] = logt[...]
    mass_out[...] = jnp.sum(terms[...], axis=0)[:, :PART]


def per_device(embeddings, assignments, parents, starting_coarse_label):
    vmem = pl.BlockSpec(memory_space=pltpu.VMEM)
    hbm = pl.BlockSpec(memory_space=pltpu.HBM)
    anywhere = pl.BlockSpec(memory_space=pl.ANY)
    dma = pltpu.SemaphoreType.DMA
    operands = (assignments.reshape(32, RUN), starting_coarse_label.reshape(1, RUN), embeddings, parents)
    cent, logt, terms = pl.pallas_call(
        kernel,
        out_shape=(
            jax.ShapeDtypeStruct((RUN, W), BF16),
            jax.ShapeDtypeStruct((1, RUN), F32),
            jax.ShapeDtypeStruct((2 * DP, 1, RUN), F32),
        ),
        in_specs=[hbm, hbm, hbm, hbm],
        out_specs=(anywhere, anywhere, anywhere),
        scratch_shapes=[
            pltpu.VMEM((32, RUN), jnp.int32),
            pltpu.VMEM((1, RUN), jnp.int32),
            pltpu.VMEM((NTILE, ROWS, TILE), BF16),
            pltpu.VMEM((2, SLOTS, ROWS), BF16),
            pltpu.VMEM((16, ROWS), BF16),
            pltpu.VMEM((2, 32, RUN), jnp.int32),
            pltpu.VMEM((2, DP, CAP, COLS), BF16),
            pltpu.VMEM((DP, CAP, W), BF16),
            pltpu.VMEM((DP, 1, SLOTS), F32),
            pltpu.VMEM((DP, 1, SLOTS), F32),
            pltpu.VMEM((EARLY + LATE, W), BF16),
            pltpu.VMEM((4, RUN, W), BF16),
            pltpu.VMEM((6, 8, RUN), F32),
            pltpu.VMEM((EARLY + LATE, 4 * RUN), F32),
            pltpu.VMEM((4, 4 * RUN), F32),
            pltpu.VMEM((4, 4 * RUN), F32),
            pltpu.VMEM((6, 8, RUN), F32),
            pltpu.VMEM((4, 4 * RUN), F32),
            pltpu.VMEM((4, 1, MCH), F32),
            pltpu.VMEM((2, 1, 1024), F32),
            pltpu.VMEM((1, 1024), F32),
            pltpu.VMEM((2 * DP, 1, RUN), F32),
            pltpu.VMEM((1, RUN), F32),
            dma((NTILE,)),
            dma((2,)),
            dma((2,)),
            dma,
            dma,
            dma,
            dma,
            dma,
            dma((12,)),
            dma((12,)),
            dma((10,)),
            dma((10,)),
            dma((6,)),
            dma((6,)),
            dma((6,)),
            dma((6,)),
            dma,
            dma,
            dma,
            dma,
            dma((3,)),
            dma((2,)),
        ],
        compiler_params=pltpu.CompilerParams(collective_id=0, has_side_effects=True, vmem_limit_bytes=52 << 20),
        name="handover",
    )(
        *(pltpu.with_memory_space_constraint(v, pltpu.HBM) for v in operands),
    )
    cent, logt, mass = pl.pallas_call(
        hand_on,
        out_shape=(
            jax.ShapeDtypeStruct((RUN, W), BF16),
            jax.ShapeDtypeStruct((1, RUN), F32),
            jax.ShapeDtypeStruct((1, PART), F32),
        ),
        in_specs=[vmem, vmem, vmem],
        out_specs=(vmem, vmem, vmem),
        compiler_params=pltpu.CompilerParams(vmem_limit_bytes=2 << 20),
        name="finish",
    )(cent, logt, terms)
    return cent, logt.reshape(RUN), mass.reshape(PART)


def solution(mesh):
    return jax.shard_map(
        per_device,
        mesh=mesh,
        in_specs=(P("dp", None), P("dp"), P("cent", None), P(("cent", "dp"))),
        out_specs=(P(("cent", "dp"), None), P(("cent", "dp")), P(("cent", "dp"))),
        check_vma=False,
    )
```

```python
import jax
import jax.numpy as jnp
from jax import lax
from jax.experimental import pallas as pl
from jax.experimental.pallas import tpu as pltpu
from jax.sharding import PartitionSpec as P

MESH = pl.DeviceIdType.MESH
F32 = jnp.float32
BF16 = jnp.bfloat16

W = 1536
RUN = 128
CAP = 48
DP = 8
SLOTS = DP * CAP
TILE = 256
COLS = W // 2
NTILE = COLS // TILE
ROWS = 4096
SLAB = 512
PART = 64
EARLY, LATE = 1536, 512
BLK = 128
MCH = 512
PIECES = (0, 2, 1, 3)
INV_SOFT = 1.0 / 0.5
REWARD = 1.5

RANGES = ((0, 256), (256, 512))
SEND_AFTER = (0, 2)
FAR_FIRST = (5, 3, 4, 6, 2, 7, 1)


def kernel(
    a_hbm, label_hbm, e_hbm, p_hbm,
    cent_hbm, logt_hbm, mr,
    a_v, label_v, e_v, oht, place, slot_v, send, recv, id_send, id_recv, par, cb, meta, scores, mch, sch, stat, fac, terms, mp, sib_in, ms, logt_v,
    e_sem, p_sem, row_ss, row_rs, sib_ss, sib_rs, id_ss, id_rs, par_ss, par_rs, cb_ss, cb_rs, meta_ss, meta_rs, stat_ss, stat_rs,
    m1_ss, m1_rs, m2_ss, m2_rs, o_sem, in_sem,
):
    d = lax.axis_index("dp")
    c = lax.axis_index("cent")
    zlo = d % 2
    zhi = c // 8
    y = (c // 2) % 4
    k = c % 2

    def cent_of(zh, yy, kk):
        return zh * 8 + yy * 2 + kk

    yp, ym, y2 = (y + 1) % 4, (y + 3) % 4, (y + 2) % 4
    x = d // 2
    q = x % 2
    xp, xm = (x + 1) % 4, (x + 3) % 4
    other_z = cent_of(1 - zhi, y, k)
    ZN, XM, XP, ZXM, ZXP = 1, 2, 3, 4, 5
    group = {
        ZN: (x * 2 + 1 - zlo, other_z),
        XM: (xm * 2 + zlo, c),
        XP: (xp * 2 + zlo, c),
        ZXM: (xm * 2 + 1 - zlo, other_z),
        ZXP: (xp * 2 + 1 - zlo, other_z),
    }
    inverse = {ZN: ZN, XM: XP, XP: XM, ZXM: ZXP, ZXP: ZXM}
    sibling = (d, cent_of(zhi, y, 1 - k))
    up = (d, cent_of(zhi, yp, k))
    down = (d, cent_of(zhi, ym, k))
    y_of = (y, ym, yp, y2)

    def owner(t, ra, rb):
        a, b = (x // 2 + ra) % 2, (zlo + rb) % 2
        return 4 * t + 2 * a + b, ((2 * a + q) * 2 + b, cent_of(zhi, y_of[t], k))

    owners = [(t, ra, rb) for t in (3, 2, 1, 0) for ra in (1, 0) for rb in (1, 0) if (t, ra, rb) != (0, 0, 0)]

    def row_peer(r):
        return ((d + r) % DP, c)

    def rcopy(src, dst, ss, rs, dev):
        return pltpu.make_async_remote_copy(
            src_ref=src, dst_ref=dst, send_sem=ss, recv_sem=rs, device_id=dev, device_id_type=MESH
        )

    load_a = pltpu.make_async_copy(a_hbm, a_v, in_sem.at[0])
    load_label = pltpu.make_async_copy(label_hbm, label_v, in_sem.at[1])
    e_copies = [
        pltpu.make_async_copy(
            e_hbm.at[:, pl.ds(pl.multiple_of(COLS * k + TILE * n, TILE), TILE)], e_v.at[n], e_sem.at[n]
        )
        for n in range(NTILE)
    ]
    def mine(a):
        return p_hbm.at[pl.ds(pl.multiple_of(2 * BLK * a + BLK * q, BLK), BLK)]

    def place_of(core, t, a=0, n=1):
        start = (EARLY + 256 * core if t == 3 else 768 * core + 256 * t) + BLK * a
        return par.at[pl.ds(start, BLK * n)]

    own_par = [pltpu.make_async_copy(mine(a), place_of(0, 0, a), p_sem.at[a]) for a in range(2)]
    load_a.start()
    e_copies[0].start()

    barrier = pltpu.get_barrier_semaphore()
    partners = [row_peer(r) for r in range(1, DP)] + [group[ZN], group[ZXM], group[ZXP], sibling]
    partners += [((d + r) % DP, cent_of(zhi, y, 1 - k)) for r in range(1, DP)]
    partners += [owner(*o)[1] for o in owners if o[0] != 0]
    for dev in partners:
        pl.semaphore_signal(barrier, inc=1, device_id=dev, device_id_type=MESH)

    e_copies[1].start()
    load_label.start()
    load_a.wait()

    a = a_v[...]
    run_id = lax.broadcasted_iota(jnp.int32, (32, 8, RUN), 1)
    upper = (
        lax.broadcasted_iota(jnp.int32, (RUN, RUN), 0) < lax.broadcasted_iota(jnp.int32, (RUN, RUN), 1)
    ).astype(F32).astype(BF16)
    ri = lax.broadcasted_iota(jnp.int32, (256, 256), 0)
    ci = lax.broadcasted_iota(jnp.int32, (256, 256), 1)
    before = (((ri & 7) == (ci & 7)) & (ci < ri)).astype(F32).astype(BF16)
    base = ((lax.broadcasted_iota(jnp.int32, (256, RUN), 0) & 7) * CAP + 1).astype(F32)
    def find_slots(stage):
        rel = lax.shift_right_logical(a, 7) - cent_of(zhi, y, stage) * DP
        member = (rel[:, None, :] == run_id).astype(F32).reshape(256, RUN)
        member_b = member.astype(BF16)
        within = jnp.dot(member_b, upper, preferred_element_type=F32)
        earlier = jnp.dot(before, member_b, preferred_element_type=F32).astype(BF16)
        ahead = jnp.dot(earlier, jnp.ones((RUN, RUN), BF16), preferred_element_type=F32)
        slot = jnp.sum((member * (within + ahead + base)).reshape(32, 8, RUN), axis=1) - 1.0
        slot_v[stage] = slot.astype(jnp.int32)

    find_slots(0)

    def par_copy(src, dst, idx, dev):
        return rcopy(src, dst, par_ss.at[idx], par_rs.at[idx], dev)

    to_up = [par_copy(mine(a), place_of(0, 1, a), a, up) for a in range(2)]
    to_down = [par_copy(mine(a), place_of(0, 2, a), 2 + a, down) for a in range(2)]
    on_up = par_copy(place_of(0, 1, 0), place_of(0, 3, 0), 4, up)
    on_down = par_copy(place_of(0, 2, 1), place_of(0, 3, 1), 5, down)
    to_sib = [par_copy(mine(a), place_of(1, 0, a), 6 + a, sibling) for a in range(2)]
    sib_early = [par_copy(place_of(0, t, 0, 2), place_of(1, t, 0, 2), 7 + t, sibling) for t in (1, 2)]
    sib_late = [par_copy(place_of(0, 3, a), place_of(1, 3, a), 10 + a, sibling) for a in range(2)]

    def build(stage):
        def block(b, carry):
            cols = pl.ds(pl.multiple_of(b * RUN, RUN), RUN)
            line = slot_v[stage, pl.ds(b, 1), :]
            oht[stage, :, cols] = (lax.broadcasted_iota(jnp.int32, (SLOTS, RUN), 0) == line).astype(F32).astype(BF16)
            return carry

        lax.fori_loop(0, ROWS // RUN, block, 0)

    pl.semaphore_wait(barrier, len(partners))
    for cp in (to_up[0], to_down[1], to_up[1], to_down[0]):
        cp.start()
    build(0)

    for cp in e_copies[2:]:
        cp.start()

    def there(start, size):
        return pl.ds(pl.multiple_of(COLS * k + start, TILE), size)

    def row_copy(r, stage, g):
        start, size = RANGES[g]
        to = (d + r) % DP
        return rcopy(
            send.at[stage, to, :, pl.ds(start, size)],
            recv.at[d, :, there(start, size)],
            row_ss.at[stage],
            row_rs,
            (to, cent_of(zhi, y, stage)),
        )

    peers = pl.ds(0, DP - 1)
    rows_in = rcopy(recv.at[peers], recv.at[peers], row_ss.at[0], row_rs, row_peer(1))
    rows_out = [rcopy(send.at[i, peers], send.at[i, peers], row_ss.at[i], row_rs, row_peer(1)) for i in range(2)]
    rows_sib = rcopy(send.at[1 - k, d], recv.at[d, :, there(0, COLS)], sib_ss, sib_rs, sibling)
    id_total = rcopy(id_send.at[peers], id_recv.at[peers], id_ss, id_rs, row_peer(1))

    for stage in range(2):
        for n in range(NTILE):
            if stage == 0:
                e_copies[n].wait()
            part = jnp.dot(oht[stage], e_v[n], preferred_element_type=F32)
            send[stage, :, :, TILE * n : TILE * (n + 1)] = part.astype(BF16).reshape(DP, CAP, TILE)
            if n in SEND_AFTER:
                for r in FAR_FIRST:
                    row_copy(r, stage, SEND_AFTER.index(n)).start()
        if stage == 0:
            for cp in (*own_par, *to_sib):
                cp.start()
            find_slots(1)
            build(1)
            spot = ((a & (RUN - 1)) + 1).astype(F32)
            for b in range(ROWS // RUN):
                place[:, RUN * b : RUN * (b + 1)] = jnp.broadcast_to(spot[b : b + 1, :], (16, RUN)).astype(BF16)
            spots = lax.dot_general(place[...], oht[k], (((1,), (1,)), ((), ())), preferred_element_type=F32)[:8]
            lane = lax.broadcasted_iota(jnp.int32, (DP, SLOTS), 1)
            mine_at = jnp.where(lane // CAP == lax.broadcasted_iota(jnp.int32, (DP, SLOTS), 0), spots, 0.0).astype(BF16)
            lo = lax.broadcasted_iota(jnp.int32, (SLOTS, SLOTS), 0)
            hi = lax.broadcasted_iota(jnp.int32, (SLOTS, SLOTS), 1)
            shift = ((lo % CAP == hi % CAP) & (hi // CAP == d)).astype(F32).astype(BF16)
            moved = jnp.dot(mine_at, shift, preferred_element_type=F32)
            for i in range(DP):
                id_send[i] = moved[i : i + 1, :]
            for r in FAR_FIRST:
                dev = row_peer(r)
                rcopy(id_send.at[dev[0]], id_recv.at[d], id_ss, id_rs, dev).start()
    rows_sib.start()
    recv[d, :, there(0, COLS)] = send[k, d]
    id_recv[d] = id_send[d]
    ms[...] = jnp.zeros_like(ms)
    to_up[0].wait_recv()
    on_up.start()
    to_down[1].wait_recv()
    on_down.start()

    id_total.wait_recv()
    ids = jnp.sum(id_recv[...], axis=0).astype(jnp.int32) - 1
    onehot = (lax.broadcasted_iota(jnp.int32, (RUN, SLOTS), 0) == ids).astype(F32)
    counts_col = jnp.sum(onehot, axis=1, keepdims=True)
    onehot = onehot.astype(BF16)
    counts_row = lax.dot_general(jnp.ones((16, SLOTS), BF16), onehot, (((1,), (1,)), ((), ())), preferred_element_type=F32)[:1]
    rows_in.wait_recv()
    rows_sib.wait_recv()
    sums = jnp.dot(onehot, recv[...].reshape(SLOTS, W), preferred_element_type=F32)
    mean = sums / jnp.maximum(counts_col, 1.0)
    scale = jnp.sqrt(jnp.sum(mean * mean, axis=1, keepdims=True) + 1e-06)
    normed = (mean / scale).astype(BF16)
    cb[0] = normed
    cent_out = pltpu.make_async_copy(cb.at[0], cent_hbm, o_sem.at[0])
    cent_out.start()
    load_label.wait()
    meta[0, 0:1, :] = counts_row.astype(BF16).astype(F32)
    meta[0, 1:2, :] = label_v[...].astype(F32)
    meta[0, 2:8, :] = jnp.zeros((6, RUN), F32)

    def cent_copy(src, dst, start, size, idx, dev):
        rows = pl.ds(start, size)
        return rcopy(cb.at[src, rows], cb.at[dst, rows], cb_ss.at[idx], cb_rs.at[idx], dev)

    over_z = [cent_copy(0, 2, 32 * i, 32, i, group[ZN]) for i in range(4)]
    over_x = [cent_copy(0, 1, 64 * h, 64, 4 + h, group[(XP, XM)[h]]) for h in range(2)]
    pass_on = [cent_copy(2, 3, 32 * i, 32, 6 + i, group[(XP, XM)[i // 2]]) for i in range(4)]
    over_z[PIECES[0]].start()
    for cp in over_x:
        cp.start()
    for i in PIECES[1:]:
        over_z[i].start()
    metas = {p: rcopy(meta.at[0], meta.at[inverse[p]], meta_ss.at[p], meta_rs.at[inverse[p]], group[p]) for p in group}
    for p in (ZXM, ZXP, ZN, XM, XP):
        metas[p].start()

    def arrived(p):
        return rcopy(meta.at[0], meta.at[p], meta_ss.at[p], meta_rs.at[p], group[p])

    for cp in (*rows_out, rows_sib):
        cp.wait_send()
    id_total.wait_send()
    to_up[1].wait_recv()
    sib_early[0].start()
    to_down[0].wait_recv()
    sib_early[1].start()
    for i in PIECES:
        over_z[i].wait_recv()
        pass_on[i].start()
    for cp in own_par:
        cp.wait()
    for cp in (*to_sib, *over_x, *sib_early):
        cp.wait_recv()
    for p in group:
        arrived(p).wait_recv()

    low_lanes = lax.broadcasted_iota(jnp.int32, (1, RUN), 1) < RUN // 2

    def halves(low, high):
        return jnp.where(low_lanes, low, high)

    def meta_line(i):
        return [
            meta[0, i : i + 1, :],
            halves(meta[XM, i : i + 1, :], meta[XP, i : i + 1, :]),
            meta[ZN, i : i + 1, :],
            halves(meta[ZXM, i : i + 1, :], meta[ZXP, i : i + 1, :]),
        ]

    weights, labels = meta_line(0), meta_line(1)

    firsts = [
        cent_of(zhi, y_of[t], core) * SLAB + 2 * BLK * a + BLK * q
        for times in ((0, 1, 2), (3,))
        for core in (k, 1 - k)
        for t in times
        for a in range(2)
    ]

    def score(pair, size, first_step, steps):
        cols = slice(2 * RUN * pair, 2 * RUN * (pair + 1))
        label = jnp.concatenate([labels[2 * pair], labels[2 * pair + 1]], axis=1).astype(jnp.int32)
        per = size // BLK

        def step(i, carry):
            rows = pl.ds(pl.multiple_of(i * size, size), size)
            block = cb[2 * pair : 2 * pair + 2].reshape(2 * RUN, W)
            s = lax.dot_general(par[rows, :], block, (((1,), (1,)), ((), ())), preferred_element_type=F32)
            line = lax.broadcasted_iota(jnp.int32, (BLK, 2 * RUN), 0)
            parts = []
            for b in range(per):
                first = firsts[per * first_step + b]
                for other in range(first_step + 1, first_step + steps):
                    first = jnp.where(i == other, firsts[per * other + b], first)
                bonus = jnp.where(line == label - first, REWARD, 0.0)
                parts.append(s[BLK * b : BLK * (b + 1)] * INV_SOFT + bonus)
            s = jnp.concatenate(parts, axis=0)
            top = jnp.max(s, axis=0, keepdims=True)
            e = jnp.exp(s - top)
            scores[rows, cols] = e
            total = jnp.sum(e, axis=0, keepdims=True)
            for h in range(size // MCH):
                at = pl.ds(i * (size // MCH) + h, 1)
                mch[at, cols] = top
                sch[at, cols] = total if h == 0 else jnp.zeros_like(total)
            return carry

        lax.fori_loop(first_step, first_step + steps, step, 0)

    score(0, 2 * MCH, 0, 1)
    score(0, MCH, 2, 1)
    on_up.wait_recv()
    sib_late[0].start()
    on_down.wait_recv()
    sib_late[1].start()
    for cp in pass_on:
        cp.wait_recv()
    score(1, 2 * MCH, 0, 1)
    score(1, MCH, 2, 1)
    for cp in (*to_up, *to_down, *to_sib, *sib_early, *metas.values(), *over_x):
        cp.wait_send()
    cent_out.wait()
    for cp in sib_late:
        cp.wait_recv()
    score(0, MCH, 3, 1)
    score(1, MCH, 3, 1)

    m_loc = jnp.max(mch[...], axis=0, keepdims=True)
    s_loc = jnp.sum(sch[...] * jnp.exp(mch[...] - m_loc), axis=0, keepdims=True)
    for j in range(4):
        stat[0, j : j + 1, :] = m_loc[:, RUN * j : RUN * (j + 1)]
        stat[0, 4 + j : 5 + j, :] = s_loc[:, RUN * j : RUN * (j + 1)]
    stats = {p: rcopy(stat.at[0], stat.at[inverse[p]], stat_ss.at[p], stat_rs.at[inverse[p]], group[p]) for p in group}
    for p in (ZXM, ZXP, ZN, XM, XP):
        stats[p].start()
    for cp in (*over_z, *pass_on, on_up, on_down, *sib_late):
        cp.wait_send()
    for p in group:
        rcopy(stat.at[0], stat.at[p], stat_ss.at[p], stat_rs.at[p], group[p]).wait_recv()
    elsewhere = (
        (((XP, 1), (XM, 1)), ((ZN, 2), (ZN, 2)), ((ZXP, 3), (ZXM, 3))),
        (((XM, 0), (XP, 0)), ((ZXM, 2), (ZXP, 2)), ((ZN, 3), (ZN, 3))),
        (((ZN, 0), (ZN, 0)), ((XP, 3), (XM, 3)), ((ZXP, 1), (ZXM, 1))),
        (((ZXM, 0), (ZXP, 0)), ((XM, 2), (XP, 2)), ((ZN, 1), (ZN, 1))),
    )
    for j in range(4):

        def line(at, i):
            return stat[at[0], i + at[1] : i + at[1] + 1, :]

        m = [stat[0, j : j + 1, :]] + [halves(line(lo, 0), line(hi, 0)) for lo, hi in elsewhere[j]]
        s = [stat[0, 4 + j : 5 + j, :]] + [halves(line(lo, 4), line(hi, 4)) for lo, hi in elsewhere[j]]
        top = jnp.maximum(jnp.maximum(m[0], m[1]), jnp.maximum(m[2], m[3]))
        total = sum(s[i] * jnp.exp(m[i] - top) for i in range(4))
        log_total = top + jnp.log(total)
        if j == 0:
            logt_v[...] = log_total
            logt_out = pltpu.make_async_copy(logt_v, logt_hbm, o_sem.at[1])
            logt_out.start()
        cols = slice(RUN * j, RUN * (j + 1))
        fac[:, cols] = weights[j] * jnp.exp(mch[:, cols] - log_total)

    def mass_step(i, carry):
        f = fac[pl.ds(i, 1), :]
        rows = pl.ds(pl.multiple_of(i * MCH, MCH), MCH)
        acc = jnp.zeros((MCH, RUN), F32)
        for j in range(4):
            cols = slice(RUN * j, RUN * (j + 1))
            acc = acc + scores[rows, cols] * f[:, cols]
        terms[i] = jnp.sum(acc.T, axis=0, keepdims=True)
        return carry

    lax.fori_loop(0, 4, mass_step, 0)
    mp[0, :, 0:512] = terms[0]
    mp[0, :, 512:768] = terms[1][:, :256]
    mp[0, :, 768:1024] = terms[3][:, :256]
    mp[1, :, 0:256] = terms[1][:, 256:]
    mp[1, :, 256:768] = terms[2]
    mp[1, :, 768:1024] = terms[3][:, 256:]

    to_sib_mass = rcopy(mp.at[1], sib_in, m1_ss, m1_rs, sibling)
    to_sib_mass.start()
    to_sib_mass.wait_recv()
    both = mp[0] + sib_in[...]
    for i in range(2 * DP):
        ms[i, :, :PART] = both[:, PART * i : PART * (i + 1)]

    for i, o in enumerate(owners):
        at, dev = owner(*o)
        rcopy(ms.at[at], mr.at[i], m2_ss, m2_rs, dev).start()
    own_mass = pltpu.make_async_copy(ms.at[owner(0, 0, 0)[0]], mr.at[2 * DP - 1], o_sem.at[2])
    own_mass.start()
    for cp in [to_sib_mass, *stats.values()]:
        cp.wait_send()
    logt_out.wait()
    own_mass.wait()
    lines = pl.ds(0, 2 * DP - 1)
    rcopy(ms.at[lines], mr.at[lines], m2_ss, m2_rs, row_peer(1)).wait()


def hand_on(cent, logt, terms, cent_out, logt_out, mass_out):
    cent_out[...] = cent[...]
    logt_out[...] = logt[...]
    mass_out[...] = jnp.sum(terms[...], axis=0)[:, :PART]


def per_device(embeddings, assignments, parents, starting_coarse_label):
    vmem = pl.BlockSpec(memory_space=pltpu.VMEM)
    hbm = pl.BlockSpec(memory_space=pltpu.HBM)
    anywhere = pl.BlockSpec(memory_space=pl.ANY)
    dma = pltpu.SemaphoreType.DMA
    operands = (assignments.reshape(32, RUN), starting_coarse_label.reshape(1, RUN), embeddings, parents)
    cent, logt, terms = pl.pallas_call(
        kernel,
        out_shape=(
            jax.ShapeDtypeStruct((RUN, W), BF16),
            jax.ShapeDtypeStruct((1, RUN), F32),
            jax.ShapeDtypeStruct((2 * DP, 1, RUN), F32),
        ),
        in_specs=[hbm, hbm, hbm, hbm],
        out_specs=(anywhere, anywhere, anywhere),
        scratch_shapes=[
            pltpu.VMEM((32, RUN), jnp.int32),
            pltpu.VMEM((1, RUN), jnp.int32),
            pltpu.VMEM((NTILE, ROWS, TILE), BF16),
            pltpu.VMEM((2, SLOTS, ROWS), BF16),
            pltpu.VMEM((16, ROWS), BF16),
            pltpu.VMEM((2, 32, RUN), jnp.int32),
            pltpu.VMEM((2, DP, CAP, COLS), BF16),
            pltpu.VMEM((DP, CAP, W), BF16),
            pltpu.VMEM((DP, 1, SLOTS), F32),
            pltpu.VMEM((DP, 1, SLOTS), F32),
            pltpu.VMEM((EARLY + LATE, W), BF16),
            pltpu.VMEM((4, RUN, W), BF16),
            pltpu.VMEM((6, 8, RUN), F32),
            pltpu.VMEM((EARLY + LATE, 4 * RUN), F32),
            pltpu.VMEM((4, 4 * RUN), F32),
            pltpu.VMEM((4, 4 * RUN), F32),
            pltpu.VMEM((6, 8, RUN), F32),
            pltpu.VMEM((4, 4 * RUN), F32),
            pltpu.VMEM((4, 1, MCH), F32),
            pltpu.VMEM((2, 1, 1024), F32),
            pltpu.VMEM((1, 1024), F32),
            pltpu.VMEM((2 * DP, 1, RUN), F32),
            pltpu.VMEM((1, RUN), F32),
            dma((NTILE,)),
            dma((2,)),
            dma((2,)),
            dma,
            dma,
            dma,
            dma,
            dma,
            dma((12,)),
            dma((12,)),
            dma((10,)),
            dma((10,)),
            dma((6,)),
            dma((6,)),
            dma((6,)),
            dma((6,)),
            dma,
            dma,
            dma,
            dma,
            dma((3,)),
            dma((2,)),
        ],
        compiler_params=pltpu.CompilerParams(collective_id=0, has_side_effects=True, vmem_limit_bytes=52 << 20),
        name="handover",
    )(
        *(pltpu.with_memory_space_constraint(v, pltpu.HBM) for v in operands),
    )
    cent, logt, mass = pl.pallas_call(
        hand_on,
        out_shape=(
            jax.ShapeDtypeStruct((RUN, W), BF16),
            jax.ShapeDtypeStruct((1, RUN), F32),
            jax.ShapeDtypeStruct((1, PART), F32),
        ),
        in_specs=[vmem, vmem, vmem],
        out_specs=(vmem, vmem, vmem),
        compiler_params=pltpu.CompilerParams(vmem_limit_bytes=2 << 20),
        name="finish",
    )(cent, logt, terms)
    return cent, logt.reshape(RUN), mass.reshape(PART)


def solution(mesh):
    return jax.shard_map(
        per_device,
        mesh=mesh,
        in_specs=(P("dp", None), P("dp"), P("cent", None), P(("cent", "dp"))),
        out_specs=(P(("cent", "dp"), None), P(("cent", "dp")), P(("cent", "dp"))),
        check_vma=False,
    )
```

```python
import jax
import jax.numpy as jnp
from jax import lax
from jax.experimental import pallas as pl
from jax.experimental.pallas import tpu as pltpu
from jax.sharding import PartitionSpec as P

MESH = pl.DeviceIdType.MESH
F32 = jnp.float32
BF16 = jnp.bfloat16

W = 1536
RUN = 128
CAP = 48
DP = 8
SLOTS = DP * CAP
TILE = 256
COLS = W // 2
NTILE = COLS // TILE
ROWS = 4096
SLAB = 512
PART = 64
EARLY, LATE = 1536, 512
BLK = 128
MCH = 512
PIECES = (0, 2, 1, 3)
INV_SOFT = 1.0 / 0.5
REWARD = 1.5

RANGES = ((0, 256), (256, 512))
SEND_AFTER = (0, 2)
FAR_FIRST = (5, 3, 4, 6, 2, 7, 1)


def kernel(
    a_hbm, label_hbm, e_hbm, p_hbm,
    cent_hbm, logt_hbm, mr,
    a_v, label_v, e_v, oht, place, slot_v, send, recv, id_send, id_recv, par, cb, meta, scores, mch, sch, stat, fac, terms, mp, sib_in, ms, logt_v,
    e_sem, p_sem, row_ss, row_rs, sib_ss, sib_rs, id_ss, id_rs, par_ss, par_rs, cb_ss, cb_rs, meta_ss, meta_rs, stat_ss, stat_rs,
    m1_ss, m1_rs, m2_ss, m2_rs, o_sem, in_sem,
):
    d = lax.axis_index("dp")
    c = lax.axis_index("cent")
    zlo = d % 2
    zhi = c // 8
    y = (c // 2) % 4
    k = c % 2

    def cent_of(zh, yy, kk):
        return zh * 8 + yy * 2 + kk

    yp, ym, y2 = (y + 1) % 4, (y + 3) % 4, (y + 2) % 4
    x = d // 2
    q = x % 2
    xp, xm = (x + 1) % 4, (x + 3) % 4
    other_z = cent_of(1 - zhi, y, k)
    ZN, XM, XP, ZXM, ZXP = 1, 2, 3, 4, 5
    group = {
        ZN: (x * 2 + 1 - zlo, other_z),
        XM: (xm * 2 + zlo, c),
        XP: (xp * 2 + zlo, c),
        ZXM: (xm * 2 + 1 - zlo, other_z),
        ZXP: (xp * 2 + 1 - zlo, other_z),
    }
    inverse = {ZN: ZN, XM: XP, XP: XM, ZXM: ZXP, ZXP: ZXM}
    sibling = (d, cent_of(zhi, y, 1 - k))
    up = (d, cent_of(zhi, yp, k))
    down = (d, cent_of(zhi, ym, k))
    y_of = (y, ym, yp, y2)

    def owner(t, ra, rb):
        a, b = (x // 2 + ra) % 2, (zlo + rb) % 2
        return 4 * t + 2 * a + b, ((2 * a + q) * 2 + b, cent_of(zhi, y_of[t], k))

    owners = [(t, ra, rb) for t in (3, 2, 1, 0) for ra in (1, 0) for rb in (1, 0) if (t, ra, rb) != (0, 0, 0)]

    def row_peer(r):
        return ((d + r) % DP, c)

    def rcopy(src, dst, ss, rs, dev):
        return pltpu.make_async_remote_copy(
            src_ref=src, dst_ref=dst, send_sem=ss, recv_sem=rs, device_id=dev, device_id_type=MESH
        )

    load_a = pltpu.make_async_copy(a_hbm, a_v, in_sem.at[0])
    load_label = pltpu.make_async_copy(label_hbm, label_v, in_sem.at[1])
    e_copies = [
        pltpu.make_async_copy(
            e_hbm.at[:, pl.ds(pl.multiple_of(COLS * k + TILE * n, TILE), TILE)], e_v.at[n], e_sem.at[n]
        )
        for n in range(NTILE)
    ]
    def mine(a):
        return p_hbm.at[pl.ds(pl.multiple_of(2 * BLK * a + BLK * q, BLK), BLK)]

    def place_of(core, t, a=0, n=1):
        start = (EARLY + 256 * core if t == 3 else 768 * core + 256 * t) + BLK * a
        return par.at[pl.ds(start, BLK * n)]

    own_par = [pltpu.make_async_copy(mine(a), place_of(0, 0, a), p_sem.at[a]) for a in range(2)]
    load_a.start()
    e_copies[0].start()

    barrier = pltpu.get_barrier_semaphore()
    partners = [row_peer(r) for r in range(1, DP)] + [group[ZN], group[ZXM], group[ZXP], sibling]
    partners += [((d + r) % DP, cent_of(zhi, y, 1 - k)) for r in range(1, DP)]
    partners += [owner(*o)[1] for o in owners if o[0] != 0]
    for dev in partners:
        pl.semaphore_signal(barrier, inc=1, device_id=dev, device_id_type=MESH)

    e_copies[1].start()
    load_label.start()
    load_a.wait()

    a = a_v[...]
    run_id = lax.broadcasted_iota(jnp.int32, (32, 8, RUN), 1)
    upper = (
        lax.broadcasted_iota(jnp.int32, (RUN, RUN), 0) < lax.broadcasted_iota(jnp.int32, (RUN, RUN), 1)
    ).astype(F32).astype(BF16)
    ri = lax.broadcasted_iota(jnp.int32, (256, 256), 0)
    ci = lax.broadcasted_iota(jnp.int32, (256, 256), 1)
    before = (((ri & 7) == (ci & 7)) & (ci < ri)).astype(F32).astype(BF16)
    base = ((lax.broadcasted_iota(jnp.int32, (256, RUN), 0) & 7) * CAP + 1).astype(F32)
    for stage in range(2):
        rel = lax.shift_right_logical(a, 7) - cent_of(zhi, y, stage) * DP
        member = (rel[:, None, :] == run_id).astype(F32).reshape(256, RUN)
        member_b = member.astype(BF16)
        within = jnp.dot(member_b, upper, preferred_element_type=F32)
        earlier = jnp.dot(before, member_b, preferred_element_type=F32).astype(BF16)
        ahead = jnp.dot(earlier, jnp.ones((RUN, RUN), BF16), preferred_element_type=F32)
        slot = jnp.sum((member * (within + ahead + base)).reshape(32, 8, RUN), axis=1) - 1.0
        slot_v[stage] = slot.astype(jnp.int32)
    spot = ((a & (RUN - 1)) + 1).astype(F32)
    for b in range(ROWS // RUN):
        place[:, RUN * b : RUN * (b + 1)] = jnp.broadcast_to(spot[b : b + 1, :], (16, RUN)).astype(BF16)

    def par_copy(src, dst, idx, dev):
        return rcopy(src, dst, par_ss.at[idx], par_rs.at[idx], dev)

    to_up = [par_copy(mine(a), place_of(0, 1, a), a, up) for a in range(2)]
    to_down = [par_copy(mine(a), place_of(0, 2, a), 2 + a, down) for a in range(2)]
    on_up = par_copy(place_of(0, 1, 0), place_of(0, 3, 0), 4, up)
    on_down = par_copy(place_of(0, 2, 1), place_of(0, 3, 1), 5, down)
    to_sib = [par_copy(mine(a), place_of(1, 0, a), 6 + a, sibling) for a in range(2)]
    sib_early = [par_copy(place_of(0, t, 0, 2), place_of(1, t, 0, 2), 7 + t, sibling) for t in (1, 2)]
    sib_late = [par_copy(place_of(0, 3, a), place_of(1, 3, a), 10 + a, sibling) for a in range(2)]

    def build(stage):
        def block(b, carry):
            cols = pl.ds(pl.multiple_of(b * RUN, RUN), RUN)
            line = slot_v[stage, pl.ds(b, 1), :]
            oht[stage, :, cols] = (lax.broadcasted_iota(jnp.int32, (SLOTS, RUN), 0) == line).astype(F32).astype(BF16)
            return carry

        lax.fori_loop(0, ROWS // RUN, block, 0)

    build(0)

    for cp in e_copies[2:]:
        cp.start()
    pl.semaphore_wait(barrier, len(partners))
    for cp in (to_up[0], to_down[1], to_up[1], to_down[0]):
        cp.start()

    def there(start, size):
        return pl.ds(pl.multiple_of(COLS * k + start, TILE), size)

    def row_copy(r, stage, g):
        start, size = RANGES[g]
        to = (d + r) % DP
        return rcopy(
            send.at[stage, to, :, pl.ds(start, size)],
            recv.at[d, :, there(start, size)],
            row_ss.at[stage],
            row_rs,
            (to, cent_of(zhi, y, stage)),
        )

    peers = pl.ds(0, DP - 1)
    rows_in = rcopy(recv.at[peers], recv.at[peers], row_ss.at[0], row_rs, row_peer(1))
    rows_out = [rcopy(send.at[i, peers], send.at[i, peers], row_ss.at[i], row_rs, row_peer(1)) for i in range(2)]
    rows_sib = rcopy(send.at[1 - k, d], recv.at[d, :, there(0, COLS)], sib_ss, sib_rs, sibling)
    id_total = rcopy(id_send.at[peers], id_recv.at[peers], id_ss, id_rs, row_peer(1))

    for stage in range(2):
        for n in range(NTILE):
            if stage == 0:
                e_copies[n].wait()
            part = jnp.dot(oht[stage], e_v[n], preferred_element_type=F32)
            send[stage, :, :, TILE * n : TILE * (n + 1)] = part.astype(BF16).reshape(DP, CAP, TILE)
            if n in SEND_AFTER:
                for r in FAR_FIRST:
                    row_copy(r, stage, SEND_AFTER.index(n)).start()
        if stage == 0:
            for cp in (*own_par, *to_sib):
                cp.start()
            build(1)
            spots = lax.dot_general(place[...], oht[k], (((1,), (1,)), ((), ())), preferred_element_type=F32)[:8]
            lane = lax.broadcasted_iota(jnp.int32, (DP, SLOTS), 1)
            mine_at = jnp.where(lane // CAP == lax.broadcasted_iota(jnp.int32, (DP, SLOTS), 0), spots, 0.0).astype(BF16)
            lo = lax.broadcasted_iota(jnp.int32, (SLOTS, SLOTS), 0)
            hi = lax.broadcasted_iota(jnp.int32, (SLOTS, SLOTS), 1)
            shift = ((lo % CAP == hi % CAP) & (hi // CAP == d)).astype(F32).astype(BF16)
            moved = jnp.dot(mine_at, shift, preferred_element_type=F32)
            for i in range(DP):
                id_send[i] = moved[i : i + 1, :]
            for r in FAR_FIRST:
                dev = row_peer(r)
                rcopy(id_send.at[dev[0]], id_recv.at[d], id_ss, id_rs, dev).start()
    rows_sib.start()
    recv[d, :, there(0, COLS)] = send[k, d]
    id_recv[d] = id_send[d]
    ms[...] = jnp.zeros_like(ms)
    to_up[0].wait_recv()
    on_up.start()
    to_down[1].wait_recv()
    on_down.start()

    id_total.wait_recv()
    ids = jnp.sum(id_recv[...], axis=0).astype(jnp.int32) - 1
    onehot = (lax.broadcasted_iota(jnp.int32, (RUN, SLOTS), 0) == ids).astype(F32)
    counts_col = jnp.sum(onehot, axis=1, keepdims=True)
    onehot = onehot.astype(BF16)
    counts_row = lax.dot_general(jnp.ones((16, SLOTS), BF16), onehot, (((1,), (1,)), ((), ())), preferred_element_type=F32)[:1]
    rows_in.wait_recv()
    rows_sib.wait_recv()
    sums = jnp.dot(onehot, recv[...].reshape(SLOTS, W), preferred_element_type=F32)
    mean = sums / jnp.maximum(counts_col, 1.0)
    scale = jnp.sqrt(jnp.sum(mean * mean, axis=1, keepdims=True) + 1e-06)
    normed = (mean / scale).astype(BF16)
    cb[0] = normed
    cent_out = pltpu.make_async_copy(cb.at[0], cent_hbm, o_sem.at[0])
    cent_out.start()
    load_label.wait()
    meta[0, 0:1, :] = counts_row.astype(BF16).astype(F32)
    meta[0, 1:2, :] = label_v[...].astype(F32)
    meta[0, 2:8, :] = jnp.zeros((6, RUN), F32)

    def cent_copy(src, dst, start, size, idx, dev):
        rows = pl.ds(start, size)
        return rcopy(cb.at[src, rows], cb.at[dst, rows], cb_ss.at[idx], cb_rs.at[idx], dev)

    over_z = [cent_copy(0, 2, 32 * i, 32, i, group[ZN]) for i in range(4)]
    over_x = [cent_copy(0, 1, 64 * h, 64, 4 + h, group[(XP, XM)[h]]) for h in range(2)]
    pass_on = [cent_copy(2, 3, 32 * i, 32, 6 + i, group[(XP, XM)[i // 2]]) for i in range(4)]
    over_z[PIECES[0]].start()
    for cp in over_x:
        cp.start()
    for i in PIECES[1:]:
        over_z[i].start()
    metas = {p: rcopy(meta.at[0], meta.at[inverse[p]], meta_ss.at[p], meta_rs.at[inverse[p]], group[p]) for p in group}
    for p in (ZXM, ZXP, ZN, XM, XP):
        metas[p].start()

    def arrived(p):
        return rcopy(meta.at[0], meta.at[p], meta_ss.at[p], meta_rs.at[p], group[p])

    for cp in (*rows_out, rows_sib):
        cp.wait_send()
    id_total.wait_send()
    to_up[1].wait_recv()
    sib_early[0].start()
    to_down[0].wait_recv()
    sib_early[1].start()
    for i in PIECES:
        over_z[i].wait_recv()
        pass_on[i].start()
    for cp in own_par:
        cp.wait()
    for cp in (*to_sib, *over_x, *sib_early):
        cp.wait_recv()
    for p in group:
        arrived(p).wait_recv()

    low_lanes = lax.broadcasted_iota(jnp.int32, (1, RUN), 1) < RUN // 2

    def halves(low, high):
        return jnp.where(low_lanes, low, high)

    def meta_line(i):
        return [
            meta[0, i : i + 1, :],
            halves(meta[XM, i : i + 1, :], meta[XP, i : i + 1, :]),
            meta[ZN, i : i + 1, :],
            halves(meta[ZXM, i : i + 1, :], meta[ZXP, i : i + 1, :]),
        ]

    weights, labels = meta_line(0), meta_line(1)

    firsts = [
        cent_of(zhi, y_of[t], core) * SLAB + 2 * BLK * a + BLK * q
        for times in ((0, 1, 2), (3,))
        for core in (k, 1 - k)
        for t in times
        for a in range(2)
    ]

    def score(pair, size, first_step, steps):
        cols = slice(2 * RUN * pair, 2 * RUN * (pair + 1))
        label = jnp.concatenate([labels[2 * pair], labels[2 * pair + 1]], axis=1).astype(jnp.int32)
        per = size // BLK

        def step(i, carry):
            rows = pl.ds(pl.multiple_of(i * size, size), size)
            block = cb[2 * pair : 2 * pair + 2].reshape(2 * RUN, W)
            s = lax.dot_general(par[rows, :], block, (((1,), (1,)), ((), ())), preferred_element_type=F32)
            line = lax.broadcasted_iota(jnp.int32, (BLK, 2 * RUN), 0)
            parts = []
            for b in range(per):
                first = firsts[per * first_step + b]
                for other in range(first_step + 1, first_step + steps):
                    first = jnp.where(i == other, firsts[per * other + b], first)
                bonus = jnp.where(line == label - first, REWARD, 0.0)
                parts.append(s[BLK * b : BLK * (b + 1)] * INV_SOFT + bonus)
            s = jnp.concatenate(parts, axis=0)
            top = jnp.max(s, axis=0, keepdims=True)
            e = jnp.exp(s - top)
            scores[rows, cols] = e
            total = jnp.sum(e, axis=0, keepdims=True)
            for h in range(size // MCH):
                at = pl.ds(i * (size // MCH) + h, 1)
                mch[at, cols] = top
                sch[at, cols] = total if h == 0 else jnp.zeros_like(total)
            return carry

        lax.fori_loop(first_step, first_step + steps, step, 0)

    score(0, 2 * MCH, 0, 1)
    score(0, MCH, 2, 1)
    on_up.wait_recv()
    sib_late[0].start()
    on_down.wait_recv()
    sib_late[1].start()
    for cp in pass_on:
        cp.wait_recv()
    score(1, 2 * MCH, 0, 1)
    score(1, MCH, 2, 1)
    for cp in sib_late:
        cp.wait_recv()
    score(0, MCH, 3, 1)
    score(1, MCH, 3, 1)

    m_loc = jnp.max(mch[...], axis=0, keepdims=True)
    s_loc = jnp.sum(sch[...] * jnp.exp(mch[...] - m_loc), axis=0, keepdims=True)
    for j in range(4):
        stat[0, j : j + 1, :] = m_loc[:, RUN * j : RUN * (j + 1)]
        stat[0, 4 + j : 5 + j, :] = s_loc[:, RUN * j : RUN * (j + 1)]
    stats = {p: rcopy(stat.at[0], stat.at[inverse[p]], stat_ss.at[p], stat_rs.at[inverse[p]], group[p]) for p in group}
    for p in (ZXM, ZXP, ZN, XM, XP):
        stats[p].start()
    for cp in (*to_up, *to_down, *to_sib, *sib_early, *metas.values(), *over_x):
        cp.wait_send()
    cent_out.wait()
    for cp in (*over_z, *pass_on, on_up, on_down, *sib_late):
        cp.wait_send()
    for p in group:
        rcopy(stat.at[0], stat.at[p], stat_ss.at[p], stat_rs.at[p], group[p]).wait_recv()
    elsewhere = (
        (((XP, 1), (XM, 1)), ((ZN, 2), (ZN, 2)), ((ZXP, 3), (ZXM, 3))),
        (((XM, 0), (XP, 0)), ((ZXM, 2), (ZXP, 2)), ((ZN, 3), (ZN, 3))),
        (((ZN, 0), (ZN, 0)), ((XP, 3), (XM, 3)), ((ZXP, 1), (ZXM, 1))),
        (((ZXM, 0), (ZXP, 0)), ((XM, 2), (XP, 2)), ((ZN, 1), (ZN, 1))),
    )
    for j in range(4):

        def line(at, i):
            return stat[at[0], i + at[1] : i + at[1] + 1, :]

        m = [stat[0, j : j + 1, :]] + [halves(line(lo, 0), line(hi, 0)) for lo, hi in elsewhere[j]]
        s = [stat[0, 4 + j : 5 + j, :]] + [halves(line(lo, 4), line(hi, 4)) for lo, hi in elsewhere[j]]
        top = jnp.maximum(jnp.maximum(m[0], m[1]), jnp.maximum(m[2], m[3]))
        total = sum(s[i] * jnp.exp(m[i] - top) for i in range(4))
        log_total = top + jnp.log(total)
        if j == 0:
            logt_v[...] = log_total
            logt_out = pltpu.make_async_copy(logt_v, logt_hbm, o_sem.at[1])
            logt_out.start()
        cols = slice(RUN * j, RUN * (j + 1))
        fac[:, cols] = weights[j] * jnp.exp(mch[:, cols] - log_total)

    def mass_step(i, carry):
        f = fac[pl.ds(i, 1), :]
        rows = pl.ds(pl.multiple_of(i * MCH, MCH), MCH)
        acc = jnp.zeros((MCH, RUN), F32)
        for j in range(4):
            cols = slice(RUN * j, RUN * (j + 1))
            acc = acc + scores[rows, cols] * f[:, cols]
        terms[i] = jnp.sum(acc.T, axis=0, keepdims=True)
        return carry

    lax.fori_loop(0, 4, mass_step, 0)
    mp[0, :, 0:512] = terms[0]
    mp[0, :, 512:768] = terms[1][:, :256]
    mp[0, :, 768:1024] = terms[3][:, :256]
    mp[1, :, 0:256] = terms[1][:, 256:]
    mp[1, :, 256:768] = terms[2]
    mp[1, :, 768:1024] = terms[3][:, 256:]

    to_sib_mass = rcopy(mp.at[1], sib_in, m1_ss, m1_rs, sibling)
    to_sib_mass.start()
    to_sib_mass.wait_recv()
    both = mp[0] + sib_in[...]
    for i in range(2 * DP):
        ms[i, :, :PART] = both[:, PART * i : PART * (i + 1)]

    for i, o in enumerate(owners):
        at, dev = owner(*o)
        rcopy(ms.at[at], mr.at[i], m2_ss, m2_rs, dev).start()
    own_mass = pltpu.make_async_copy(ms.at[owner(0, 0, 0)[0]], mr.at[2 * DP - 1], o_sem.at[2])
    own_mass.start()
    for cp in [to_sib_mass, *stats.values()]:
        cp.wait_send()
    logt_out.wait()
    own_mass.wait()
    lines = pl.ds(0, 2 * DP - 1)
    rcopy(ms.at[lines], mr.at[lines], m2_ss, m2_rs, row_peer(1)).wait()


def hand_on(cent, logt, terms, cent_out, logt_out, mass_out):
    cent_out[...] = cent[...]
    logt_out[...] = logt[...]
    mass_out[...] = jnp.sum(terms[...], axis=0)[:, :PART]


def per_device(embeddings, assignments, parents, starting_coarse_label):
    vmem = pl.BlockSpec(memory_space=pltpu.VMEM)
    hbm = pl.BlockSpec(memory_space=pltpu.HBM)
    anywhere = pl.BlockSpec(memory_space=pl.ANY)
    dma = pltpu.SemaphoreType.DMA
    operands = (assignments.reshape(32, RUN), starting_coarse_label.reshape(1, RUN), embeddings, parents)
    cent, logt, terms = pl.pallas_call(
        kernel,
        out_shape=(
            jax.ShapeDtypeStruct((RUN, W), BF16),
            jax.ShapeDtypeStruct((1, RUN), F32),
            jax.ShapeDtypeStruct((2 * DP, 1, RUN), F32),
        ),
        in_specs=[hbm, hbm, hbm, hbm],
        out_specs=(anywhere, anywhere, anywhere),
        scratch_shapes=[
            pltpu.VMEM((32, RUN), jnp.int32),
            pltpu.VMEM((1, RUN), jnp.int32),
            pltpu.VMEM((NTILE, ROWS, TILE), BF16),
            pltpu.VMEM((2, SLOTS, ROWS), BF16),
            pltpu.VMEM((16, ROWS), BF16),
            pltpu.VMEM((2, 32, RUN), jnp.int32),
            pltpu.VMEM((2, DP, CAP, COLS), BF16),
            pltpu.VMEM((DP, CAP, W), BF16),
            pltpu.VMEM((DP, 1, SLOTS), F32),
            pltpu.VMEM((DP, 1, SLOTS), F32),
            pltpu.VMEM((EARLY + LATE, W), BF16),
            pltpu.VMEM((4, RUN, W), BF16),
            pltpu.VMEM((6, 8, RUN), F32),
            pltpu.VMEM((EARLY + LATE, 4 * RUN), F32),
            pltpu.VMEM((4, 4 * RUN), F32),
            pltpu.VMEM((4, 4 * RUN), F32),
            pltpu.VMEM((6, 8, RUN), F32),
            pltpu.VMEM((4, 4 * RUN), F32),
            pltpu.VMEM((4, 1, MCH), F32),
            pltpu.VMEM((2, 1, 1024), F32),
            pltpu.VMEM((1, 1024), F32),
            pltpu.VMEM((2 * DP, 1, RUN), F32),
            pltpu.VMEM((1, RUN), F32),
            dma((NTILE,)),
            dma((2,)),
            dma((2,)),
            dma,
            dma,
            dma,
            dma,
            dma,
            dma((12,)),
            dma((12,)),
            dma((10,)),
            dma((10,)),
            dma((6,)),
            dma((6,)),
            dma((6,)),
            dma((6,)),
            dma,
            dma,
            dma,
            dma,
            dma((3,)),
            dma((2,)),
        ],
        compiler_params=pltpu.CompilerParams(collective_id=0, has_side_effects=True, vmem_limit_bytes=52 << 20),
        name="handover",
    )(
        *(pltpu.with_memory_space_constraint(v, pltpu.HBM) for v in operands),
    )
    cent, logt, mass = pl.pallas_call(
        hand_on,
        out_shape=(
            jax.ShapeDtypeStruct((RUN, W), BF16),
            jax.ShapeDtypeStruct((1, RUN), F32),
            jax.ShapeDtypeStruct((1, PART), F32),
        ),
        in_specs=[vmem, vmem, vmem],
        out_specs=(vmem, vmem, vmem),
        compiler_params=pltpu.CompilerParams(vmem_limit_bytes=2 << 20),
        name="finish",
    )(cent, logt, terms)
    return cent, logt.reshape(RUN), mass.reshape(PART)


def solution(mesh):
    return jax.shard_map(
        per_device,
        mesh=mesh,
        in_specs=(P("dp", None), P("dp"), P("cent", None), P(("cent", "dp"))),
        out_specs=(P(("cent", "dp"), None), P(("cent", "dp")), P(("cent", "dp"))),
        check_vma=False,
    )
```
